32 devices in a mesh: lat: 8 (over y, x, core), wave: 4 (over z).
Axes of the slice: x: 2, y: 2, z: 4, core: 2. Of those that a mesh axis runs over, the one named last changes fastest.
Arguments:
- fourier_rows: bfloat16 [128, 1600, 384], P('wave', 'lat'), may hold values from -0.796875 to 0.796875
- legendre: float32 [128, 1600, 800], P('wave', 'lat'), may hold values from -0.21875 to 0.21875
- wavenumber: int32 [128], replicated, may hold values from 0 to 1599, as said below
- lower_diag: float32 [128, 1600], P('wave'), may hold values from -0.9 to 0.9
- main_diag: float32 [128, 1600], P('wave'), may hold values from 2 to 4
- upper_diag: float32 [128, 1600], P('wave'), may hold values from -0.9 to 0.9
Outputs:
- grid: bfloat16 [3200, 307200], P('wave', 'lat')
The draws below stay inside these ranges and needn't reach their ends.
Inputs may be any that keep to these rules, and one draw needn't show every extreme that they name: `wavenumber`: distinct wavenumbers; slot 2 i holds some a below 800 and slot 2 i + 1 holds 1599 - a; both ends of the range occur.
All inputs are finite; a program needn't handle non-finite values.
Results may differ from the reference program's by a relative error of at most 0.0055.
Values may be sent and summed in bfloat16 or wider, within the bound.
No kernel may reach another device: no remote copies, remote signals or barrier semaphores. Data moves between devices by JAX's collectives and lax.ppermute only.
A program may use at most 320 MiB of HBM per device.

```python
import math
import jax
import jax.numpy as jnp
from jax import lax

NLAT = 1600
NLON = 3200
LEV = 64
NPAIR = 800
MW = 128
N_WAVE = 4


def draw_wavenumber(key, part):
    low_pick = jax.random.permutation(key, NPAIR)[:MW // 2]
    low_pick = (low_pick - low_pick[0]) % NPAIR
    high_pick = NLAT - 1 - low_pick
    return jnp.stack([low_pick, high_pick], axis=1).reshape(MW).astype(jnp.int32)


def block_scale(rng, shape, cuts, least, high):
    def one(dim, blocks):
        steps = jax.random.uniform(jax.random.fold_in(jax.random.fold_in(rng, 6), dim), (blocks,), jnp.float32, least / len(cuts), high / len(cuts))
        return jnp.repeat(jnp.exp(steps), shape[dim] // blocks).reshape((-1,) + (1,) * (len(shape) - dim - 1))

    loudness = one(*cuts[0])
    for cut in cuts[1:]:
        loudness = loudness * one(*cut)
    return loudness


def bell_draw(key, extent, spread, reach, pieces=(), kind=jnp.bfloat16):
    factor_of = block_scale(key, extent, pieces, -0.22, 0.18) if pieces else 1.0
    array = jax.random.normal(key, extent, jnp.float32) * spread * factor_of
    return jnp.minimum(jnp.maximum(array, -reach), reach).astype(kind)


def setup_inputs(seed: int = 0) -> dict:
    arg_keys = jax.random.split(jax.random.key(seed), 7)
    return {
        "fourier_rows": bell_draw(arg_keys[0], (MW, NLAT, 6 * LEV), 0.1, 0.796875, ((0, 4), (1, 8))),
        "legendre": bell_draw(arg_keys[1], (MW, NLAT, NPAIR), NPAIR ** -0.5, 0.21875, ((0, 4), (1, 8)), jnp.float32),
        "wavenumber": draw_wavenumber(jax.random.fold_in(arg_keys[6], 71), 0),
        "lower_diag": jnp.clip(jax.random.uniform(arg_keys[3], (MW, NLAT), jnp.float32, -0.9, 0.9) * block_scale(arg_keys[3], (MW, NLAT), ((0, 4),), -0.4, 0.0), -0.9, 0.9),
        "main_diag": jnp.clip(2.0 + 2.0 * jax.random.uniform(arg_keys[4], (MW, NLAT), jnp.float32) ** block_scale(arg_keys[4], (MW, NLAT), ((0, 4),), -0.2, 0.2), 2.0, 4.0),
        "upper_diag": jnp.clip(jax.random.uniform(arg_keys[5], (MW, NLAT), jnp.float32, -0.9, 0.9) * block_scale(arg_keys[5], (MW, NLAT), ((0, 4),), -0.4, 0.0), -0.9, 0.9),
    }


precise = lax.Precision.HIGHEST
damping_rate = 4.0

def spectral_step(inputs):
    rows, legendre_rows, wave_id, lower_band, main_band, upper_band = inputs
    pair_count = NLAT // 2
    values = rows.astype(jnp.float32)
    upper_half = values[:pair_count]
    lower_half = values[pair_count:]
    parity_parts = jnp.stack([upper_half + lower_half, upper_half - lower_half])
    table_parts = legendre_rows.reshape(2, pair_count, pair_count)
    spectral = jnp.einsum('pcq,pqk->pck', table_parts, parity_parts, precision=precise)
    column_ids = jnp.arange(pair_count, dtype=jnp.int32)
    parity_ids = jnp.arange(2, dtype=jnp.int32)
    degree_int = wave_id + 2 * column_ids[None, :] + parity_ids[:, None]
    inside_mask = degree_int < NLAT
    inside = inside_mask.astype(jnp.float32)
    degree = degree_int.astype(jnp.float32)
    degree_ratio = degree * (degree + 1.0) / (NLAT * (NLAT - 1.0))
    damping = 1.0 / (1.0 + damping_rate * degree_ratio * degree_ratio)
    spectral = spectral * inside[:, :, None]
    fields = spectral.reshape(2, pair_count, 2, 3, LEV)
    vorticity = fields[:, :, :, 0:1, :]
    div_temp = fields[:, :, :, 1:, :].reshape(2, pair_count, 4 * LEV)
    not_first = (column_ids > 0).astype(jnp.float32)
    not_last = (column_ids < pair_count - 1).astype(jnp.float32)
    sub_band = lower_band.reshape(2, pair_count) * inside * not_first[None, :]
    super_band = upper_band.reshape(2, pair_count) * inside * not_last[None, :]
    center = jnp.where(inside_mask, main_band.reshape(2, pair_count), 1.0)
    solved = lax.linalg.tridiagonal_solve(sub_band, center, super_band, div_temp)
    merged = jnp.concatenate([vorticity, solved.reshape(2, pair_count, 2, 2, LEV)], axis=3)
    merged = merged.reshape(2, pair_count, 6 * LEV) * damping[:, :, None]
    grid_parts = jnp.einsum('pcq,pck->pqk', table_parts, merged, precision=precise)
    north_rows = grid_parts[0] + grid_parts[1]
    south_rows = grid_parts[0] - grid_parts[1]
    return jnp.concatenate([north_rows, south_rows], axis=0).astype(jnp.bfloat16)

def zonal_table(wave_ids, lon_ids):
    phase_index = wave_ids[:, None] * lon_ids[None, :] % NLON
    phase_angle = phase_index.astype(jnp.float32) * (2.0 * math.pi / NLON)
    return jnp.stack([jnp.cos(phase_angle), -jnp.sin(phase_angle)], axis=1).astype(jnp.bfloat16)

def reference(fourier_rows, legendre, wavenumber, lower_diag, main_diag, upper_diag):
    fourier_new = lax.map(spectral_step, (fourier_rows, legendre, wavenumber, lower_diag, main_diag, upper_diag))
    rows_wide = fourier_new.reshape(MW, NLAT, 2, 3 * LEV).astype(jnp.float32)
    lon_block = NLON // N_WAVE

    def synthesize(block_id):
        lon_ids = block_id * lon_block + jnp.arange(lon_block, dtype=jnp.int32)
        zonal_trig = zonal_table(wavenumber, lon_ids).astype(jnp.float32)
        return jnp.einsum('mcl,mrcj->lrj', zonal_trig, rows_wide).astype(jnp.bfloat16)
    blocks = lax.map(synthesize, jnp.arange(N_WAVE, dtype=jnp.int32))
    return blocks.reshape(NLON, NLAT * 3 * LEV)
```

```python
import functools
import math

import jax
import jax.numpy as jnp
from jax import lax
from jax.experimental import pallas as pl
from jax.experimental.pallas import tpu as pltpu
from jax.sharding import PartitionSpec as P

NLON = 3200
LEV = 64
damping_rate = 4.0
BLOCKS = 8
VMEM_LIMIT = 56 * 2**20
f32 = jnp.float32
bf16 = jnp.bfloat16


def zonal_matrix(wave_ids, lon_ids):
    phase_index = lon_ids[:, None, None] * wave_ids[None] % NLON
    phase_angle = phase_index.astype(f32) * (2.0 * math.pi / NLON)
    table = jnp.stack([jnp.cos(phase_angle), -jnp.sin(phase_angle)], axis=2).astype(bf16)
    return table.reshape(lon_ids.shape[0], 2 * wave_ids.size)


def factor_kernel(bands_ref, factors_ref, links_ref):
    systems, _, _, steps = bands_ref.shape
    sub, center, sup, inside, damping = (bands_ref[:, n] for n in range(5))
    lanes = lax.broadcasted_iota(jnp.int32, (systems, BLOCKS, steps), 2)

    def column(values, i):
        return values[:, :, i : i + 1]

    def place(values, i, new):
        return jnp.where(lanes == i, new, values)

    zero = jnp.zeros((systems, BLOCKS, steps), f32)
    inv, scaled_sub, scaled_sup, left, right = zero, zero, zero, zero, zero
    for i in range(steps):
        pivot = column(center, i)
        if i:
            pivot = pivot - column(sub, i) * sup_part
        inv_part = 1.0 / pivot
        sub_part = column(sub, i) * inv_part
        sup_part = column(sup, i) * inv_part
        left_part = -sub_part * left_part if i else sub_part
        inv = place(inv, i, inv_part)
        scaled_sub = place(scaled_sub, i, sub_part)
        scaled_sup = place(scaled_sup, i, sup_part)
        left = place(left, i, left_part)
    solved_left = zero
    for i in reversed(range(steps)):
        if i == steps - 1:
            right_part = column(scaled_sup, i)
            left_part = column(left, i)
        else:
            right_part = -column(scaled_sup, i) * right_part
            left_part = column(left, i) - column(scaled_sup, i) * left_part
        right = place(right, i, right_part)
        solved_left = place(solved_left, i, left_part)
    for n, values in enumerate((inv * inside, scaled_sub, scaled_sup, right, solved_left, damping * inside)):
        factors_ref[:, n] = values
    right_first, right_last = column(right, 0), column(right, steps - 1)
    left_first, left_last = column(solved_left, 0), column(solved_left, steps - 1)
    beta = jnp.zeros((systems, 1, 1), f32)
    width = links_ref.shape[-1]
    for b in range(BLOCKS):
        row = slice(b, b + 1)
        scale = 1.0 / (1.0 - left_first[:, row] * beta)
        step = right_first[:, row] * scale
        across = left_last[:, row] * beta
        beta = right_last[:, row] + across * step
        for n, value in enumerate((scale, left_first[:, row] * scale, step, left_last[:, row], across, beta)):
            links_ref[:, n, b : b + 1, :] = jnp.broadcast_to(value, (systems, 1, width))


def wave_kernel(arrived_ref, factors_ref, links_ref, home_ref, spec, part):
    _, pair_count, width = home_ref.shape
    steps = pair_count // BLOCKS
    tiles = width // 128
    north = arrived_ref[0, :, :width].astype(f32)
    south = arrived_ref[1, :, :width].astype(f32)
    for p in range(2):
        folded = (north + south if p == 0 else north - south).astype(bf16)
        spectral = jnp.dot(arrived_ref[p, :, width:], folded, preferred_element_type=f32)
        for t in range(tiles):
            spec[p, t] = spectral[:, 128 * t : 128 * t + 128]

    def spec_rows(p, i):
        return jnp.concatenate([spec[p, t, pl.ds(i, BLOCKS, stride=steps), :] for t in range(tiles)], axis=1)

    def factor(p, n, i):
        return factors_ref[p, n, :, i : i + 1]

    running = [None, None]
    for i in range(steps):
        for p in range(2):
            value = spec_rows(p, i) * factor(p, 0, i)
            if i:
                value = value - factor(p, 1, i) * running[p]
            part[p, i] = value
            running[p] = value
    last = list(running)
    for i in reversed(range(steps - 1)):
        for p in range(2):
            value = part[p, i] - factor(p, 2, i) * running[p]
            part[p, i] = value
            running[p] = value
    first = running
    after, before = [], []
    for p in range(2):
        def link(n, b):
            return jnp.concatenate([links_ref[p, n, b : b + 1, :]] * tiles, axis=1)

        alpha = jnp.zeros((1, width), f32)
        heads, tails = [], []
        for b in range(BLOCKS):
            row = slice(b, b + 1)
            head = first[p][row] * link(0, b) - link(1, b) * alpha
            alpha = last[p][row] - link(3, b) * alpha + link(4, b) * head
            heads.append(head)
            tails.append(alpha)
        ahead = jnp.zeros((1, width), f32)
        next_heads, prev_tails = [None] * BLOCKS, [jnp.zeros((1, width), f32)] * BLOCKS
        for b in reversed(range(BLOCKS)):
            next_heads[b] = ahead
            if b + 1 < BLOCKS:
                prev_tails[b + 1] = tails[b] - link(5, b) * ahead
            ahead = heads[b] - link(2, b) * ahead
        after.append(jnp.concatenate(next_heads, axis=0))
        before.append(jnp.concatenate(prev_tails, axis=0))
    half = lax.broadcasted_iota(jnp.int32, (BLOCKS, width), 1) % (width // 2)
    untouched = half < LEV
    for i in range(steps):
        for p in range(2):
            solved = part[p, i] - factor(p, 3, i) * after[p] - factor(p, 4, i) * before[p]
            damped = jnp.where(untouched, spec_rows(p, i), solved) * factor(p, 5, i)
            for t in range(tiles):
                spec[p, t, pl.ds(i, BLOCKS, stride=steps), :] = damped[:, 128 * t : 128 * t + 128]
    parts = []
    for p in range(2):
        damped = jnp.concatenate([spec[p, t].astype(bf16) for t in range(tiles)], axis=1)
        parts.append(
            lax.dot_general(
                arrived_ref[p, :, width:], damped, (((0,), (0,)), ((), ())), preferred_element_type=f32
            )
        )
    home_ref[0] = (parts[0] + parts[1]).astype(bf16)
    home_ref[1] = (parts[0] - parts[1]).astype(bf16)


def pair_kernel(rows_ref, pairs_ref):
    slots, groups, rows, width = rows_ref.shape
    order = slots * rows
    out_row = lax.broadcasted_iota(jnp.int32, (order, order), 0)
    in_row = lax.broadcasted_iota(jnp.int32, (order, order), 1)
    odd, rest = out_row // (order // 2), out_row % (order // 2)
    source = (rest % slots) * rows + 2 * (rest // slots) + odd
    shuffle = (in_row == source).astype(bf16)
    first_half = lax.broadcasted_iota(jnp.int32, (order // 2, width), 1) < width // 2

    def swap(values):
        return jnp.concatenate([values[:, width // 2 :], values[:, : width // 2]], axis=1)

    def one(g, _):
        block = rows_ref[:, g].astype(f32).reshape(order, width).astype(bf16)
        moved = jnp.dot(shuffle, block, preferred_element_type=f32)
        even_rows, odd_rows = moved[: order // 2], moved[order // 2 :]
        real = jnp.where(first_half, even_rows, swap(odd_rows)).reshape(rows // 2, slots, width)
        imag = jnp.where(first_half, swap(even_rows), odd_rows).reshape(rows // 2, slots, width)
        pairs_ref[pl.ds(g * (rows // 2), rows // 2)] = jnp.concatenate([real, imag], axis=1).astype(bf16)
        return 0

    lax.fori_loop(0, groups, one, 0)


def zonal_kernel(chunks, trig_ref, *refs):
    grid_ref = refs[-1]
    waves, pairs, depth, width = refs[0].shape
    for r in range(0, pairs, 2):
        rhs = jnp.concatenate(
            [
                jnp.concatenate([refs[j][z, r + n] for j in range(chunks) for z in range(waves)], axis=0)
                for n in range(2)
            ],
            axis=1,
        )
        sums = jnp.dot(trig_ref[...], rhs, preferred_element_type=f32)
        grid_ref[:, r * width : (r + 2) * width] = sums.astype(bf16)


def params():
    return pltpu.CompilerParams(vmem_limit_bytes=VMEM_LIMIT)


def whole_vmem(count):
    return [pl.BlockSpec(memory_space=pltpu.VMEM)] * count


def make_factors(bands):
    systems, _, _, steps = bands.shape
    return pl.pallas_call(
        factor_kernel,
        out_shape=(
            jax.ShapeDtypeStruct((systems, 6, BLOCKS, steps), f32),
            jax.ShapeDtypeStruct((systems, 6, BLOCKS, 128), f32),
        ),
        in_specs=whole_vmem(1),
        out_specs=tuple(whole_vmem(2)),
        compiler_params=params(),
        cost_estimate=pl.CostEstimate(flops=2_000_000_000, bytes_accessed=2_000_000, transcendentals=0),
        name="factor",
    )(bands)


def wave_step(arrived, factors, links, width):
    _, pair_count, _ = arrived.shape
    return pl.pallas_call(
        wave_kernel,
        out_shape=jax.ShapeDtypeStruct((2, pair_count, width), bf16),
        in_specs=whole_vmem(3),
        out_specs=whole_vmem(1)[0],
        scratch_shapes=[
            pltpu.VMEM((2, width // 128, pair_count, 128), f32),
            pltpu.VMEM((2, pair_count // BLOCKS, BLOCKS, width), f32),
        ],
        compiler_params=params(),
        cost_estimate=pl.CostEstimate(flops=8_000_000_000, bytes_accessed=6_000_000, transcendentals=0),
        name="wave",
    )(arrived, factors, links)


def pair_rows(rows):
    slots, count, width = rows.shape
    if count % 8 or slots % 8:
        split = rows.reshape(slots, count // 2, 2, 2, width // 2)
        return split.transpose(1, 3, 0, 2, 4).reshape(count // 2, 2 * slots, width)
    return pl.pallas_call(
        pair_kernel,
        out_shape=jax.ShapeDtypeStruct((count // 2, 2 * slots, width), bf16),
        in_specs=whole_vmem(1),
        out_specs=whole_vmem(1)[0],
        compiler_params=params(),
        cost_estimate=pl.CostEstimate(flops=2_000_000_000, bytes_accessed=2_400_000, transcendentals=0),
        name="pair",
    )(rows.reshape(slots, count // 8, 8, width))


def synthesize(trig, gathered):
    lons, depth = trig.shape
    waves, pairs, rows, width = gathered[0].shape
    step = next(n for n in (4, 2, 1) if pairs % n == 0)
    assert step > 1
    spec = pl.BlockSpec((waves, step, rows, width), lambda i: (0, i, 0, 0))
    return pl.pallas_call(
        functools.partial(zonal_kernel, len(gathered)),
        out_shape=jax.ShapeDtypeStruct((lons, pairs * width), bf16),
        grid=(pairs // step,),
        in_specs=[pl.BlockSpec((lons, depth), lambda i: (0, 0))] + [spec] * len(gathered),
        out_specs=pl.BlockSpec((lons, step * width), lambda i: (0, i)),
        compiler_params=params(),
        cost_estimate=pl.CostEstimate(
            flops=2 * lons * depth * pairs * width, bytes_accessed=2 * lons * pairs * width, transcendentals=0
        ),
        name="zonal",
    )(trig, *gathered)


def on_device(fourier_rows, legendre, wavenumber, lower_diag, main_diag, upper_diag):
    lat_count = lax.axis_size("lat")
    wave_count = lax.axis_size("wave")
    lat_pos = lax.axis_index("lat")
    wave_pos = lax.axis_index("wave")
    group_slots, row_count, row_width = fourier_rows.shape
    pair_count = legendre.shape[2]
    lat_rows = 2 * pair_count
    chunks = group_slots // lat_count
    steps = pair_count // BLOCKS

    slot_ids = wavenumber.reshape(wave_count, chunks, lat_count)
    own_group = lax.dynamic_index_in_dim(slot_ids, wave_pos, 0, keepdims=False)
    wave_ids = lax.dynamic_index_in_dim(own_group, lat_pos, 1, keepdims=False)

    def own(band):
        return lax.dynamic_index_in_dim(
            band.reshape(chunks, lat_count, 2, pair_count), lat_pos, 1, keepdims=False
        )

    column_ids = jnp.arange(pair_count, dtype=jnp.int32)
    parity_ids = jnp.arange(2, dtype=jnp.int32)
    degree_int = wave_ids[:, None, None] + 2 * column_ids[None, None, :] + parity_ids[None, :, None]
    inside_mask = degree_int < lat_rows
    inside = inside_mask.astype(f32)
    degree = degree_int.astype(f32)
    degree_ratio = degree * (degree + 1.0) / (lat_rows * (lat_rows - 1.0))
    damping = 1.0 / (1.0 + damping_rate * degree_ratio * degree_ratio)
    not_first = (column_ids > 0).astype(f32)
    not_last = (column_ids < pair_count - 1).astype(f32)
    sub_band = own(lower_diag) * inside * not_first
    super_band = own(upper_diag) * inside * not_last
    center = jnp.where(inside_mask, own(main_diag), 1.0)
    bands = jnp.stack([sub_band, center, super_band, inside, damping], axis=2)
    factors, links = make_factors(bands.reshape(2 * chunks, 5, BLOCKS, steps))
    factors = factors.reshape(chunks, 2, 6, BLOCKS, steps)
    links = links.reshape(chunks, 2, 6, BLOCKS, 128)

    gathered = []
    ready = None
    for j in range(chunks):
        pick = slice(j * lat_count, (j + 1) * lat_count)
        outgoing = jnp.concatenate([fourier_rows[pick], legendre[pick].astype(bf16)], axis=2)
        if ready is not None:
            outgoing, _ = lax.optimization_barrier((outgoing, ready))
        arrived = lax.all_to_all(outgoing, "lat", split_axis=0, concat_axis=0, tiled=True)
        arrived = arrived.reshape(2, pair_count, row_width + pair_count)
        home = wave_step(arrived, factors[j], links[j], row_width)
        home = home.reshape(lat_count, row_count, row_width)
        rows = lax.all_to_all(home, "lat", split_axis=0, concat_axis=0, tiled=True)
        ready = pair_rows(rows)
        gathered.append(lax.all_gather(ready, "wave", axis=0))

    lon_dev = NLON // wave_count
    lon_ids = wave_pos * lon_dev + jnp.arange(lon_dev, dtype=jnp.int32)
    trig = zonal_matrix(slot_ids.transpose(1, 0, 2).reshape(chunks * wave_count, lat_count), lon_ids)
    return synthesize(trig, gathered)


def solution(mesh):
    placed = (
        P("wave", "lat", None),
        P("wave", "lat", None),
        P(),
        P("wave", None),
        P("wave", None),
        P("wave", None),
    )
    return jax.shard_map(
        on_device, mesh=mesh, in_specs=placed, out_specs=P("wave", "lat"), check_vma=False
    )
```

```python
import functools
import math

import jax
import jax.numpy as jnp
from jax import lax
from jax.experimental import pallas as pl
from jax.experimental.pallas import tpu as pltpu
from jax.sharding import PartitionSpec as P

NLON = 3200
LEV = 64
damping_rate = 4.0
BLOCKS = 8
VMEM_LIMIT = 56 * 2**20
f32 = jnp.float32
bf16 = jnp.bfloat16


def zonal_matrix(blocks, lon_ids):
    wave_ids = jnp.concatenate([jnp.concatenate([ids, ids]) for ids in blocks])
    is_sine = jnp.concatenate([jnp.arange(2 * ids.size) >= ids.size for ids in blocks])
    phase_index = lon_ids[:, None] * wave_ids[None, :] % NLON
    phase_angle = phase_index.astype(f32) * (2.0 * math.pi / NLON)
    return jnp.where(is_sine[None, :], -jnp.sin(phase_angle), jnp.cos(phase_angle)).astype(bf16)


def factor_kernel(bands_ref, factors_ref, links_ref):
    systems, _, _, steps = bands_ref.shape
    sub, center, sup, inside, damping = (bands_ref[:, n] for n in range(5))
    lanes = lax.broadcasted_iota(jnp.int32, (systems, BLOCKS, steps), 2)

    def column(values, i):
        return values[:, :, i : i + 1]

    def place(values, i, new):
        return jnp.where(lanes == i, new, values)

    zero = jnp.zeros((systems, BLOCKS, steps), f32)
    inv, scaled_sub, scaled_sup, left, right = zero, zero, zero, zero, zero
    for i in range(steps):
        pivot = column(center, i)
        if i:
            pivot = pivot - column(sub, i) * sup_part
        inv_part = 1.0 / pivot
        sub_part = column(sub, i) * inv_part
        sup_part = column(sup, i) * inv_part
        left_part = -sub_part * left_part if i else sub_part
        inv = place(inv, i, inv_part)
        scaled_sub = place(scaled_sub, i, sub_part)
        scaled_sup = place(scaled_sup, i, sup_part)
        left = place(left, i, left_part)
    solved_left = zero
    for i in reversed(range(steps)):
        if i == steps - 1:
            right_part = column(scaled_sup, i)
            left_part = column(left, i)
        else:
            right_part = -column(scaled_sup, i) * right_part
            left_part = column(left, i) - column(scaled_sup, i) * left_part
        right = place(right, i, right_part)
        solved_left = place(solved_left, i, left_part)
    for n, values in enumerate((inv * inside, scaled_sub, scaled_sup, right, solved_left, damping * inside)):
        factors_ref[:, n] = values
    right_first, right_last = column(right, 0), column(right, steps - 1)
    left_first, left_last = column(solved_left, 0), column(solved_left, steps - 1)
    beta = jnp.zeros((systems, 1, 1), f32)
    width = links_ref.shape[-1]
    for b in range(BLOCKS):
        row = slice(b, b + 1)
        scale = 1.0 / (1.0 - left_first[:, row] * beta)
        step = right_first[:, row] * scale
        across = left_last[:, row] * beta
        beta = right_last[:, row] + across * step
        for n, value in enumerate((scale, left_first[:, row] * scale, step, left_last[:, row], across, beta)):
            links_ref[:, n, b : b + 1, :] = jnp.broadcast_to(value, (systems, 1, width))


def wave_kernel(arrived_ref, factors_ref, links_ref, home_ref, spec, part):
    _, pair_count, width = home_ref.shape
    steps = pair_count // BLOCKS
    tiles = width // 128
    north = arrived_ref[0, :, :width].astype(f32)
    south = arrived_ref[1, :, :width].astype(f32)
    for p in range(2):
        folded = (north + south if p == 0 else north - south).astype(bf16)
        spectral = jnp.dot(arrived_ref[p, :, width:], folded, preferred_element_type=f32)
        for t in range(tiles):
            spec[p, t] = spectral[:, 128 * t : 128 * t + 128]

    def spec_rows(p, i):
        return jnp.concatenate([spec[p, t, pl.ds(i, BLOCKS, stride=steps), :] for t in range(tiles)], axis=1)

    def factor(p, n, i):
        return factors_ref[p, n, :, i : i + 1]

    running = [None, None]
    for i in range(steps):
        for p in range(2):
            value = spec_rows(p, i) * factor(p, 0, i)
            if i:
                value = value - factor(p, 1, i) * running[p]
            part[p, i] = value
            running[p] = value
    last = list(running)
    for i in reversed(range(steps - 1)):
        for p in range(2):
            value = part[p, i] - factor(p, 2, i) * running[p]
            part[p, i] = value
            running[p] = value
    first = running
    after, before = [], []
    for p in range(2):
        def link(n, b):
            return jnp.concatenate([links_ref[p, n, b : b + 1, :]] * tiles, axis=1)

        alpha = jnp.zeros((1, width), f32)
        heads, tails = [], []
        for b in range(BLOCKS):
            row = slice(b, b + 1)
            head = first[p][row] * link(0, b) - link(1, b) * alpha
            alpha = last[p][row] - link(3, b) * alpha + link(4, b) * head
            heads.append(head)
            tails.append(alpha)
        ahead = jnp.zeros((1, width), f32)
        next_heads, prev_tails = [None] * BLOCKS, [jnp.zeros((1, width), f32)] * BLOCKS
        for b in reversed(range(BLOCKS)):
            next_heads[b] = ahead
            if b + 1 < BLOCKS:
                prev_tails[b + 1] = tails[b] - link(5, b) * ahead
            ahead = heads[b] - link(2, b) * ahead
        after.append(jnp.concatenate(next_heads, axis=0))
        before.append(jnp.concatenate(prev_tails, axis=0))
    half = lax.broadcasted_iota(jnp.int32, (BLOCKS, width), 1) % (width // 2)
    untouched = half < LEV
    for i in range(steps):
        for p in range(2):
            solved = part[p, i] - factor(p, 3, i) * after[p] - factor(p, 4, i) * before[p]
            damped = jnp.where(untouched, spec_rows(p, i), solved) * factor(p, 5, i)
            for t in range(tiles):
                spec[p, t, pl.ds(i, BLOCKS, stride=steps), :] = damped[:, 128 * t : 128 * t + 128]
    parts = []
    for p in range(2):
        damped = jnp.concatenate([spec[p, t].astype(bf16) for t in range(tiles)], axis=1)
        parts.append(
            lax.dot_general(
                arrived_ref[p, :, width:], damped, (((0,), (0,)), ((), ())), preferred_element_type=f32
            )
        )
    home_ref[0] = (parts[0] + parts[1]).astype(bf16)
    home_ref[1] = (parts[0] - parts[1]).astype(bf16)


def pair_kernel(rows_ref, *pairs_refs):
    slots, groups, rows, width = rows_ref.shape
    order = slots * rows
    out_row = lax.broadcasted_iota(jnp.int32, (order, order), 0)
    in_row = lax.broadcasted_iota(jnp.int32, (order, order), 1)
    odd, rest = out_row // (order // 2), out_row % (order // 2)
    source = (rest % slots) * rows + 2 * (rest // slots) + odd
    shuffle = (in_row == source).astype(bf16)
    first_half = lax.broadcasted_iota(jnp.int32, (order // 2, width), 1) < width // 2

    def swap(values):
        return jnp.concatenate([values[:, width // 2 :], values[:, : width // 2]], axis=1)

    for g in range(groups):
        block = rows_ref[:, g].astype(f32).reshape(order, width).astype(bf16)
        moved = jnp.dot(shuffle, block, preferred_element_type=f32)
        even_rows, odd_rows = moved[: order // 2], moved[order // 2 :]
        real = jnp.where(first_half, even_rows, swap(odd_rows)).reshape(rows // 2, slots, width)
        imag = jnp.where(first_half, swap(even_rows), odd_rows).reshape(rows // 2, slots, width)
        both = jnp.concatenate([real, imag], axis=1).astype(bf16)
        for n in range(rows // 2):
            piece, place = divmod(g * (rows // 2) + n, pairs_refs[0].shape[0])
            pairs_refs[piece][place] = both[n]


def zonal_kernel(count, trig_ref, *refs):
    grid_ref = refs[-1]
    pairs, _, width = refs[0].shape
    for r in range(0, pairs, 2):
        rhs = jnp.concatenate(
            [jnp.concatenate([refs[m][r + n] for m in range(count)], axis=0) for n in range(2)], axis=1
        )
        sums = jnp.dot(trig_ref[...], rhs, preferred_element_type=f32)
        grid_ref[:, r * width : (r + 2) * width] = sums.astype(bf16)


def params():
    return pltpu.CompilerParams(vmem_limit_bytes=VMEM_LIMIT)


def whole_vmem(count):
    return [pl.BlockSpec(memory_space=pltpu.VMEM)] * count


def make_factors(bands):
    systems, _, _, steps = bands.shape
    return pl.pallas_call(
        factor_kernel,
        out_shape=(
            jax.ShapeDtypeStruct((systems, 6, BLOCKS, steps), f32),
            jax.ShapeDtypeStruct((systems, 6, BLOCKS, 128), f32),
        ),
        in_specs=whole_vmem(1),
        out_specs=tuple(whole_vmem(2)),
        compiler_params=params(),
        cost_estimate=pl.CostEstimate(flops=2_000_000_000, bytes_accessed=2_000_000, transcendentals=0),
        name="factor",
    )(bands)


def wave_step(arrived, factors, links, width):
    _, pair_count, _ = arrived.shape
    return pl.pallas_call(
        wave_kernel,
        out_shape=jax.ShapeDtypeStruct((2, pair_count, width), bf16),
        in_specs=whole_vmem(3),
        out_specs=whole_vmem(1)[0],
        scratch_shapes=[
            pltpu.VMEM((2, width // 128, pair_count, 128), f32),
            pltpu.VMEM((2, pair_count // BLOCKS, BLOCKS, width), f32),
        ],
        compiler_params=params(),
        cost_estimate=pl.CostEstimate(flops=8_000_000_000, bytes_accessed=6_000_000, transcendentals=0),
        name="wave",
    )(arrived, factors, links)


def pair_rows(rows, pieces=1):
    slots, count, width = rows.shape
    if count % 8 or slots % 8:
        split = rows.reshape(slots, count // 2, 2, 2, width // 2)
        joined = split.transpose(1, 3, 0, 2, 4).reshape(pieces, count // 2 // pieces, 2 * slots, width)
        return [joined[n] for n in range(pieces)]
    shape = jax.ShapeDtypeStruct((count // 2 // pieces, 2 * slots, width), bf16)
    pairs = pl.pallas_call(
        pair_kernel,
        out_shape=[shape] * pieces,
        in_specs=whole_vmem(1),
        out_specs=whole_vmem(pieces),
        compiler_params=params(),
        cost_estimate=pl.CostEstimate(flops=2_000_000_000, bytes_accessed=2_400_000, transcendentals=0),
        name="pair",
    )(rows.reshape(slots, count // 8, 8, width))
    return list(pairs)


def synthesize(trig, whole, last):
    lons, depth = trig.shape
    pairs, _, width = whole[0].shape
    piece_pairs = pairs // len(last)
    step = next(n for n in (10, 8, 6, 4, 2) if piece_pairs % n == 0)
    steps = piece_pairs // step
    grid = None
    for piece, extra in enumerate(last):

        def spec(array, first):
            return pl.BlockSpec((step,) + array.shape[1:], lambda i: (first + i, 0, 0))

        first = piece * steps
        operands = [trig, *whole, *extra]
        in_specs = [pl.BlockSpec((lons, depth), lambda i: (0, 0))]
        in_specs += [spec(array, first) for array in whole] + [spec(array, 0) for array in extra]
        if grid is not None:
            operands.append(grid)
            in_specs.append(pl.BlockSpec(memory_space=pl.ANY))
        grid = pl.pallas_call(
            functools.partial(zonal_kernel, len(whole) + len(extra)),
            out_shape=jax.ShapeDtypeStruct((lons, pairs * width), bf16),
            grid=(steps,),
            in_specs=in_specs,
            out_specs=pl.BlockSpec((lons, step * width), lambda i, first=first: (0, first + i)),
            input_output_aliases={len(operands) - 1: 0} if piece else {},
            compiler_params=params(),
            cost_estimate=pl.CostEstimate(
                flops=2 * lons * depth * piece_pairs * width,
                bytes_accessed=2 * lons * piece_pairs * width,
                transcendentals=0,
            ),
            name="zonal",
        )(*operands)
    return grid


def on_device(fourier_rows, legendre, wavenumber, lower_diag, main_diag, upper_diag):
    lat_count = lax.axis_size("lat")
    wave_count = lax.axis_size("wave")
    lat_pos = lax.axis_index("lat")
    wave_pos = lax.axis_index("wave")
    group_slots, row_count, row_width = fourier_rows.shape
    pair_count = legendre.shape[2]
    lat_rows = 2 * pair_count
    chunks = group_slots // lat_count
    steps = pair_count // BLOCKS

    slot_ids = wavenumber.reshape(wave_count, chunks, lat_count)
    own_group = lax.dynamic_index_in_dim(slot_ids, wave_pos, 0, keepdims=False)
    wave_ids = lax.dynamic_index_in_dim(own_group, lat_pos, 1, keepdims=False)

    def own(band):
        return lax.dynamic_index_in_dim(
            band.reshape(chunks, lat_count, 2, pair_count), lat_pos, 1, keepdims=False
        )

    column_ids = jnp.arange(pair_count, dtype=jnp.int32)
    parity_ids = jnp.arange(2, dtype=jnp.int32)
    degree_int = wave_ids[:, None, None] + 2 * column_ids[None, None, :] + parity_ids[None, :, None]
    inside_mask = degree_int < lat_rows
    inside = inside_mask.astype(f32)
    degree = degree_int.astype(f32)
    degree_ratio = degree * (degree + 1.0) / (lat_rows * (lat_rows - 1.0))
    damping = 1.0 / (1.0 + damping_rate * degree_ratio * degree_ratio)
    not_first = (column_ids > 0).astype(f32)
    not_last = (column_ids < pair_count - 1).astype(f32)
    sub_band = own(lower_diag) * inside * not_first
    super_band = own(upper_diag) * inside * not_last
    center = jnp.where(inside_mask, own(main_diag), 1.0)
    bands = jnp.stack([sub_band, center, super_band, inside, damping], axis=2)
    factors, links = make_factors(bands.reshape(2 * chunks, 5, BLOCKS, steps))
    factors = factors.reshape(chunks, 2, 6, BLOCKS, steps)
    links = links.reshape(chunks, 2, 6, BLOCKS, 128)

    def outgoing(rows, table, j):
        pick = slice(j * lat_count, (j + 1) * lat_count)
        return jnp.concatenate([rows[pick], table[pick].astype(bf16)], axis=2)

    def swap_lat(values):
        return lax.all_to_all(values, "lat", split_axis=0, concat_axis=0, tiled=True)

    def from_waves(values):
        return [values] + [
            lax.ppermute(values, "wave", [(w, (w + k) % wave_count) for w in range(wave_count)])
            for k in range(1, wave_count)
        ]

    def wave_rows(arrived, j):
        arrived = arrived.reshape(2, pair_count, row_width + pair_count)
        return wave_step(arrived, factors[j], links[j], row_width).reshape(lat_count, row_count, row_width)

    first_out = outgoing(fourier_rows, legendre, 0)
    rows_later, table_later, _ = lax.optimization_barrier((fourier_rows, legendre, first_out))
    ready = wave_rows(swap_lat(first_out), 0)
    first_rows = from_waves(ready)
    pieces = 2 if row_count % 8 == 0 else 1
    whole, last = [], []
    for j in range(1, chunks):
        out, _ = lax.optimization_barrier((outgoing(rows_later, table_later, j), ready))
        home = wave_rows(swap_lat(out), j)
        pairs = pair_rows(swap_lat(home), pieces if j == chunks - 1 else 1)
        ready = pairs[0]
        parts = [from_waves(part) for part in pairs]
        if j == chunks - 1:
            last = parts
        else:
            whole += parts[0]
    first_stack, _ = lax.optimization_barrier((jnp.stack(first_rows, axis=1), ready))
    first_stack = swap_lat(first_stack).reshape(lat_count * wave_count, row_count, row_width)
    whole = pair_rows(first_stack) + whole

    lon_dev = NLON // wave_count
    lon_ids = wave_pos * lon_dev + jnp.arange(lon_dev, dtype=jnp.int32)
    sources = (wave_pos - jnp.arange(wave_count)) % wave_count
    seen_ids = slot_ids[sources]
    blocks = [seen_ids[:, 0].T.reshape(-1)] + [seen_ids[k, j] for j in range(1, chunks) for k in range(wave_count)]
    return synthesize(zonal_matrix(blocks, lon_ids), whole, last)


def solution(mesh):
    placed = (
        P("wave", "lat", None),
        P("wave", "lat", None),
        P(),
        P("wave", None),
        P("wave", None),
        P("wave", None),
    )
    return jax.shard_map(
        on_device, mesh=mesh, in_specs=placed, out_specs=P("wave", "lat"), check_vma=False
    )
```

```python
import functools
import math

import jax
import jax.numpy as jnp
from jax import lax
from jax.experimental import pallas as pl
from jax.experimental.pallas import tpu as pltpu
from jax.sharding import PartitionSpec as P

NLON = 3200
LEV = 64
damping_rate = 4.0
BLOCKS = 8
VMEM_LIMIT = 56 * 2**20
f32 = jnp.float32
bf16 = jnp.bfloat16


def zonal_matrix(blocks, lon_ids):
    wave_ids = jnp.concatenate([jnp.concatenate([ids, ids]) for ids in blocks])
    is_sine = jnp.concatenate([jnp.arange(2 * ids.size) >= ids.size for ids in blocks])
    phase_index = lon_ids[:, None] * wave_ids[None, :] % NLON
    phase_angle = phase_index.astype(f32) * (2.0 * math.pi / NLON)
    return jnp.where(is_sine[None, :], -jnp.sin(phase_angle), jnp.cos(phase_angle)).astype(bf16)


def factor_kernel(bands_ref, factors_ref, links_ref):
    systems, _, _, steps = bands_ref.shape
    sub, center, sup, inside, damping = (bands_ref[:, n] for n in range(5))
    lanes = lax.broadcasted_iota(jnp.int32, (systems, BLOCKS, steps), 2)

    def column(values, i):
        return values[:, :, i : i + 1]

    def place(values, i, new):
        return jnp.where(lanes == i, new, values)

    zero = jnp.zeros((systems, BLOCKS, steps), f32)
    inv, scaled_sub, scaled_sup, left, right = zero, zero, zero, zero, zero
    for i in range(steps):
        pivot = column(center, i)
        if i:
            pivot = pivot - column(sub, i) * sup_part
        inv_part = 1.0 / pivot
        sub_part = column(sub, i) * inv_part
        sup_part = column(sup, i) * inv_part
        left_part = -sub_part * left_part if i else sub_part
        inv = place(inv, i, inv_part)
        scaled_sub = place(scaled_sub, i, sub_part)
        scaled_sup = place(scaled_sup, i, sup_part)
        left = place(left, i, left_part)
    solved_left = zero
    for i in reversed(range(steps)):
        if i == steps - 1:
            right_part = column(scaled_sup, i)
            left_part = column(left, i)
        else:
            right_part = -column(scaled_sup, i) * right_part
            left_part = column(left, i) - column(scaled_sup, i) * left_part
        right = place(right, i, right_part)
        solved_left = place(solved_left, i, left_part)
    for n, values in enumerate((inv * inside, scaled_sub, scaled_sup, right, solved_left, damping * inside)):
        factors_ref[:, n] = values
    right_first, right_last = column(right, 0), column(right, steps - 1)
    left_first, left_last = column(solved_left, 0), column(solved_left, steps - 1)
    beta = jnp.zeros((systems, 1, 1), f32)
    width = links_ref.shape[-1]
    for b in range(BLOCKS):
        row = slice(b, b + 1)
        scale = 1.0 / (1.0 - left_first[:, row] * beta)
        step = right_first[:, row] * scale
        across = left_last[:, row] * beta
        beta = right_last[:, row] + across * step
        for n, value in enumerate((scale, left_first[:, row] * scale, step, left_last[:, row], across, beta)):
            links_ref[:, n, b : b + 1, :] = jnp.broadcast_to(value, (systems, 1, width))


def wave_kernel(arrived_ref, factors_ref, links_ref, home_ref, spec, part):
    _, pair_count, width = home_ref.shape
    steps = pair_count // BLOCKS
    tiles = width // 128
    north = arrived_ref[0, :, :width].astype(f32)
    south = arrived_ref[1, :, :width].astype(f32)
    for p in range(2):
        folded = (north + south if p == 0 else north - south).astype(bf16)
        spectral = jnp.dot(arrived_ref[p, :, width:], folded, preferred_element_type=f32)
        for t in range(tiles):
            spec[p, t] = spectral[:, 128 * t : 128 * t + 128]

    def spec_rows(p, i):
        return jnp.concatenate([spec[p, t, pl.ds(i, BLOCKS, stride=steps), :] for t in range(tiles)], axis=1)

    def factor(p, n, i):
        return factors_ref[p, n, :, i : i + 1]

    running = [None, None]
    for i in range(steps):
        for p in range(2):
            value = spec_rows(p, i) * factor(p, 0, i)
            if i:
                value = value - factor(p, 1, i) * running[p]
            part[p, i] = value
            running[p] = value
    last = list(running)
    for i in reversed(range(steps - 1)):
        for p in range(2):
            value = part[p, i] - factor(p, 2, i) * running[p]
            part[p, i] = value
            running[p] = value
    first = running
    after, before = [], []
    for p in range(2):
        def link(n, b):
            return jnp.concatenate([links_ref[p, n, b : b + 1, :]] * tiles, axis=1)

        alpha = jnp.zeros((1, width), f32)
        heads, tails = [], []
        for b in range(BLOCKS):
            row = slice(b, b + 1)
            head = first[p][row] * link(0, b) - link(1, b) * alpha
            alpha = last[p][row] - link(3, b) * alpha + link(4, b) * head
            heads.append(head)
            tails.append(alpha)
        ahead = jnp.zeros((1, width), f32)
        next_heads, prev_tails = [None] * BLOCKS, [jnp.zeros((1, width), f32)] * BLOCKS
        for b in reversed(range(BLOCKS)):
            next_heads[b] = ahead
            if b + 1 < BLOCKS:
                prev_tails[b + 1] = tails[b] - link(5, b) * ahead
            ahead = heads[b] - link(2, b) * ahead
        after.append(jnp.concatenate(next_heads, axis=0))
        before.append(jnp.concatenate(prev_tails, axis=0))
    half = lax.broadcasted_iota(jnp.int32, (BLOCKS, width), 1) % (width // 2)
    untouched = half < LEV
    for i in range(steps):
        for p in range(2):
            solved = part[p, i] - factor(p, 3, i) * after[p] - factor(p, 4, i) * before[p]
            damped = jnp.where(untouched, spec_rows(p, i), solved) * factor(p, 5, i)
            for t in range(tiles):
                spec[p, t, pl.ds(i, BLOCKS, stride=steps), :] = damped[:, 128 * t : 128 * t + 128]
    parts = []
    for p in range(2):
        damped = jnp.concatenate([spec[p, t].astype(bf16) for t in range(tiles)], axis=1)
        parts.append(
            lax.dot_general(
                arrived_ref[p, :, width:], damped, (((0,), (0,)), ((), ())), preferred_element_type=f32
            )
        )
    home_ref[0] = (parts[0] + parts[1]).astype(bf16)
    home_ref[1] = (parts[0] - parts[1]).astype(bf16)


def pair_kernel(rows_ref, *pairs_refs):
    slots, groups, rows, width = rows_ref.shape
    order = slots * rows
    out_row = lax.broadcasted_iota(jnp.int32, (order, order), 0)
    in_row = lax.broadcasted_iota(jnp.int32, (order, order), 1)
    odd, rest = out_row // (order // 2), out_row % (order // 2)
    source = (rest % slots) * rows + 2 * (rest // slots) + odd
    shuffle = (in_row == source).astype(bf16)
    first_half = lax.broadcasted_iota(jnp.int32, (order // 2, width), 1) < width // 2

    def swap(values):
        return jnp.concatenate([values[:, width // 2 :], values[:, : width // 2]], axis=1)

    places = [ref.at[n] for ref in pairs_refs for n in range(ref.shape[0])]
    for g in range(groups):
        block = rows_ref[:, g].astype(f32).reshape(order, width).astype(bf16)
        moved = jnp.dot(shuffle, block, preferred_element_type=f32)
        even_rows, odd_rows = moved[: order // 2], moved[order // 2 :]
        real = jnp.where(first_half, even_rows, swap(odd_rows)).reshape(rows // 2, slots, width)
        imag = jnp.where(first_half, swap(even_rows), odd_rows).reshape(rows // 2, slots, width)
        both = jnp.concatenate([real, imag], axis=1).astype(bf16)
        for n in range(rows // 2):
            places[g * (rows // 2) + n][...] = both[n]


def zonal_kernel(trig_ref, *refs):
    grid_ref = refs[-1]
    pairs, width = refs[0].shape[-3], refs[0].shape[-1]

    def coefficients(r):
        found = []
        for ref in refs[:-1]:
            found += [ref[r]] if ref.ndim == 3 else [ref[z, r] for z in range(ref.shape[0])]
        return jnp.concatenate(found, axis=0)

    for r in range(0, pairs, 2):
        rhs = jnp.concatenate([coefficients(r), coefficients(r + 1)], axis=1)
        sums = jnp.dot(trig_ref[...], rhs, preferred_element_type=f32)
        grid_ref[:, r * width : (r + 2) * width] = sums.astype(bf16)


def zonal_tail_kernel(trig_ref, *refs):
    zonal_kernel(trig_ref, *refs[:-2], refs[-1])


def params():
    return pltpu.CompilerParams(vmem_limit_bytes=VMEM_LIMIT)


def whole_vmem(count):
    return [pl.BlockSpec(memory_space=pltpu.VMEM)] * count


def make_factors(bands):
    systems, _, _, steps = bands.shape
    return pl.pallas_call(
        factor_kernel,
        out_shape=(
            jax.ShapeDtypeStruct((systems, 6, BLOCKS, steps), f32),
            jax.ShapeDtypeStruct((systems, 6, BLOCKS, 128), f32),
        ),
        in_specs=whole_vmem(1),
        out_specs=tuple(whole_vmem(2)),
        compiler_params=params(),
        cost_estimate=pl.CostEstimate(flops=2_000_000_000, bytes_accessed=2_000_000, transcendentals=0),
        name="factor",
    )(bands)


def wave_step(arrived, factors, links, width):
    _, pair_count, _ = arrived.shape
    return pl.pallas_call(
        wave_kernel,
        out_shape=jax.ShapeDtypeStruct((2, pair_count, width), bf16),
        in_specs=whole_vmem(3),
        out_specs=whole_vmem(1)[0],
        scratch_shapes=[
            pltpu.VMEM((2, width // 128, pair_count, 128), f32),
            pltpu.VMEM((2, pair_count // BLOCKS, BLOCKS, width), f32),
        ],
        compiler_params=params(),
        cost_estimate=pl.CostEstimate(flops=8_000_000_000, bytes_accessed=6_000_000, transcendentals=0),
        name="wave",
    )(arrived, factors, links)


def cut_pairs(count):
    pairs = count // 2
    return [pairs * 4 // 5, pairs // 5] if pairs % 10 == 0 and count % 8 == 0 else [pairs]


def pair_rows(rows, pieces):
    slots, count, width = rows.shape
    if count % 8 or slots % 8:
        split = rows.reshape(slots, count // 2, 2, 2, width // 2)
        joined = split.transpose(1, 3, 0, 2, 4).reshape(count // 2, 2 * slots, width)
        return [joined[sum(pieces[:n]) : sum(pieces[: n + 1])] for n in range(len(pieces))]
    pairs = pl.pallas_call(
        pair_kernel,
        out_shape=[jax.ShapeDtypeStruct((piece, 2 * slots, width), bf16) for piece in pieces],
        in_specs=whole_vmem(1),
        out_specs=whole_vmem(len(pieces)),
        compiler_params=params(),
        cost_estimate=pl.CostEstimate(flops=2_000_000_000, bytes_accessed=2_400_000, transcendentals=0),
        name="pair",
    )(rows.reshape(slots, count // 8, 8, width))
    return list(pairs)


def synthesize(trig, whole, extra, first, pieces, grid):
    lons, depth = trig.shape
    piece, pairs = extra[0].shape[-3], sum(pieces)
    width = extra[0].shape[-1]
    step = next(n for n in (10, 8, 6, 4, 2) if piece % n == 0 and first % n == 0)
    ahead = first // step

    def spec(array, shift):
        lead = array.shape[:-3]
        block = lead + (step,) + array.shape[-2:]
        return pl.BlockSpec(block, lambda i: (0,) * len(lead) + (shift + i, 0, 0))

    operands = [trig, *whole, *extra]
    in_specs = [pl.BlockSpec((lons, depth), lambda i: (0, 0))]
    in_specs += [spec(array, ahead) for array in whole] + [spec(array, 0) for array in extra]
    if grid is not None:
        operands.append(grid)
        in_specs.append(pl.BlockSpec(memory_space=pl.ANY))
    return pl.pallas_call(
        zonal_kernel if grid is None else zonal_tail_kernel,
        out_shape=jax.ShapeDtypeStruct((lons, pairs * width), bf16),
        grid=(piece // step,),
        in_specs=in_specs,
        out_specs=pl.BlockSpec((lons, step * width), lambda i: (0, ahead + i)),
        input_output_aliases={} if grid is None else {len(operands) - 1: 0},
        compiler_params=params(),
        cost_estimate=pl.CostEstimate(
            flops=4 * lons * depth * piece * width, bytes_accessed=2 * lons * piece * width, transcendentals=0
        ),
        name="zonal",
    )(*operands)


def on_device(fourier_rows, legendre, wavenumber, lower_diag, main_diag, upper_diag):
    lat_count = lax.axis_size("lat")
    wave_count = lax.axis_size("wave")
    lat_pos = lax.axis_index("lat")
    wave_pos = lax.axis_index("wave")
    group_slots, row_count, row_width = fourier_rows.shape
    pair_count = legendre.shape[2]
    lat_rows = 2 * pair_count
    chunks = group_slots // lat_count
    steps = pair_count // BLOCKS

    slot_ids = wavenumber.reshape(wave_count, chunks, lat_count)
    own_group = lax.dynamic_index_in_dim(slot_ids, wave_pos, 0, keepdims=False)
    wave_ids = lax.dynamic_index_in_dim(own_group, lat_pos, 1, keepdims=False)

    def own(band):
        return lax.dynamic_index_in_dim(
            band.reshape(chunks, lat_count, 2, pair_count), lat_pos, 1, keepdims=False
        )

    column_ids = jnp.arange(pair_count, dtype=jnp.int32)
    parity_ids = jnp.arange(2, dtype=jnp.int32)
    degree_int = wave_ids[:, None, None] + 2 * column_ids[None, None, :] + parity_ids[None, :, None]
    inside_mask = degree_int < lat_rows
    inside = inside_mask.astype(f32)
    degree = degree_int.astype(f32)
    degree_ratio = degree * (degree + 1.0) / (lat_rows * (lat_rows - 1.0))
    damping = 1.0 / (1.0 + damping_rate * degree_ratio * degree_ratio)
    not_first = (column_ids > 0).astype(f32)
    not_last = (column_ids < pair_count - 1).astype(f32)
    sub_band = own(lower_diag) * inside * not_first
    super_band = own(upper_diag) * inside * not_last
    center = jnp.where(inside_mask, own(main_diag), 1.0)
    bands = jnp.stack([sub_band, center, super_band, inside, damping], axis=2)
    factors, links = make_factors(bands.reshape(2 * chunks, 5, BLOCKS, steps))
    factors = factors.reshape(chunks, 2, 6, BLOCKS, steps)
    links = links.reshape(chunks, 2, 6, BLOCKS, 128)

    def outgoing(rows, table, j):
        pick = slice(j * lat_count, (j + 1) * lat_count)
        return jnp.concatenate([rows[pick], table[pick].astype(bf16)], axis=2)

    def swap_lat(values):
        return lax.all_to_all(values, "lat", split_axis=0, concat_axis=0, tiled=True)

    def gather_waves(values):
        return lax.all_gather(values, "wave", axis=0)

    def from_waves(values):
        return [values] + [
            lax.ppermute(values, "wave", [(w, (w + k) % wave_count) for w in range(wave_count)])
            for k in range(1, wave_count)
        ]

    def wave_rows(arrived, j):
        arrived = arrived.reshape(2, pair_count, row_width + pair_count)
        return wave_step(arrived, factors[j], links[j], row_width).reshape(lat_count, row_count, row_width)

    first_out = outgoing(fourier_rows, legendre, 0)
    rows_later, table_later, _ = lax.optimization_barrier((fourier_rows, legendre, first_out))
    ready = wave_rows(swap_lat(first_out), 0)
    first_rows = gather_waves(ready)
    pieces = cut_pairs(row_count)
    whole, last = [], []
    for j in range(1, chunks):
        out, _ = lax.optimization_barrier((outgoing(rows_later, table_later, j), ready))
        home = wave_rows(swap_lat(out), j)
        pairs = pair_rows(swap_lat(home), pieces if j == chunks - 1 else [row_count // 2])
        ready = pairs[0]
        if j == chunks - 1:
            last = pairs
        else:
            whole.append(gather_waves(ready))
    last_gathered = gather_waves(last[0])
    first_stack, _ = lax.optimization_barrier((first_rows.swapaxes(0, 1), ready))
    first_stack = swap_lat(first_stack).reshape(lat_count * wave_count, row_count, row_width)
    whole = pair_rows(first_stack, [row_count // 2]) + whole

    lon_dev = NLON // wave_count
    lon_ids = wave_pos * lon_dev + jnp.arange(lon_dev, dtype=jnp.int32)
    blocks = [slot_ids[:, 0].T.reshape(-1)]
    blocks += [slot_ids[w, j] for j in range(1, chunks) for w in range(wave_count)]
    grid = synthesize(zonal_matrix(blocks, lon_ids), whole, [last_gathered], 0, pieces, None)
    if len(pieces) > 1:
        rest, _, _ = lax.optimization_barrier((last[1], last_gathered, whole[0]))
        sources = (wave_pos - jnp.arange(wave_count)) % wave_count
        seen_ids = slot_ids[sources, chunks - 1]
        blocks = blocks[:-wave_count] + [seen_ids[k] for k in range(wave_count)]
        grid = synthesize(zonal_matrix(blocks, lon_ids), whole, from_waves(rest), pieces[0], pieces, grid)
    return grid


def solution(mesh):
    placed = (
        P("wave", "lat", None),
        P("wave", "lat", None),
        P(),
        P("wave", None),
        P("wave", None),
        P("wave", None),
    )
    return jax.shard_map(
        on_device, mesh=mesh, in_specs=placed, out_specs=P("wave", "lat"), check_vma=False
    )
```

```python
import functools
import math

import jax
import jax.numpy as jnp
from jax import lax
from jax.experimental import pallas as pl
from jax.experimental.pallas import tpu as pltpu
from jax.sharding import PartitionSpec as P

NLON = 3200
LEV = 64
damping_rate = 4.0
BLOCKS = 8
VMEM_LIMIT = 56 * 2**20
f32 = jnp.float32
bf16 = jnp.bfloat16


def zonal_matrix(blocks, lon_ids):
    wave_ids = jnp.concatenate([jnp.concatenate([ids, ids]) for ids in blocks])
    is_sine = jnp.concatenate([jnp.arange(2 * ids.size) >= ids.size for ids in blocks])
    phase_index = lon_ids[:, None] * wave_ids[None, :] % NLON
    phase_angle = phase_index.astype(f32) * (2.0 * math.pi / NLON)
    return jnp.where(is_sine[None, :], -jnp.sin(phase_angle), jnp.cos(phase_angle)).astype(bf16)


def factor_kernel(bands_ref, factors_ref, links_ref):
    systems, _, _, steps = bands_ref.shape
    sub, center, sup, inside, damping = (bands_ref[:, n] for n in range(5))
    lanes = lax.broadcasted_iota(jnp.int32, (systems, BLOCKS, steps), 2)

    def column(values, i):
        return values[:, :, i : i + 1]

    def place(values, i, new):
        return jnp.where(lanes == i, new, values)

    zero = jnp.zeros((systems, BLOCKS, steps), f32)
    inv, scaled_sub, scaled_sup, left, right = zero, zero, zero, zero, zero
    for i in range(steps):
        pivot = column(center, i)
        if i:
            pivot = pivot - column(sub, i) * sup_part
        inv_part = 1.0 / pivot
        sub_part = column(sub, i) * inv_part
        sup_part = column(sup, i) * inv_part
        left_part = -sub_part * left_part if i else sub_part
        inv = place(inv, i, inv_part)
        scaled_sub = place(scaled_sub, i, sub_part)
        scaled_sup = place(scaled_sup, i, sup_part)
        left = place(left, i, left_part)
    solved_left = zero
    for i in reversed(range(steps)):
        if i == steps - 1:
            right_part = column(scaled_sup, i)
            left_part = column(left, i)
        else:
            right_part = -column(scaled_sup, i) * right_part
            left_part = column(left, i) - column(scaled_sup, i) * left_part
        right = place(right, i, right_part)
        solved_left = place(solved_left, i, left_part)
    for n, values in enumerate((inv * inside, scaled_sub, scaled_sup, right, solved_left, damping * inside)):
        factors_ref[:, n] = values
    right_first, right_last = column(right, 0), column(right, steps - 1)
    left_first, left_last = column(solved_left, 0), column(solved_left, steps - 1)
    beta = jnp.zeros((systems, 1, 1), f32)
    width = links_ref.shape[-1]
    for b in range(BLOCKS):
        row = slice(b, b + 1)
        scale = 1.0 / (1.0 - left_first[:, row] * beta)
        step = right_first[:, row] * scale
        across = left_last[:, row] * beta
        beta = right_last[:, row] + across * step
        for n, value in enumerate((scale, left_first[:, row] * scale, step, left_last[:, row], across, beta)):
            links_ref[:, n, b : b + 1, :] = jnp.broadcast_to(value, (systems, 1, width))


def outgoing_kernel(rows_ref, table_ref, out_ref):
    width = rows_ref.shape[-1]
    out_ref[:, :, :width] = rows_ref[...]
    out_ref[:, :, width:] = table_ref[...].astype(bf16)


def wave_kernel(arrived_ref, factors_ref, links_ref, home_ref, spec, part):
    _, pair_count, width = home_ref.shape
    steps = pair_count // BLOCKS
    tiles = width // 128
    north = arrived_ref[0, :, :width].astype(f32)
    south = arrived_ref[1, :, :width].astype(f32)
    for p in range(2):
        folded = (north + south if p == 0 else north - south).astype(bf16)
        spectral = jnp.dot(arrived_ref[p, :, width:], folded, preferred_element_type=f32)
        for t in range(tiles):
            spec[p, t] = spectral[:, 128 * t : 128 * t + 128]

    def spec_rows(p, i):
        return jnp.concatenate([spec[p, t, pl.ds(i, BLOCKS, stride=steps), :] for t in range(tiles)], axis=1)

    def factor(p, n, i):
        return factors_ref[p, n, :, i : i + 1]

    running = [None, None]
    for i in range(steps):
        for p in range(2):
            value = spec_rows(p, i) * factor(p, 0, i)
            if i:
                value = value - factor(p, 1, i) * running[p]
            part[p, i] = value
            running[p] = value
    last = list(running)
    for i in reversed(range(steps - 1)):
        for p in range(2):
            value = part[p, i] - factor(p, 2, i) * running[p]
            part[p, i] = value
            running[p] = value
    first = running
    after, before = [], []
    for p in range(2):
        def link(n, b):
            return jnp.concatenate([links_ref[p, n, b : b + 1, :]] * tiles, axis=1)

        alpha = jnp.zeros((1, width), f32)
        heads, tails = [], []
        for b in range(BLOCKS):
            row = slice(b, b + 1)
            head = first[p][row] * link(0, b) - link(1, b) * alpha
            alpha = last[p][row] - link(3, b) * alpha + link(4, b) * head
            heads.append(head)
            tails.append(alpha)
        ahead = jnp.zeros((1, width), f32)
        next_heads, prev_tails = [None] * BLOCKS, [jnp.zeros((1, width), f32)] * BLOCKS
        for b in reversed(range(BLOCKS)):
            next_heads[b] = ahead
            if b + 1 < BLOCKS:
                prev_tails[b + 1] = tails[b] - link(5, b) * ahead
            ahead = heads[b] - link(2, b) * ahead
        after.append(jnp.concatenate(next_heads, axis=0))
        before.append(jnp.concatenate(prev_tails, axis=0))
    half = lax.broadcasted_iota(jnp.int32, (BLOCKS, width), 1) % (width // 2)
    untouched = half < LEV
    for i in range(steps):
        for p in range(2):
            solved = part[p, i] - factor(p, 3, i) * after[p] - factor(p, 4, i) * before[p]
            damped = jnp.where(untouched, spec_rows(p, i), solved) * factor(p, 5, i)
            for t in range(tiles):
                spec[p, t, pl.ds(i, BLOCKS, stride=steps), :] = damped[:, 128 * t : 128 * t + 128]
    parts = []
    for p in range(2):
        damped = jnp.concatenate([spec[p, t].astype(bf16) for t in range(tiles)], axis=1)
        parts.append(
            lax.dot_general(
                arrived_ref[p, :, width:], damped, (((0,), (0,)), ((), ())), preferred_element_type=f32
            )
        )
    home_ref[0] = (parts[0] + parts[1]).astype(bf16)
    home_ref[1] = (parts[0] - parts[1]).astype(bf16)


def pair_kernel(rows_ref, *pairs_refs):
    slots, groups, rows, width = rows_ref.shape
    order = slots * rows
    out_row = lax.broadcasted_iota(jnp.int32, (order, order), 0)
    in_row = lax.broadcasted_iota(jnp.int32, (order, order), 1)
    odd, rest = out_row // (order // 2), out_row % (order // 2)
    source = (rest % slots) * rows + 2 * (rest // slots) + odd
    shuffle = (in_row == source).astype(bf16)
    first_half = lax.broadcasted_iota(jnp.int32, (order // 2, width), 1) < width // 2

    def swap(values):
        return jnp.concatenate([values[:, width // 2 :], values[:, : width // 2]], axis=1)

    places = [ref.at[n] for ref in pairs_refs for n in range(ref.shape[0])]
    for g in range(groups):
        block = rows_ref[:, g].astype(f32).reshape(order, width).astype(bf16)
        moved = jnp.dot(shuffle, block, preferred_element_type=f32)
        even_rows, odd_rows = moved[: order // 2], moved[order // 2 :]
        real = jnp.where(first_half, even_rows, swap(odd_rows)).reshape(rows // 2, slots, width)
        imag = jnp.where(first_half, swap(even_rows), odd_rows).reshape(rows // 2, slots, width)
        both = jnp.concatenate([real, imag], axis=1).astype(bf16)
        for n in range(rows // 2):
            places[g * (rows // 2) + n][...] = both[n]


def zonal_kernel(trig_ref, *refs):
    grid_ref = refs[-1]
    pairs, width = refs[0].shape[-3], refs[0].shape[-1]

    def coefficients(r):
        found = []
        for ref in refs[:-1]:
            found += [ref[r]] if ref.ndim == 3 else [ref[z, r] for z in range(ref.shape[0])]
        return jnp.concatenate(found, axis=0)

    for r in range(0, pairs, 2):
        rhs = jnp.concatenate([coefficients(r), coefficients(r + 1)], axis=1)
        sums = jnp.dot(trig_ref[...], rhs, preferred_element_type=f32)
        grid_ref[:, r * width : (r + 2) * width] = sums.astype(bf16)


def zonal_tail_kernel(trig_ref, *refs):
    zonal_kernel(trig_ref, *refs[:-2], refs[-1])


def params():
    return pltpu.CompilerParams(vmem_limit_bytes=VMEM_LIMIT)


def whole_vmem(count):
    return [pl.BlockSpec(memory_space=pltpu.VMEM)] * count


def make_factors(bands):
    systems, _, _, steps = bands.shape
    return pl.pallas_call(
        factor_kernel,
        out_shape=(
            jax.ShapeDtypeStruct((systems, 6, BLOCKS, steps), f32),
            jax.ShapeDtypeStruct((systems, 6, BLOCKS, 128), f32),
        ),
        in_specs=whole_vmem(1),
        out_specs=tuple(whole_vmem(2)),
        compiler_params=params(),
        cost_estimate=pl.CostEstimate(flops=2_000_000_000, bytes_accessed=2_000_000, transcendentals=0),
        name="factor",
    )(bands)


def outgoing(fourier_rows, legendre, slots, j):
    _, rows, width = fourier_rows.shape
    pair_count = legendre.shape[2]

    def spec(columns, first):
        return pl.BlockSpec((1, rows, columns), lambda i: (first + i, 0, 0))

    return pl.pallas_call(
        outgoing_kernel,
        out_shape=jax.ShapeDtypeStruct((slots, rows, width + pair_count), bf16),
        grid=(slots,),
        in_specs=[spec(width, j * slots), spec(pair_count, j * slots)],
        out_specs=spec(width + pair_count, 0),
        compiler_params=params(),
        cost_estimate=pl.CostEstimate(
            flops=0, bytes_accessed=slots * rows * (4 * width + 6 * pair_count), transcendentals=0
        ),
        name="outgoing",
    )(fourier_rows, legendre)


def wave_step(arrived, factors, links, width):
    _, pair_count, _ = arrived.shape
    return pl.pallas_call(
        wave_kernel,
        out_shape=jax.ShapeDtypeStruct((2, pair_count, width), bf16),
        in_specs=whole_vmem(3),
        out_specs=whole_vmem(1)[0],
        scratch_shapes=[
            pltpu.VMEM((2, width // 128, pair_count, 128), f32),
            pltpu.VMEM((2, pair_count // BLOCKS, BLOCKS, width), f32),
        ],
        compiler_params=params(),
        cost_estimate=pl.CostEstimate(flops=8_000_000_000, bytes_accessed=6_000_000, transcendentals=0),
        name="wave",
    )(arrived, factors, links)


def cut_pairs(count):
    pairs = count // 2
    return [pairs * 4 // 5, pairs // 5] if pairs % 10 == 0 and count % 8 == 0 else [pairs]


def pair_rows(rows, pieces):
    slots, count, width = rows.shape
    if count % 8 or slots % 8:
        split = rows.reshape(slots, count // 2, 2, 2, width // 2)
        joined = split.transpose(1, 3, 0, 2, 4).reshape(count // 2, 2 * slots, width)
        return [joined[sum(pieces[:n]) : sum(pieces[: n + 1])] for n in range(len(pieces))]
    pairs = pl.pallas_call(
        pair_kernel,
        out_shape=[jax.ShapeDtypeStruct((piece, 2 * slots, width), bf16) for piece in pieces],
        in_specs=whole_vmem(1),
        out_specs=whole_vmem(len(pieces)),
        compiler_params=params(),
        cost_estimate=pl.CostEstimate(flops=2_000_000_000, bytes_accessed=2_400_000, transcendentals=0),
        name="pair",
    )(rows.reshape(slots, count // 8, 8, width))
    return list(pairs)


def synthesize(trig, whole, extra, first, pieces, grid):
    lons, depth = trig.shape
    piece, pairs = extra[0].shape[-3], sum(pieces)
    width = extra[0].shape[-1]
    step = next(n for n in (10, 8, 6, 4, 2) if piece % n == 0 and first % n == 0)
    ahead = first // step

    def spec(array, shift):
        lead = array.shape[:-3]
        block = lead + (step,) + array.shape[-2:]
        return pl.BlockSpec(block, lambda i: (0,) * len(lead) + (shift + i, 0, 0))

    operands = [trig, *whole, *extra]
    in_specs = [pl.BlockSpec((lons, depth), lambda i: (0, 0))]
    in_specs += [spec(array, ahead) for array in whole] + [spec(array, 0) for array in extra]
    if grid is not None:
        operands.append(grid)
        in_specs.append(pl.BlockSpec(memory_space=pl.ANY))
    return pl.pallas_call(
        zonal_kernel if grid is None else zonal_tail_kernel,
        out_shape=jax.ShapeDtypeStruct((lons, pairs * width), bf16),
        grid=(piece // step,),
        in_specs=in_specs,
        out_specs=pl.BlockSpec((lons, step * width), lambda i: (0, ahead + i)),
        input_output_aliases={} if grid is None else {len(operands) - 1: 0},
        compiler_params=params(),
        cost_estimate=pl.CostEstimate(
            flops=4 * lons * depth * piece * width, bytes_accessed=2 * lons * piece * width, transcendentals=0
        ),
        name="zonal",
    )(*operands)


def on_device(fourier_rows, legendre, wavenumber, lower_diag, main_diag, upper_diag):
    lat_count = lax.axis_size("lat")
    wave_count = lax.axis_size("wave")
    lat_pos = lax.axis_index("lat")
    wave_pos = lax.axis_index("wave")
    group_slots, row_count, row_width = fourier_rows.shape
    pair_count = legendre.shape[2]
    lat_rows = 2 * pair_count
    chunks = group_slots // lat_count
    steps = pair_count // BLOCKS

    slot_ids = wavenumber.reshape(wave_count, chunks, lat_count)
    own_group = lax.dynamic_index_in_dim(slot_ids, wave_pos, 0, keepdims=False)
    wave_ids = lax.dynamic_index_in_dim(own_group, lat_pos, 1, keepdims=False)

    def own(band):
        return lax.dynamic_index_in_dim(
            band.reshape(chunks, lat_count, 2, pair_count), lat_pos, 1, keepdims=False
        )

    column_ids = jnp.arange(pair_count, dtype=jnp.int32)
    parity_ids = jnp.arange(2, dtype=jnp.int32)
    degree_int = wave_ids[:, None, None] + 2 * column_ids[None, None, :] + parity_ids[None, :, None]
    inside_mask = degree_int < lat_rows
    inside = inside_mask.astype(f32)
    degree = degree_int.astype(f32)
    degree_ratio = degree * (degree + 1.0) / (lat_rows * (lat_rows - 1.0))
    damping = 1.0 / (1.0 + damping_rate * degree_ratio * degree_ratio)
    not_first = (column_ids > 0).astype(f32)
    not_last = (column_ids < pair_count - 1).astype(f32)
    sub_band = own(lower_diag) * inside * not_first
    super_band = own(upper_diag) * inside * not_last
    center = jnp.where(inside_mask, own(main_diag), 1.0)
    bands = jnp.stack([sub_band, center, super_band, inside, damping], axis=2)
    factors, links = make_factors(bands.reshape(2 * chunks, 5, BLOCKS, steps))
    factors = factors.reshape(chunks, 2, 6, BLOCKS, steps)
    links = links.reshape(chunks, 2, 6, BLOCKS, 128)

    def swap_lat(values):
        return lax.all_to_all(values, "lat", split_axis=0, concat_axis=0, tiled=True)

    def gather_waves(values):
        return lax.all_gather(values, "wave", axis=0)

    def from_waves(values):
        return [values] + [
            lax.ppermute(values, "wave", [(w, (w + k) % wave_count) for w in range(wave_count)])
            for k in range(1, wave_count)
        ]

    def wave_rows(arrived, j):
        arrived = arrived.reshape(2, pair_count, row_width + pair_count)
        return wave_step(arrived, factors[j], links[j], row_width).reshape(lat_count, row_count, row_width)

    first_out = outgoing(fourier_rows, legendre, lat_count, 0)
    rows_later, table_later, first_out = lax.optimization_barrier((fourier_rows, legendre, first_out))
    ready = wave_rows(swap_lat(first_out), 0)
    pieces = cut_pairs(row_count)
    gathered, rest = [], None
    for j in range(1, chunks):
        out, ready = lax.optimization_barrier((outgoing(rows_later, table_later, lat_count, j), ready))
        gathered.append(gather_waves(ready))
        home = wave_rows(swap_lat(out), j)
        ready, *rest = pair_rows(swap_lat(home), pieces if j == chunks - 1 else [row_count // 2])
    first_rows, ready = lax.optimization_barrier((gathered[0], ready))
    last = gather_waves(ready)
    first_rows = swap_lat(first_rows.swapaxes(0, 1)).reshape(lat_count * wave_count, row_count, row_width)
    whole = pair_rows(first_rows, [row_count // 2]) + gathered[1:]

    lon_dev = NLON // wave_count
    lon_ids = wave_pos * lon_dev + jnp.arange(lon_dev, dtype=jnp.int32)
    blocks = [slot_ids[:, 0].T.reshape(-1)]
    blocks += [slot_ids[w, j] for j in range(1, chunks) for w in range(wave_count)]
    trig = zonal_matrix(blocks, lon_ids)
    if not rest:
        return synthesize(trig, whole, [last], 0, pieces, None)
    sources = (wave_pos - jnp.arange(wave_count)) % wave_count
    seen_ids = slot_ids[sources, chunks - 1]
    rest_trig = zonal_matrix(blocks[:-wave_count] + [seen_ids[k] for k in range(wave_count)], lon_ids)
    rest, last, trig, rest_trig, *whole = lax.optimization_barrier((rest[0], last, trig, rest_trig, *whole))
    rest = from_waves(rest)
    grid = synthesize(trig, whole, [last], 0, pieces, None)
    return synthesize(rest_trig, whole, rest, pieces[0], pieces, grid)


def solution(mesh):
    placed = (
        P("wave", "lat", None),
        P("wave", "lat", None),
        P(),
        P("wave", None),
        P("wave", None),
        P("wave", None),
    )
    return jax.shard_map(
        on_device, mesh=mesh, in_specs=placed, out_specs=P("wave", "lat"), check_vma=False
    )
```

```python
import functools
import math

import jax
import jax.numpy as jnp
from jax import lax
from jax.experimental import pallas as pl
from jax.experimental.pallas import tpu as pltpu
from jax.sharding import PartitionSpec as P

NLON = 3200
LEV = 64
damping_rate = 4.0
BLOCKS = 8
VMEM_LIMIT = 56 * 2**20
f32 = jnp.float32
bf16 = jnp.bfloat16


def zonal_matrix(blocks, lon_ids):
    wave_ids = jnp.concatenate([jnp.concatenate([ids, ids]) for ids in blocks])
    is_sine = jnp.concatenate([jnp.arange(2 * ids.size) >= ids.size for ids in blocks])
    phase_index = lon_ids[:, None] * wave_ids[None, :] % NLON
    phase_angle = phase_index.astype(f32) * (2.0 * math.pi / NLON)
    return jnp.where(is_sine[None, :], -jnp.sin(phase_angle), jnp.cos(phase_angle)).astype(bf16)


def factor_kernel(bands_ref, factors_ref, links_ref):
    systems, _, _, steps = bands_ref.shape
    sub, center, sup, inside, damping = (bands_ref[:, n] for n in range(5))
    lanes = lax.broadcasted_iota(jnp.int32, (systems, BLOCKS, steps), 2)

    def column(values, i):
        return values[:, :, i : i + 1]

    def place(values, i, new):
        return jnp.where(lanes == i, new, values)

    zero = jnp.zeros((systems, BLOCKS, steps), f32)
    inv, scaled_sub, scaled_sup, left, right = zero, zero, zero, zero, zero
    for i in range(steps):
        pivot = column(center, i)
        if i:
            pivot = pivot - column(sub, i) * sup_part
        inv_part = 1.0 / pivot
        sub_part = column(sub, i) * inv_part
        sup_part = column(sup, i) * inv_part
        left_part = -sub_part * left_part if i else sub_part
        inv = place(inv, i, inv_part)
        scaled_sub = place(scaled_sub, i, sub_part)
        scaled_sup = place(scaled_sup, i, sup_part)
        left = place(left, i, left_part)
    solved_left = zero
    for i in reversed(range(steps)):
        if i == steps - 1:
            right_part = column(scaled_sup, i)
            left_part = column(left, i)
        else:
            right_part = -column(scaled_sup, i) * right_part
            left_part = column(left, i) - column(scaled_sup, i) * left_part
        right = place(right, i, right_part)
        solved_left = place(solved_left, i, left_part)
    for n, values in enumerate((inv * inside, scaled_sub, scaled_sup, right, solved_left, damping * inside)):
        factors_ref[:, n] = values
    right_first, right_last = column(right, 0), column(right, steps - 1)
    left_first, left_last = column(solved_left, 0), column(solved_left, steps - 1)
    beta = jnp.zeros((systems, 1, 1), f32)
    width = links_ref.shape[-1]
    for b in range(BLOCKS):
        row = slice(b, b + 1)
        scale = 1.0 / (1.0 - left_first[:, row] * beta)
        step = right_first[:, row] * scale
        across = left_last[:, row] * beta
        beta = right_last[:, row] + across * step
        for n, value in enumerate((scale, left_first[:, row] * scale, step, left_last[:, row], across, beta)):
            links_ref[:, n, b : b + 1, :] = jnp.broadcast_to(value, (systems, 1, width))


def outgoing_kernel(rows_ref, table_ref, out_ref):
    width = rows_ref.shape[-1]
    out_ref[:, :, :width] = rows_ref[...]
    out_ref[:, :, width:] = table_ref[...].astype(bf16)


def wave_kernel(arrived_ref, factors_ref, links_ref, home_ref, spec, part):
    _, pair_count, width = home_ref.shape
    steps = pair_count // BLOCKS
    tiles = width // 128
    north = arrived_ref[0, :, :width].astype(f32)
    south = arrived_ref[1, :, :width].astype(f32)
    for p in range(2):
        folded = (north + south if p == 0 else north - south).astype(bf16)
        spectral = jnp.dot(arrived_ref[p, :, width:], folded, preferred_element_type=f32)
        for t in range(tiles):
            spec[p, t] = spectral[:, 128 * t : 128 * t + 128]

    def spec_rows(p, i):
        return jnp.concatenate([spec[p, t, pl.ds(i, BLOCKS, stride=steps), :] for t in range(tiles)], axis=1)

    def factor(p, n, i):
        return factors_ref[p, n, :, i : i + 1]

    running = [None, None]
    for i in range(steps):
        for p in range(2):
            value = spec_rows(p, i) * factor(p, 0, i)
            if i:
                value = value - factor(p, 1, i) * running[p]
            part[p, i] = value
            running[p] = value
    last = list(running)
    for i in reversed(range(steps - 1)):
        for p in range(2):
            value = part[p, i] - factor(p, 2, i) * running[p]
            part[p, i] = value
            running[p] = value
    first = running
    after, before = [], []
    for p in range(2):
        def link(n, b):
            return jnp.concatenate([links_ref[p, n, b : b + 1, :]] * tiles, axis=1)

        alpha = jnp.zeros((1, width), f32)
        heads, tails = [], []
        for b in range(BLOCKS):
            row = slice(b, b + 1)
            head = first[p][row] * link(0, b) - link(1, b) * alpha
            alpha = last[p][row] - link(3, b) * alpha + link(4, b) * head
            heads.append(head)
            tails.append(alpha)
        ahead = jnp.zeros((1, width), f32)
        next_heads, prev_tails = [None] * BLOCKS, [jnp.zeros((1, width), f32)] * BLOCKS
        for b in reversed(range(BLOCKS)):
            next_heads[b] = ahead
            if b + 1 < BLOCKS:
                prev_tails[b + 1] = tails[b] - link(5, b) * ahead
            ahead = heads[b] - link(2, b) * ahead
        after.append(jnp.concatenate(next_heads, axis=0))
        before.append(jnp.concatenate(prev_tails, axis=0))
    half = lax.broadcasted_iota(jnp.int32, (BLOCKS, width), 1) % (width // 2)
    untouched = half < LEV
    for i in range(steps):
        for p in range(2):
            solved = part[p, i] - factor(p, 3, i) * after[p] - factor(p, 4, i) * before[p]
            damped = jnp.where(untouched, spec_rows(p, i), solved) * factor(p, 5, i)
            for t in range(tiles):
                spec[p, t, pl.ds(i, BLOCKS, stride=steps), :] = damped[:, 128 * t : 128 * t + 128]
    parts = []
    for p in range(2):
        damped = jnp.concatenate([spec[p, t].astype(bf16) for t in range(tiles)], axis=1)
        parts.append(
            lax.dot_general(
                arrived_ref[p, :, width:], damped, (((0,), (0,)), ((), ())), preferred_element_type=f32
            )
        )
    home_ref[0] = (parts[0] + parts[1]).astype(bf16)
    home_ref[1] = (parts[0] - parts[1]).astype(bf16)


def pair_kernel(rows_ref, *pairs_refs):
    slots, groups, rows, width = rows_ref.shape
    order = slots * rows
    out_row = lax.broadcasted_iota(jnp.int32, (order, order), 0)
    in_row = lax.broadcasted_iota(jnp.int32, (order, order), 1)
    odd, rest = out_row // (order // 2), out_row % (order // 2)
    source = (rest % slots) * rows + 2 * (rest // slots) + odd
    shuffle = (in_row == source).astype(bf16)
    first_half = lax.broadcasted_iota(jnp.int32, (order // 2, width), 1) < width // 2

    def swap(values):
        return jnp.concatenate([values[:, width // 2 :], values[:, : width // 2]], axis=1)

    places = [ref.at[n] for ref in pairs_refs for n in range(ref.shape[0])]
    for g in range(groups):
        block = rows_ref[:, g].astype(f32).reshape(order, width).astype(bf16)
        moved = jnp.dot(shuffle, block, preferred_element_type=f32)
        even_rows, odd_rows = moved[: order // 2], moved[order // 2 :]
        real = jnp.where(first_half, even_rows, swap(odd_rows)).reshape(rows // 2, slots, width)
        imag = jnp.where(first_half, swap(even_rows), odd_rows).reshape(rows // 2, slots, width)
        both = jnp.concatenate([real, imag], axis=1).astype(bf16)
        for n in range(rows // 2):
            places[g * (rows // 2) + n][...] = both[n]


def zonal_kernel(trig_ref, *refs):
    grid_ref = refs[-1]
    pairs, width = refs[0].shape[-3], refs[0].shape[-1]

    def coefficients(r):
        found = []
        for ref in refs[:-1]:
            found += [ref[r]] if ref.ndim == 3 else [ref[z, r] for z in range(ref.shape[0])]
        return jnp.concatenate(found, axis=0)

    for r in range(0, pairs, 2):
        rhs = jnp.concatenate([coefficients(r), coefficients(r + 1)], axis=1)
        sums = jnp.dot(trig_ref[...], rhs, preferred_element_type=f32)
        grid_ref[:, r * width : (r + 2) * width] = sums.astype(bf16)


def zonal_tail_kernel(trig_ref, *refs):
    zonal_kernel(trig_ref, *refs[:-2], refs[-1])


def params():
    return pltpu.CompilerParams(vmem_limit_bytes=VMEM_LIMIT)


def whole_vmem(count):
    return [pl.BlockSpec(memory_space=pltpu.VMEM)] * count


def make_factors(bands):
    systems, _, _, steps = bands.shape
    return pl.pallas_call(
        factor_kernel,
        out_shape=(
            jax.ShapeDtypeStruct((systems, 6, BLOCKS, steps), f32),
            jax.ShapeDtypeStruct((systems, 6, BLOCKS, 128), f32),
        ),
        in_specs=whole_vmem(1),
        out_specs=tuple(whole_vmem(2)),
        compiler_params=params(),
        cost_estimate=pl.CostEstimate(flops=2_000_000_000, bytes_accessed=2_000_000, transcendentals=0),
        name="factor",
    )(bands)


def outgoing(fourier_rows, legendre, slots, j):
    _, rows, width = fourier_rows.shape
    pair_count = legendre.shape[2]

    def spec(columns, first):
        return pl.BlockSpec((1, rows, columns), lambda i: (first + i, 0, 0))

    return pl.pallas_call(
        outgoing_kernel,
        out_shape=jax.ShapeDtypeStruct((slots, rows, width + pair_count), bf16),
        grid=(slots,),
        in_specs=[spec(width, j * slots), spec(pair_count, j * slots)],
        out_specs=spec(width + pair_count, 0),
        compiler_params=params(),
        cost_estimate=pl.CostEstimate(
            flops=0, bytes_accessed=slots * rows * (4 * width + 6 * pair_count), transcendentals=0
        ),
        name="outgoing",
    )(fourier_rows, legendre)


def wave_step(arrived, factors, links, width):
    _, pair_count, _ = arrived.shape
    return pl.pallas_call(
        wave_kernel,
        out_shape=jax.ShapeDtypeStruct((2, pair_count, width), bf16),
        in_specs=whole_vmem(3),
        out_specs=whole_vmem(1)[0],
        scratch_shapes=[
            pltpu.VMEM((2, width // 128, pair_count, 128), f32),
            pltpu.VMEM((2, pair_count // BLOCKS, BLOCKS, width), f32),
        ],
        compiler_params=params(),
        cost_estimate=pl.CostEstimate(flops=8_000_000_000, bytes_accessed=6_000_000, transcendentals=0),
        name="wave",
    )(arrived, factors, links)


def cut_pairs(count):
    pairs = count // 2
    return [pairs * 4 // 5, pairs // 5] if pairs % 10 == 0 and count % 8 == 0 else [pairs]


def pair_rows(rows, pieces):
    slots, count, width = rows.shape
    if count % 8 or slots % 8:
        split = rows.reshape(slots, count // 2, 2, 2, width // 2)
        joined = split.transpose(1, 3, 0, 2, 4).reshape(count // 2, 2 * slots, width)
        return [joined[sum(pieces[:n]) : sum(pieces[: n + 1])] for n in range(len(pieces))]
    pairs = pl.pallas_call(
        pair_kernel,
        out_shape=[jax.ShapeDtypeStruct((piece, 2 * slots, width), bf16) for piece in pieces],
        in_specs=whole_vmem(1),
        out_specs=whole_vmem(len(pieces)),
        compiler_params=params(),
        cost_estimate=pl.CostEstimate(flops=2_000_000_000, bytes_accessed=2_400_000, transcendentals=0),
        name="pair",
    )(rows.reshape(slots, count // 8, 8, width))
    return list(pairs)


def synthesize(trig, whole, extra, first, pieces, grid):
    lons, depth = trig.shape
    piece, pairs = extra[0].shape[-3], sum(pieces)
    width = extra[0].shape[-1]
    step = next(n for n in (10, 8, 6, 4, 2) if piece % n == 0 and first % n == 0)
    ahead = first // step

    def spec(array, shift):
        lead = array.shape[:-3]
        block = lead + (step,) + array.shape[-2:]
        return pl.BlockSpec(block, lambda i: (0,) * len(lead) + (shift + i, 0, 0))

    operands = [trig, *whole, *extra]
    in_specs = [pl.BlockSpec((lons, depth), lambda i: (0, 0))]
    in_specs += [spec(array, ahead) for array in whole] + [spec(array, 0) for array in extra]
    if grid is not None:
        operands.append(grid)
        in_specs.append(pl.BlockSpec(memory_space=pl.ANY))
    return pl.pallas_call(
        zonal_kernel if grid is None else zonal_tail_kernel,
        out_shape=jax.ShapeDtypeStruct((lons, pairs * width), bf16),
        grid=(piece // step,),
        in_specs=in_specs,
        out_specs=pl.BlockSpec((lons, step * width), lambda i: (0, ahead + i)),
        input_output_aliases={} if grid is None else {len(operands) - 1: 0},
        compiler_params=params(),
        cost_estimate=pl.CostEstimate(
            flops=4 * lons * depth * piece * width, bytes_accessed=2 * lons * piece * width, transcendentals=0
        ),
        name="zonal",
    )(*operands)


def on_device(fourier_rows, legendre, wavenumber, lower_diag, main_diag, upper_diag):
    lat_count = lax.axis_size("lat")
    wave_count = lax.axis_size("wave")
    lat_pos = lax.axis_index("lat")
    wave_pos = lax.axis_index("wave")
    group_slots, row_count, row_width = fourier_rows.shape
    pair_count = legendre.shape[2]
    lat_rows = 2 * pair_count
    chunks = group_slots // lat_count
    steps = pair_count // BLOCKS

    slot_ids = wavenumber.reshape(wave_count, chunks, lat_count)
    own_group = lax.dynamic_index_in_dim(slot_ids, wave_pos, 0, keepdims=False)
    wave_ids = lax.dynamic_index_in_dim(own_group, lat_pos, 1, keepdims=False)

    def own(band):
        return lax.dynamic_index_in_dim(
            band.reshape(chunks, lat_count, 2, pair_count), lat_pos, 1, keepdims=False
        )

    column_ids = jnp.arange(pair_count, dtype=jnp.int32)
    parity_ids = jnp.arange(2, dtype=jnp.int32)
    degree_int = wave_ids[:, None, None] + 2 * column_ids[None, None, :] + parity_ids[None, :, None]
    inside_mask = degree_int < lat_rows
    inside = inside_mask.astype(f32)
    degree = degree_int.astype(f32)
    degree_ratio = degree * (degree + 1.0) / (lat_rows * (lat_rows - 1.0))
    damping = 1.0 / (1.0 + damping_rate * degree_ratio * degree_ratio)
    not_first = (column_ids > 0).astype(f32)
    not_last = (column_ids < pair_count - 1).astype(f32)
    sub_band = own(lower_diag) * inside * not_first
    super_band = own(upper_diag) * inside * not_last
    center = jnp.where(inside_mask, own(main_diag), 1.0)
    bands = jnp.stack([sub_band, center, super_band, inside, damping], axis=2)
    factors, links = make_factors(bands.reshape(2 * chunks, 5, BLOCKS, steps))
    factors = factors.reshape(chunks, 2, 6, BLOCKS, steps)
    links = links.reshape(chunks, 2, 6, BLOCKS, 128)

    def swap_lat(values):
        return lax.all_to_all(values, "lat", split_axis=0, concat_axis=0, tiled=True)

    def gather_waves(values):
        return lax.all_gather(values, "wave", axis=0)

    def from_waves(values):
        return [values] + [
            lax.ppermute(values, "wave", [(w, (w + k) % wave_count) for w in range(wave_count)])
            for k in range(1, wave_count)
        ]

    def wave_rows(arrived, j):
        arrived = arrived.reshape(2, pair_count, row_width + pair_count)
        home = wave_step(arrived, factors[j], links[j], row_width)
        return home.reshape(lat_count, row_count, row_width)

    first_out = outgoing(fourier_rows, legendre, lat_count, 0)
    rows_later, table_later, first_out = lax.optimization_barrier((fourier_rows, legendre, first_out))
    ready = wave_rows(swap_lat(first_out), 0)
    pieces = cut_pairs(row_count)
    gathered, permuted, rest, waiting = [], [], [], []
    for j in range(1, chunks):
        out = outgoing(rows_later, table_later, lat_count, j)
        done = gathered[: j - 2] if j > 2 else []
        out, ready, rest, waiting, done = lax.optimization_barrier((out, ready, rest, waiting, done))
        gathered[: len(done)] = done
        permuted += waiting
        gathered.append(gather_waves(ready))
        waiting = from_waves(rest[0]) if rest else []
        home = wave_rows(swap_lat(out), j)
        ready, *rest = pair_rows(swap_lat(home), pieces)
    last = gather_waves(ready)
    gathered, rest, waiting = lax.optimization_barrier((gathered, rest, waiting))
    first_rows, *gathered = gathered
    gathered.append(last)
    permuted += waiting
    first_rows = swap_lat(first_rows.swapaxes(0, 1)).reshape(lat_count * wave_count, row_count, row_width)
    whole = pair_rows(first_rows, [row_count // 2])

    lon_dev = NLON // wave_count
    lon_ids = wave_pos * lon_dev + jnp.arange(lon_dev, dtype=jnp.int32)
    first_ids = [slot_ids[:, 0].T.reshape(-1)]
    blocks = [slot_ids[w, j] for j in range(1, chunks) for w in range(wave_count)]
    trig = zonal_matrix(first_ids + blocks, lon_ids)
    if not rest:
        return synthesize(trig, whole, gathered, 0, pieces, None)
    seen_ids = slot_ids[(wave_pos - jnp.arange(wave_count)) % wave_count]
    blocks = [seen_ids[k, j] for j in range(1, chunks) for k in range(wave_count)]
    rest_trig = zonal_matrix(first_ids + blocks, lon_ids)
    rest, trig, rest_trig, *held = lax.optimization_barrier((rest[0], trig, rest_trig, *whole, *gathered))
    whole, gathered = held[:1], held[1:]
    permuted += from_waves(rest)
    grid = synthesize(trig, whole, gathered, 0, pieces, None)
    return synthesize(rest_trig, whole, permuted, pieces[0], pieces, grid)


def solution(mesh):
    placed = (
        P("wave", "lat", None),
        P("wave", "lat", None),
        P(),
        P("wave", None),
        P("wave", None),
        P("wave", None),
    )
    return jax.shard_map(
        on_device, mesh=mesh, in_specs=placed, out_specs=P("wave", "lat"), check_vma=False
    )
```

```python
import functools
import math

import jax
import jax.numpy as jnp
from jax import lax
from jax.experimental import pallas as pl
from jax.experimental.pallas import tpu as pltpu
from jax.sharding import PartitionSpec as P

NLON = 3200
LEV = 64
damping_rate = 4.0
BLOCKS = 8
VMEM_LIMIT = 56 * 2**20
f32 = jnp.float32
bf16 = jnp.bfloat16


def zonal_matrix(blocks, lon_ids):
    wave_ids = jnp.concatenate([jnp.concatenate([ids, ids]) for ids in blocks])
    is_sine = jnp.concatenate([jnp.arange(2 * ids.size) >= ids.size for ids in blocks])
    phase_index = lon_ids[:, None] * wave_ids[None, :] % NLON
    phase_angle = phase_index.astype(f32) * (2.0 * math.pi / NLON)
    return jnp.where(is_sine[None, :], -jnp.sin(phase_angle), jnp.cos(phase_angle)).astype(bf16)


def factor_kernel(bands_ref, factors_ref, links_ref):
    systems, _, _, steps = bands_ref.shape
    sub, center, sup, inside, damping = (bands_ref[:, n] for n in range(5))
    lanes = lax.broadcasted_iota(jnp.int32, (systems, BLOCKS, steps), 2)

    def column(values, i):
        return values[:, :, i : i + 1]

    def place(values, i, new):
        return jnp.where(lanes == i, new, values)

    zero = jnp.zeros((systems, BLOCKS, steps), f32)
    inv, scaled_sub, scaled_sup, left, right = zero, zero, zero, zero, zero
    for i in range(steps):
        pivot = column(center, i)
        if i:
            pivot = pivot - column(sub, i) * sup_part
        inv_part = 1.0 / pivot
        sub_part = column(sub, i) * inv_part
        sup_part = column(sup, i) * inv_part
        left_part = -sub_part * left_part if i else sub_part
        inv = place(inv, i, inv_part)
        scaled_sub = place(scaled_sub, i, sub_part)
        scaled_sup = place(scaled_sup, i, sup_part)
        left = place(left, i, left_part)
    solved_left = zero
    for i in reversed(range(steps)):
        if i == steps - 1:
            right_part = column(scaled_sup, i)
            left_part = column(left, i)
        else:
            right_part = -column(scaled_sup, i) * right_part
            left_part = column(left, i) - column(scaled_sup, i) * left_part
        right = place(right, i, right_part)
        solved_left = place(solved_left, i, left_part)
    for n, values in enumerate((inv * inside, scaled_sub, scaled_sup, right, solved_left, damping * inside)):
        factors_ref[:, n] = values
    right_first, right_last = column(right, 0), column(right, steps - 1)
    left_first, left_last = column(solved_left, 0), column(solved_left, steps - 1)
    beta = jnp.zeros((systems, 1, 1), f32)
    width = links_ref.shape[-1]
    for b in range(BLOCKS):
        row = slice(b, b + 1)
        scale = 1.0 / (1.0 - left_first[:, row] * beta)
        step = right_first[:, row] * scale
        across = left_last[:, row] * beta
        beta = right_last[:, row] + across * step
        for n, value in enumerate((scale, left_first[:, row] * scale, step, left_last[:, row], across, beta)):
            links_ref[:, n, b : b + 1, :] = jnp.broadcast_to(value, (systems, 1, width))


def outgoing_kernel(first, rows_hbm, table_hbm, out_hbm, table, joined, rows_sems, table_sems, out_sems):
    slots, _, width = joined.shape[0], joined.shape[1], rows_hbm.shape[2]
    copies = []
    for s in range(slots):
        copies.append(pltpu.make_async_copy(table_hbm.at[first + s], table.at[s], table_sems.at[s]))
        copies.append(
            pltpu.make_async_copy(rows_hbm.at[first + s], joined.at[s, :, pl.ds(0, width)], rows_sems.at[s])
        )
    for copy in copies:
        copy.start()
    sends = []
    for s in range(slots):
        copies[2 * s].wait()
        joined[s, :, width:] = table[s].astype(bf16)
        copies[2 * s + 1].wait()
        sends.append(pltpu.make_async_copy(joined.at[s], out_hbm.at[s], out_sems.at[s]))
        sends[s].start()
    for send in sends:
        send.wait()


def wave_kernel(arrived_ref, factors_ref, links_ref, home_ref, spec, part):
    _, pair_count, width = home_ref.shape
    steps = pair_count // BLOCKS
    tiles = width // 128
    north = arrived_ref[0, :, :width].astype(f32)
    south = arrived_ref[1, :, :width].astype(f32)
    for p in range(2):
        folded = (north + south if p == 0 else north - south).astype(bf16)
        spectral = jnp.dot(arrived_ref[p, :, width:], folded, preferred_element_type=f32)
        for t in range(tiles):
            spec[p, t] = spectral[:, 128 * t : 128 * t + 128]

    def spec_rows(p, i):
        return jnp.concatenate([spec[p, t, pl.ds(i, BLOCKS, stride=steps), :] for t in range(tiles)], axis=1)

    def factor(p, n, i):
        return factors_ref[p, n, :, i : i + 1]

    running = [None, None]
    for i in range(steps):
        for p in range(2):
            value = spec_rows(p, i) * factor(p, 0, i)
            if i:
                value = value - factor(p, 1, i) * running[p]
            part[p, i] = value
            running[p] = value
    last = list(running)
    for i in reversed(range(steps - 1)):
        for p in range(2):
            value = part[p, i] - factor(p, 2, i) * running[p]
            part[p, i] = value
            running[p] = value
    first = running
    after, before = [], []
    for p in range(2):
        def link(n, b):
            return jnp.concatenate([links_ref[p, n, b : b + 1, :]] * tiles, axis=1)

        alpha = jnp.zeros((1, width), f32)
        heads, tails = [], []
        for b in range(BLOCKS):
            row = slice(b, b + 1)
            head = first[p][row] * link(0, b) - link(1, b) * alpha
            alpha = last[p][row] - link(3, b) * alpha + link(4, b) * head
            heads.append(head)
            tails.append(alpha)
        ahead = jnp.zeros((1, width), f32)
        next_heads, prev_tails = [None] * BLOCKS, [jnp.zeros((1, width), f32)] * BLOCKS
        for b in reversed(range(BLOCKS)):
            next_heads[b] = ahead
            if b + 1 < BLOCKS:
                prev_tails[b + 1] = tails[b] - link(5, b) * ahead
            ahead = heads[b] - link(2, b) * ahead
        after.append(jnp.concatenate(next_heads, axis=0))
        before.append(jnp.concatenate(prev_tails, axis=0))
    half = lax.broadcasted_iota(jnp.int32, (BLOCKS, width), 1) % (width // 2)
    untouched = half < LEV
    for i in range(steps):
        for p in range(2):
            solved = part[p, i] - factor(p, 3, i) * after[p] - factor(p, 4, i) * before[p]
            damped = jnp.where(untouched, spec_rows(p, i), solved) * factor(p, 5, i)
            for t in range(tiles):
                spec[p, t, pl.ds(i, BLOCKS, stride=steps), :] = damped[:, 128 * t : 128 * t + 128]
    parts = []
    for p in range(2):
        damped = jnp.concatenate([spec[p, t].astype(bf16) for t in range(tiles)], axis=1)
        parts.append(
            lax.dot_general(
                arrived_ref[p, :, width:], damped, (((0,), (0,)), ((), ())), preferred_element_type=f32
            )
        )
    home_ref[0] = (parts[0] + parts[1]).astype(bf16)
    home_ref[1] = (parts[0] - parts[1]).astype(bf16)


def pair_kernel(rows_ref, *pairs_refs):
    slots, groups, rows, width = rows_ref.shape
    order = slots * rows
    out_row = lax.broadcasted_iota(jnp.int32, (order, order), 0)
    in_row = lax.broadcasted_iota(jnp.int32, (order, order), 1)
    odd, rest = out_row // (order // 2), out_row % (order // 2)
    source = (rest % slots) * rows + 2 * (rest // slots) + odd
    shuffle = (in_row == source).astype(bf16)
    first_half = lax.broadcasted_iota(jnp.int32, (order // 2, width), 1) < width // 2

    def swap(values):
        return jnp.concatenate([values[:, width // 2 :], values[:, : width // 2]], axis=1)

    places = [ref.at[n] for ref in pairs_refs for n in range(ref.shape[0])]
    for g in range(groups):
        block = rows_ref[:, g].astype(f32).reshape(order, width).astype(bf16)
        moved = jnp.dot(shuffle, block, preferred_element_type=f32)
        even_rows, odd_rows = moved[: order // 2], moved[order // 2 :]
        real = jnp.where(first_half, even_rows, swap(odd_rows)).reshape(rows // 2, slots, width)
        imag = jnp.where(first_half, swap(even_rows), odd_rows).reshape(rows // 2, slots, width)
        both = jnp.concatenate([real, imag], axis=1).astype(bf16)
        for n in range(rows // 2):
            places[g * (rows // 2) + n][...] = both[n]


def zonal_kernel(first, trig_ref, *refs):
    *operands, grid_hbm, sums, sems = refs
    pairs, width = operands[0].shape[-3], operands[0].shape[-1]
    parts = pairs // 2
    step, steps = pl.program_id(0), pl.num_programs(0)
    slot = lax.rem(step, 2)

    def coefficients(r):
        found = []
        for ref in operands:
            found += [ref[r]] if ref.ndim == 3 else [ref[z, r] for z in range(ref.shape[0])]
        return jnp.concatenate(found, axis=0)

    def send(at_step, at_slot, n):
        column = pl.multiple_of((first + at_step * pairs + 2 * n) * width, 128)
        return pltpu.make_async_copy(
            sums.at[at_slot, n], grid_hbm.at[:, pl.ds(column, 2 * width)], sems.at[at_slot, n]
        )

    for n in range(parts):
        rhs = jnp.concatenate([coefficients(2 * n), coefficients(2 * n + 1)], axis=1)

        @pl.when(step >= 2)
        def _():
            send(step - 2, slot, n).wait()

        sums[slot, n] = jnp.dot(trig_ref[...], rhs, preferred_element_type=f32).astype(bf16)
        send(step, slot, n).start()

    @pl.when(step == steps - 1)
    def _():
        for n in range(parts):

            @pl.when(steps >= 2)
            def _():
                send(step - 1, 1 - slot, n).wait()

            send(step, slot, n).wait()


def zonal_tail_kernel(first, trig_ref, *refs):
    zonal_kernel(first, trig_ref, *refs[:-4], *refs[-3:])


def params():
    return pltpu.CompilerParams(vmem_limit_bytes=VMEM_LIMIT)


def whole_vmem(count):
    return [pl.BlockSpec(memory_space=pltpu.VMEM)] * count


def make_factors(bands):
    systems, _, _, steps = bands.shape
    return pl.pallas_call(
        factor_kernel,
        out_shape=(
            jax.ShapeDtypeStruct((systems, 6, BLOCKS, steps), f32),
            jax.ShapeDtypeStruct((systems, 6, BLOCKS, 128), f32),
        ),
        in_specs=whole_vmem(1),
        out_specs=tuple(whole_vmem(2)),
        compiler_params=params(),
        cost_estimate=pl.CostEstimate(flops=2_000_000_000, bytes_accessed=2_000_000, transcendentals=0),
        name="factor",
    )(bands)


def outgoing(fourier_rows, legendre, slots, j):
    _, rows, width = fourier_rows.shape
    pair_count = legendre.shape[2]

    anywhere = pl.BlockSpec(memory_space=pl.ANY)
    return pl.pallas_call(
        functools.partial(outgoing_kernel, j * slots),
        out_shape=jax.ShapeDtypeStruct((slots, rows, width + pair_count), bf16),
        in_specs=[anywhere, anywhere],
        out_specs=anywhere,
        scratch_shapes=[
            pltpu.VMEM((slots, rows, pair_count), f32),
            pltpu.VMEM((slots, rows, width + pair_count), bf16),
            pltpu.SemaphoreType.DMA((slots,)),
            pltpu.SemaphoreType.DMA((slots,)),
            pltpu.SemaphoreType.DMA((slots,)),
        ],
        compiler_params=params(),
        cost_estimate=pl.CostEstimate(
            flops=0, bytes_accessed=slots * rows * (4 * width + 6 * pair_count), transcendentals=0
        ),
        name="outgoing",
    )(fourier_rows, legendre)


def wave_step(arrived, factors, links, width):
    _, pair_count, _ = arrived.shape
    return pl.pallas_call(
        wave_kernel,
        out_shape=jax.ShapeDtypeStruct((2, pair_count, width), bf16),
        in_specs=whole_vmem(3),
        out_specs=whole_vmem(1)[0],
        scratch_shapes=[
            pltpu.VMEM((2, width // 128, pair_count, 128), f32),
            pltpu.VMEM((2, pair_count // BLOCKS, BLOCKS, width), f32),
        ],
        compiler_params=params(),
        cost_estimate=pl.CostEstimate(flops=8_000_000_000, bytes_accessed=6_000_000, transcendentals=0),
        name="wave",
    )(arrived, factors, links)


def cut_pairs(count):
    pairs = count // 2
    return [pairs * 4 // 5, pairs // 5] if pairs % 10 == 0 and count % 8 == 0 else [pairs]


def pair_rows(rows, pieces):
    slots, count, width = rows.shape
    if count % 8 or slots % 8:
        split = rows.reshape(slots, count // 2, 2, 2, width // 2)
        joined = split.transpose(1, 3, 0, 2, 4).reshape(count // 2, 2 * slots, width)
        return [joined[sum(pieces[:n]) : sum(pieces[: n + 1])] for n in range(len(pieces))]
    pairs = pl.pallas_call(
        pair_kernel,
        out_shape=[jax.ShapeDtypeStruct((piece, 2 * slots, width), bf16) for piece in pieces],
        in_specs=whole_vmem(1),
        out_specs=whole_vmem(len(pieces)),
        compiler_params=params(),
        cost_estimate=pl.CostEstimate(flops=2_000_000_000, bytes_accessed=2_400_000, transcendentals=0),
        name="pair",
    )(rows.reshape(slots, count // 8, 8, width))
    return list(pairs)


def synthesize(trig, whole, extra, first, pieces, grid):
    lons, depth = trig.shape
    piece, pairs = extra[0].shape[-3], sum(pieces)
    width = extra[0].shape[-1]
    step = next(n for n in (10, 8, 6, 4, 2) if piece % n == 0 and first % n == 0)
    ahead = first // step

    def spec(array, shift):
        lead = array.shape[:-3]
        block = lead + (step,) + array.shape[-2:]
        return pl.BlockSpec(block, lambda i: (0,) * len(lead) + (shift + i, 0, 0))

    operands = [trig, *whole, *extra]
    in_specs = [pl.BlockSpec((lons, depth), lambda i: (0, 0))]
    in_specs += [spec(array, ahead) for array in whole] + [spec(array, 0) for array in extra]
    if grid is not None:
        operands.append(grid)
        in_specs.append(pl.BlockSpec(memory_space=pl.ANY))
    return pl.pallas_call(
        functools.partial(zonal_kernel if grid is None else zonal_tail_kernel, first),
        out_shape=jax.ShapeDtypeStruct((lons, pairs * width), bf16),
        grid=(piece // step,),
        in_specs=in_specs,
        out_specs=pl.BlockSpec(memory_space=pl.ANY),
        scratch_shapes=[
            pltpu.VMEM((2, step // 2, lons, 2 * width), bf16),
            pltpu.SemaphoreType.DMA((2, step // 2)),
        ],
        input_output_aliases={} if grid is None else {len(operands) - 1: 0},
        compiler_params=params(),
        cost_estimate=pl.CostEstimate(
            flops=4 * lons * depth * piece * width, bytes_accessed=2 * lons * piece * width, transcendentals=0
        ),
        name="zonal",
    )(*operands)


def on_device(fourier_rows, legendre, wavenumber, lower_diag, main_diag, upper_diag):
    lat_count = lax.axis_size("lat")
    wave_count = lax.axis_size("wave")
    lat_pos = lax.axis_index("lat")
    wave_pos = lax.axis_index("wave")
    group_slots, row_count, row_width = fourier_rows.shape
    pair_count = legendre.shape[2]
    lat_rows = 2 * pair_count
    chunks = group_slots // lat_count
    steps = pair_count // BLOCKS

    slot_ids = wavenumber.reshape(wave_count, chunks, lat_count)
    own_group = lax.dynamic_index_in_dim(slot_ids, wave_pos, 0, keepdims=False)
    wave_ids = lax.dynamic_index_in_dim(own_group, lat_pos, 1, keepdims=False)

    def own(band):
        return lax.dynamic_index_in_dim(
            band.reshape(chunks, lat_count, 2, pair_count), lat_pos, 1, keepdims=False
        )

    column_ids = jnp.arange(pair_count, dtype=jnp.int32)
    parity_ids = jnp.arange(2, dtype=jnp.int32)
    degree_int = wave_ids[:, None, None] + 2 * column_ids[None, None, :] + parity_ids[None, :, None]
    inside_mask = degree_int < lat_rows
    inside = inside_mask.astype(f32)
    degree = degree_int.astype(f32)
    degree_ratio = degree * (degree + 1.0) / (lat_rows * (lat_rows - 1.0))
    damping = 1.0 / (1.0 + damping_rate * degree_ratio * degree_ratio)
    not_first = (column_ids > 0).astype(f32)
    not_last = (column_ids < pair_count - 1).astype(f32)
    sub_band = own(lower_diag) * inside * not_first
    super_band = own(upper_diag) * inside * not_last
    center = jnp.where(inside_mask, own(main_diag), 1.0)
    bands = jnp.stack([sub_band, center, super_band, inside, damping], axis=2)
    factors, links = make_factors(bands.reshape(2 * chunks, 5, BLOCKS, steps))
    factors = factors.reshape(chunks, 2, 6, BLOCKS, steps)
    links = links.reshape(chunks, 2, 6, BLOCKS, 128)

    def swap_lat(values):
        return lax.all_to_all(values, "lat", split_axis=0, concat_axis=0, tiled=True)

    def gather_waves(values):
        return lax.all_gather(values, "wave", axis=0)

    def from_waves(values):
        return [values] + [
            lax.ppermute(values, "wave", [(w, (w + k) % wave_count) for w in range(wave_count)])
            for k in range(1, wave_count)
        ]

    def wave_rows(arrived, j):
        arrived = arrived.reshape(2, pair_count, row_width + pair_count)
        return wave_step(arrived, factors[j], links[j], row_width).reshape(lat_count, row_count, row_width)

    first_out = outgoing(fourier_rows, legendre, lat_count, 0)
    rows_later, table_later, first_out = lax.optimization_barrier((fourier_rows, legendre, first_out))
    ready = wave_rows(swap_lat(first_out), 0)
    pieces = cut_pairs(row_count)
    gathered, rest = [], None
    for j in range(1, chunks):
        out, ready = lax.optimization_barrier((outgoing(rows_later, table_later, lat_count, j), ready))
        gathered.append(gather_waves(ready))
        home = wave_rows(swap_lat(out), j)
        ready, *rest = pair_rows(swap_lat(home), pieces if j == chunks - 1 else [row_count // 2])
    first_rows, ready = lax.optimization_barrier((gathered[0], ready))
    last = gather_waves(ready)
    first_rows = swap_lat(first_rows.swapaxes(0, 1)).reshape(lat_count * wave_count, row_count, row_width)
    whole = pair_rows(first_rows, [row_count // 2]) + gathered[1:]

    lon_dev = NLON // wave_count
    lon_ids = wave_pos * lon_dev + jnp.arange(lon_dev, dtype=jnp.int32)
    blocks = [slot_ids[:, 0].T.reshape(-1)]
    blocks += [slot_ids[w, j] for j in range(1, chunks) for w in range(wave_count)]
    trig = zonal_matrix(blocks, lon_ids)
    if not rest:
        return synthesize(trig, whole, [last], 0, pieces, None)
    sources = (wave_pos - jnp.arange(wave_count)) % wave_count
    seen_ids = slot_ids[sources, chunks - 1]
    rest_trig = zonal_matrix(blocks[:-wave_count] + [seen_ids[k] for k in range(wave_count)], lon_ids)
    rest, last, trig, rest_trig, *whole = lax.optimization_barrier((rest[0], last, trig, rest_trig, *whole))
    rest = from_waves(rest)
    grid = synthesize(trig, whole, [last], 0, pieces, None)
    return synthesize(rest_trig, whole, rest, pieces[0], pieces, grid)


def solution(mesh):
    placed = (
        P("wave", "lat", None),
        P("wave", "lat", None),
        P(),
        P("wave", None),
        P("wave", None),
        P("wave", None),
    )
    return jax.shard_map(
        on_device, mesh=mesh, in_specs=placed, out_specs=P("wave", "lat"), check_vma=False
    )
```

```python
import functools
import math

import jax
import jax.numpy as jnp
from jax import lax
from jax.experimental import pallas as pl
from jax.experimental.pallas import tpu as pltpu
from jax.sharding import PartitionSpec as P

NLON = 3200
LEV = 64
damping_rate = 4.0
BLOCKS = 8
VMEM_LIMIT = 56 * 2**20
f32 = jnp.float32
bf16 = jnp.bfloat16


def zonal_matrix(blocks, lon_ids):
    wave_ids = jnp.concatenate([jnp.concatenate([ids, ids]) for ids in blocks])
    is_sine = jnp.concatenate([jnp.arange(2 * ids.size) >= ids.size for ids in blocks])
    phase_index = lon_ids[:, None] * wave_ids[None, :] % NLON
    phase_angle = phase_index.astype(f32) * (2.0 * math.pi / NLON)
    return jnp.where(is_sine[None, :], -jnp.sin(phase_angle), jnp.cos(phase_angle)).astype(bf16)


def factor_kernel(bands_ref, factors_ref, links_ref):
    systems, _, _, steps = bands_ref.shape
    sub, center, sup, inside, damping = (bands_ref[:, n] for n in range(5))
    lanes = lax.broadcasted_iota(jnp.int32, (systems, BLOCKS, steps), 2)

    def column(values, i):
        return values[:, :, i : i + 1]

    def place(values, i, new):
        return jnp.where(lanes == i, new, values)

    zero = jnp.zeros((systems, BLOCKS, steps), f32)
    inv, scaled_sub, scaled_sup, left, right = zero, zero, zero, zero, zero
    for i in range(steps):
        pivot = column(center, i)
        if i:
            pivot = pivot - column(sub, i) * sup_part
        inv_part = 1.0 / pivot
        sub_part = column(sub, i) * inv_part
        sup_part = column(sup, i) * inv_part
        left_part = -sub_part * left_part if i else sub_part
        inv = place(inv, i, inv_part)
        scaled_sub = place(scaled_sub, i, sub_part)
        scaled_sup = place(scaled_sup, i, sup_part)
        left = place(left, i, left_part)
    solved_left = zero
    for i in reversed(range(steps)):
        if i == steps - 1:
            right_part = column(scaled_sup, i)
            left_part = column(left, i)
        else:
            right_part = -column(scaled_sup, i) * right_part
            left_part = column(left, i) - column(scaled_sup, i) * left_part
        right = place(right, i, right_part)
        solved_left = place(solved_left, i, left_part)
    for n, values in enumerate((inv * inside, scaled_sub, scaled_sup, right, solved_left, damping * inside)):
        factors_ref[:, n] = values
    right_first, right_last = column(right, 0), column(right, steps - 1)
    left_first, left_last = column(solved_left, 0), column(solved_left, steps - 1)
    beta = jnp.zeros((systems, 1, 1), f32)
    width = links_ref.shape[-1]
    for b in range(BLOCKS):
        row = slice(b, b + 1)
        scale = 1.0 / (1.0 - left_first[:, row] * beta)
        step = right_first[:, row] * scale
        across = left_last[:, row] * beta
        beta = right_last[:, row] + across * step
        for n, value in enumerate((scale, left_first[:, row] * scale, step, left_last[:, row], across, beta)):
            links_ref[:, n, b : b + 1, :] = jnp.broadcast_to(value, (systems, 1, width))


def outgoing_kernel(first, rows_hbm, table_hbm, out_hbm, table, joined, rows_sems, table_sems, out_sems):
    slots, _, width = joined.shape[0], joined.shape[1], rows_hbm.shape[2]
    copies = []
    for s in range(slots):
        copies.append(pltpu.make_async_copy(table_hbm.at[first + s], table.at[s], table_sems.at[s]))
        copies.append(
            pltpu.make_async_copy(rows_hbm.at[first + s], joined.at[s, :, pl.ds(0, width)], rows_sems.at[s])
        )
    for copy in copies:
        copy.start()
    sends = []
    for s in range(slots):
        copies[2 * s].wait()
        joined[s, :, width:] = table[s].astype(bf16)
        copies[2 * s + 1].wait()
        sends.append(pltpu.make_async_copy(joined.at[s], out_hbm.at[s], out_sems.at[s]))
        sends[s].start()
    for send in sends:
        send.wait()


def wave_kernel(arrived_ref, factors_ref, links_ref, home_ref, spec, part):
    _, pair_count, width = home_ref.shape
    steps = pair_count // BLOCKS
    tiles = width // 128
    north = arrived_ref[0, :, :width].astype(f32)
    south = arrived_ref[1, :, :width].astype(f32)
    for p in range(2):
        folded = (north + south if p == 0 else north - south).astype(bf16)
        spectral = jnp.dot(arrived_ref[p, :, width:], folded, preferred_element_type=f32)
        for t in range(tiles):
            spec[p, t] = spectral[:, 128 * t : 128 * t + 128]

    def spec_rows(p, i):
        return jnp.concatenate([spec[p, t, pl.ds(i, BLOCKS, stride=steps), :] for t in range(tiles)], axis=1)

    def factor(p, n, i):
        return factors_ref[p, n, :, i : i + 1]

    running = [None, None]
    for i in range(steps):
        for p in range(2):
            value = spec_rows(p, i) * factor(p, 0, i)
            if i:
                value = value - factor(p, 1, i) * running[p]
            part[p, i] = value
            running[p] = value
    last = list(running)
    for i in reversed(range(steps - 1)):
        for p in range(2):
            value = part[p, i] - factor(p, 2, i) * running[p]
            part[p, i] = value
            running[p] = value
    first = running
    after, before = [], []
    for p in range(2):
        def link(n, b):
            return jnp.concatenate([links_ref[p, n, b : b + 1, :]] * tiles, axis=1)

        alpha = jnp.zeros((1, width), f32)
        heads, tails = [], []
        for b in range(BLOCKS):
            row = slice(b, b + 1)
            head = first[p][row] * link(0, b) - link(1, b) * alpha
            alpha = last[p][row] - link(3, b) * alpha + link(4, b) * head
            heads.append(head)
            tails.append(alpha)
        ahead = jnp.zeros((1, width), f32)
        next_heads, prev_tails = [None] * BLOCKS, [jnp.zeros((1, width), f32)] * BLOCKS
        for b in reversed(range(BLOCKS)):
            next_heads[b] = ahead
            if b + 1 < BLOCKS:
                prev_tails[b + 1] = tails[b] - link(5, b) * ahead
            ahead = heads[b] - link(2, b) * ahead
        after.append(jnp.concatenate(next_heads, axis=0))
        before.append(jnp.concatenate(prev_tails, axis=0))
    half = lax.broadcasted_iota(jnp.int32, (BLOCKS, width), 1) % (width // 2)
    untouched = half < LEV
    for i in range(steps):
        for p in range(2):
            solved = part[p, i] - factor(p, 3, i) * after[p] - factor(p, 4, i) * before[p]
            damped = jnp.where(untouched, spec_rows(p, i), solved) * factor(p, 5, i)
            for t in range(tiles):
                spec[p, t, pl.ds(i, BLOCKS, stride=steps), :] = damped[:, 128 * t : 128 * t + 128]
    parts = []
    for p in range(2):
        damped = jnp.concatenate([spec[p, t].astype(bf16) for t in range(tiles)], axis=1)
        parts.append(
            lax.dot_general(
                arrived_ref[p, :, width:], damped, (((0,), (0,)), ((), ())), preferred_element_type=f32
            )
        )
    home_ref[0] = (parts[0] + parts[1]).astype(bf16)
    home_ref[1] = (parts[0] - parts[1]).astype(bf16)


def pair_kernel(rows_ref, *pairs_refs):
    slots, groups, rows, width = rows_ref.shape
    order = slots * rows
    out_row = lax.broadcasted_iota(jnp.int32, (order, order), 0)
    in_row = lax.broadcasted_iota(jnp.int32, (order, order), 1)
    odd, rest = out_row // (order // 2), out_row % (order // 2)
    source = (rest % slots) * rows + 2 * (rest // slots) + odd
    shuffle = (in_row == source).astype(bf16)
    first_half = lax.broadcasted_iota(jnp.int32, (order // 2, width), 1) < width // 2

    def swap(values):
        return jnp.concatenate([values[:, width // 2 :], values[:, : width // 2]], axis=1)

    places = [ref.at[n] for ref in pairs_refs for n in range(ref.shape[0])]
    for g in range(groups):
        block = rows_ref[:, g].astype(f32).reshape(order, width).astype(bf16)
        moved = jnp.dot(shuffle, block, preferred_element_type=f32)
        even_rows, odd_rows = moved[: order // 2], moved[order // 2 :]
        real = jnp.where(first_half, even_rows, swap(odd_rows)).reshape(rows // 2, slots, width)
        imag = jnp.where(first_half, swap(even_rows), odd_rows).reshape(rows // 2, slots, width)
        both = jnp.concatenate([real, imag], axis=1).astype(bf16)
        for n in range(rows // 2):
            places[g * (rows // 2) + n][...] = both[n]


def zonal_kernel(tile, trig_ref, *refs):
    *operands, grid_ref = refs
    pairs, width = operands[0].shape[-3], operands[0].shape[-1]
    lons = trig_ref.shape[0]

    def coefficients(r):
        found = []
        for ref in operands:
            found += [ref[r]] if ref.ndim == 3 else [ref[z, r] for z in range(ref.shape[0])]
        return jnp.concatenate(found, axis=0)

    for r in range(0, pairs, 2):
        rhs = jnp.concatenate([coefficients(r), coefficients(r + 1)], axis=1)
        for column in range(0, 2 * width, 256):
            for lon in range(0, lons, tile):
                sums = jnp.dot(
                    trig_ref[lon : lon + tile], rhs[:, column : column + 256], preferred_element_type=f32
                )
                grid_ref[lon : lon + tile, r * width + column : r * width + column + 256] = sums.astype(bf16)


def zonal_tail_kernel(tile, trig_ref, *refs):
    zonal_kernel(tile, trig_ref, *refs[:-2], refs[-1])


def params():
    return pltpu.CompilerParams(vmem_limit_bytes=VMEM_LIMIT)


def whole_vmem(count):
    return [pl.BlockSpec(memory_space=pltpu.VMEM)] * count


def make_factors(bands):
    systems, _, _, steps = bands.shape
    return pl.pallas_call(
        factor_kernel,
        out_shape=(
            jax.ShapeDtypeStruct((systems, 6, BLOCKS, steps), f32),
            jax.ShapeDtypeStruct((systems, 6, BLOCKS, 128), f32),
        ),
        in_specs=whole_vmem(1),
        out_specs=tuple(whole_vmem(2)),
        compiler_params=params(),
        cost_estimate=pl.CostEstimate(flops=2_000_000_000, bytes_accessed=2_000_000, transcendentals=0),
        name="factor",
    )(bands)


def outgoing(fourier_rows, legendre, slots, j):
    _, rows, width = fourier_rows.shape
    pair_count = legendre.shape[2]

    anywhere = pl.BlockSpec(memory_space=pl.ANY)
    return pl.pallas_call(
        functools.partial(outgoing_kernel, j * slots),
        out_shape=jax.ShapeDtypeStruct((slots, rows, width + pair_count), bf16),
        in_specs=[anywhere, anywhere],
        out_specs=anywhere,
        scratch_shapes=[
            pltpu.VMEM((slots, rows, pair_count), f32),
            pltpu.VMEM((slots, rows, width + pair_count), bf16),
            pltpu.SemaphoreType.DMA((slots,)),
            pltpu.SemaphoreType.DMA((slots,)),
            pltpu.SemaphoreType.DMA((slots,)),
        ],
        compiler_params=params(),
        cost_estimate=pl.CostEstimate(
            flops=0, bytes_accessed=slots * rows * (4 * width + 6 * pair_count), transcendentals=0
        ),
        name="outgoing",
    )(fourier_rows, legendre)


def wave_step(arrived, factors, links, width):
    _, pair_count, _ = arrived.shape
    return pl.pallas_call(
        wave_kernel,
        out_shape=jax.ShapeDtypeStruct((2, pair_count, width), bf16),
        in_specs=whole_vmem(3),
        out_specs=whole_vmem(1)[0],
        scratch_shapes=[
            pltpu.VMEM((2, width // 128, pair_count, 128), f32),
            pltpu.VMEM((2, pair_count // BLOCKS, BLOCKS, width), f32),
        ],
        compiler_params=params(),
        cost_estimate=pl.CostEstimate(flops=8_000_000_000, bytes_accessed=6_000_000, transcendentals=0),
        name="wave",
    )(arrived, factors, links)


def cut_pairs(count):
    pairs = count // 2
    return [pairs * 4 // 5, pairs // 5] if pairs % 10 == 0 and count % 8 == 0 else [pairs]


def pair_rows(rows, pieces):
    slots, count, width = rows.shape
    if count % 8 or slots % 8:
        split = rows.reshape(slots, count // 2, 2, 2, width // 2)
        joined = split.transpose(1, 3, 0, 2, 4).reshape(count // 2, 2 * slots, width)
        return [joined[sum(pieces[:n]) : sum(pieces[: n + 1])] for n in range(len(pieces))]
    pairs = pl.pallas_call(
        pair_kernel,
        out_shape=[jax.ShapeDtypeStruct((piece, 2 * slots, width), bf16) for piece in pieces],
        in_specs=whole_vmem(1),
        out_specs=whole_vmem(len(pieces)),
        compiler_params=params(),
        cost_estimate=pl.CostEstimate(flops=2_000_000_000, bytes_accessed=2_400_000, transcendentals=0),
        name="pair",
    )(rows.reshape(slots, count // 8, 8, width))
    return list(pairs)


def synthesize(trig, whole, extra, first, pieces, grid):
    lons, depth = trig.shape
    piece, pairs = extra[0].shape[-3], sum(pieces)
    width = extra[0].shape[-1]
    step = next(n for n in (10, 8, 6, 4, 2) if piece % n == 0 and first % n == 0)
    ahead = first // step

    def spec(array, shift):
        lead = array.shape[:-3]
        block = lead + (step,) + array.shape[-2:]
        return pl.BlockSpec(block, lambda i: (0,) * len(lead) + (shift + i, 0, 0))

    operands = [trig, *whole, *extra]
    in_specs = [pl.BlockSpec((lons, depth), lambda i: (0, 0))]
    in_specs += [spec(array, ahead) for array in whole] + [spec(array, 0) for array in extra]
    if grid is not None:
        operands.append(grid)
        in_specs.append(pl.BlockSpec(memory_space=pl.ANY))
    return pl.pallas_call(
        functools.partial(zonal_kernel, lons) if grid is None else functools.partial(zonal_tail_kernel, lons if lons % 80 else lons // 5),
        out_shape=jax.ShapeDtypeStruct((lons, pairs * width), bf16),
        grid=(piece // step,),
        in_specs=in_specs,
        out_specs=pl.BlockSpec((lons, step * width), lambda i: (0, ahead + i)),
        input_output_aliases={} if grid is None else {len(operands) - 1: 0},
        compiler_params=params(),
        cost_estimate=pl.CostEstimate(
            flops=4 * lons * depth * piece * width, bytes_accessed=2 * lons * piece * width, transcendentals=0
        ),
        name="zonal",
    )(*operands)


def on_device(fourier_rows, legendre, wavenumber, lower_diag, main_diag, upper_diag):
    lat_count = lax.axis_size("lat")
    wave_count = lax.axis_size("wave")
    lat_pos = lax.axis_index("lat")
    wave_pos = lax.axis_index("wave")
    group_slots, row_count, row_width = fourier_rows.shape
    pair_count = legendre.shape[2]
    lat_rows = 2 * pair_count
    chunks = group_slots // lat_count
    steps = pair_count // BLOCKS

    slot_ids = wavenumber.reshape(wave_count, chunks, lat_count)
    own_group = lax.dynamic_index_in_dim(slot_ids, wave_pos, 0, keepdims=False)
    wave_ids = lax.dynamic_index_in_dim(own_group, lat_pos, 1, keepdims=False)

    def own(band):
        return lax.dynamic_index_in_dim(
            band.reshape(chunks, lat_count, 2, pair_count), lat_pos, 1, keepdims=False
        )

    column_ids = jnp.arange(pair_count, dtype=jnp.int32)
    parity_ids = jnp.arange(2, dtype=jnp.int32)
    degree_int = wave_ids[:, None, None] + 2 * column_ids[None, None, :] + parity_ids[None, :, None]
    inside_mask = degree_int < lat_rows
    inside = inside_mask.astype(f32)
    degree = degree_int.astype(f32)
    degree_ratio = degree * (degree + 1.0) / (lat_rows * (lat_rows - 1.0))
    damping = 1.0 / (1.0 + damping_rate * degree_ratio * degree_ratio)
    not_first = (column_ids > 0).astype(f32)
    not_last = (column_ids < pair_count - 1).astype(f32)
    sub_band = own(lower_diag) * inside * not_first
    super_band = own(upper_diag) * inside * not_last
    center = jnp.where(inside_mask, own(main_diag), 1.0)
    bands = jnp.stack([sub_band, center, super_band, inside, damping], axis=2)
    factors, links = make_factors(bands.reshape(2 * chunks, 5, BLOCKS, steps))
    factors = factors.reshape(chunks, 2, 6, BLOCKS, steps)
    links = links.reshape(chunks, 2, 6, BLOCKS, 128)

    def swap_lat(values):
        return lax.all_to_all(values, "lat", split_axis=0, concat_axis=0, tiled=True)

    def gather_waves(values):
        return lax.all_gather(values, "wave", axis=0)

    def from_waves(values):
        return [values] + [
            lax.ppermute(values, "wave", [(w, (w + k) % wave_count) for w in range(wave_count)])
            for k in range(1, wave_count)
        ]

    def wave_rows(arrived, j):
        arrived = arrived.reshape(2, pair_count, row_width + pair_count)
        return wave_step(arrived, factors[j], links[j], row_width).reshape(lat_count, row_count, row_width)

    first_out = outgoing(fourier_rows, legendre, lat_count, 0)
    rows_later, table_later, first_out = lax.optimization_barrier((fourier_rows, legendre, first_out))
    ready = wave_rows(swap_lat(first_out), 0)
    pieces = cut_pairs(row_count)
    gathered, rest = [], None
    for j in range(1, chunks):
        out, ready = lax.optimization_barrier((outgoing(rows_later, table_later, lat_count, j), ready))
        gathered.append(gather_waves(ready))
        home = wave_rows(swap_lat(out), j)
        ready, *rest = pair_rows(swap_lat(home), pieces if j == chunks - 1 else [row_count // 2])
    first_rows, ready = lax.optimization_barrier((gathered[0], ready))
    last = gather_waves(ready)
    first_rows = swap_lat(first_rows.swapaxes(0, 1)).reshape(lat_count * wave_count, row_count, row_width)
    whole = pair_rows(first_rows, [row_count // 2]) + gathered[1:]

    lon_dev = NLON // wave_count
    lon_ids = wave_pos * lon_dev + jnp.arange(lon_dev, dtype=jnp.int32)
    blocks = [slot_ids[:, 0].T.reshape(-1)]
    blocks += [slot_ids[w, j] for j in range(1, chunks) for w in range(wave_count)]
    trig = zonal_matrix(blocks, lon_ids)
    if not rest:
        return synthesize(trig, whole, [last], 0, pieces, None)
    sources = (wave_pos - jnp.arange(wave_count)) % wave_count
    seen_ids = slot_ids[sources, chunks - 1]
    rest_trig = zonal_matrix(blocks[:-wave_count] + [seen_ids[k] for k in range(wave_count)], lon_ids)
    rest, last, trig, rest_trig, *whole = lax.optimization_barrier((rest[0], last, trig, rest_trig, *whole))
    rest = from_waves(rest)
    grid = synthesize(trig, whole, [last], 0, pieces, None)
    return synthesize(rest_trig, whole, rest, pieces[0], pieces, grid)


def solution(mesh):
    placed = (
        P("wave", "lat", None),
        P("wave", "lat", None),
        P(),
        P("wave", None),
        P("wave", None),
        P("wave", None),
    )
    return jax.shard_map(
        on_device, mesh=mesh, in_specs=placed, out_specs=P("wave", "lat"), check_vma=False
    )
```

```python
import functools
import math

import jax
import jax.numpy as jnp
from jax import lax
from jax.experimental import pallas as pl
from jax.experimental.pallas import tpu as pltpu
from jax.sharding import PartitionSpec as P

NLON = 3200
LEV = 64
damping_rate = 4.0
BLOCKS = 8
VMEM_LIMIT = 56 * 2**20
f32 = jnp.float32
bf16 = jnp.bfloat16


def zonal_matrix(blocks, lon_ids):
    wave_ids = jnp.concatenate([jnp.concatenate([ids, ids]) for ids in blocks])
    is_sine = jnp.concatenate([jnp.arange(2 * ids.size) >= ids.size for ids in blocks])
    phase_index = lon_ids[:, None] * wave_ids[None, :] % NLON
    phase_angle = phase_index.astype(f32) * (2.0 * math.pi / NLON)
    return jnp.where(is_sine[None, :], -jnp.sin(phase_angle), jnp.cos(phase_angle)).astype(bf16)


def factor_kernel(bands_ref, factors_ref, links_ref):
    systems, _, _, steps = bands_ref.shape
    sub, center, sup, inside, damping = (bands_ref[:, n] for n in range(5))
    lanes = lax.broadcasted_iota(jnp.int32, (systems, BLOCKS, steps), 2)

    def column(values, i):
        return values[:, :, i : i + 1]

    def place(values, i, new):
        return jnp.where(lanes == i, new, values)

    zero = jnp.zeros((systems, BLOCKS, steps), f32)
    inv, scaled_sub, scaled_sup, left, right = zero, zero, zero, zero, zero
    for i in range(steps):
        pivot = column(center, i)
        if i:
            pivot = pivot - column(sub, i) * sup_part
        inv_part = 1.0 / pivot
        sub_part = column(sub, i) * inv_part
        sup_part = column(sup, i) * inv_part
        left_part = -sub_part * left_part if i else sub_part
        inv = place(inv, i, inv_part)
        scaled_sub = place(scaled_sub, i, sub_part)
        scaled_sup = place(scaled_sup, i, sup_part)
        left = place(left, i, left_part)
    solved_left = zero
    for i in reversed(range(steps)):
        if i == steps - 1:
            right_part = column(scaled_sup, i)
            left_part = column(left, i)
        else:
            right_part = -column(scaled_sup, i) * right_part
            left_part = column(left, i) - column(scaled_sup, i) * left_part
        right = place(right, i, right_part)
        solved_left = place(solved_left, i, left_part)
    for n, values in enumerate((inv * inside, scaled_sub, scaled_sup, right, solved_left, damping * inside)):
        factors_ref[:, n] = values
    right_first, right_last = column(right, 0), column(right, steps - 1)
    left_first, left_last = column(solved_left, 0), column(solved_left, steps - 1)
    beta = jnp.zeros((systems, 1, 1), f32)
    width = links_ref.shape[-1]
    for b in range(BLOCKS):
        row = slice(b, b + 1)
        scale = 1.0 / (1.0 - left_first[:, row] * beta)
        step = right_first[:, row] * scale
        across = left_last[:, row] * beta
        beta = right_last[:, row] + across * step
        for n, value in enumerate((scale, left_first[:, row] * scale, step, left_last[:, row], across, beta)):
            links_ref[:, n, b : b + 1, :] = jnp.broadcast_to(value, (systems, 1, width))


def outgoing_kernel(first, rows_hbm, table_hbm, out_hbm, table, joined, rows_sems, table_sems, out_sems):
    slots, _, width = joined.shape[0], joined.shape[1], rows_hbm.shape[2]
    copies = []
    for s in range(slots):
        copies.append(pltpu.make_async_copy(table_hbm.at[first + s], table.at[s], table_sems.at[s]))
        copies.append(
            pltpu.make_async_copy(rows_hbm.at[first + s], joined.at[s, :, pl.ds(0, width)], rows_sems.at[s])
        )
    for copy in copies:
        copy.start()
    sends = []
    for s in range(slots):
        copies[2 * s].wait()
        joined[s, :, width:] = table[s].astype(bf16)
        copies[2 * s + 1].wait()
        sends.append(pltpu.make_async_copy(joined.at[s], out_hbm.at[s], out_sems.at[s]))
        sends[s].start()
    for send in sends:
        send.wait()


def wave_kernel(arrived_ref, factors_ref, links_ref, home_ref, spec, part):
    _, pair_count, width = home_ref.shape
    steps = pair_count // BLOCKS
    tiles = width // 128
    north = arrived_ref[0, :, :width].astype(f32)
    south = arrived_ref[1, :, :width].astype(f32)
    for p in range(2):
        folded = (north + south if p == 0 else north - south).astype(bf16)
        spectral = jnp.dot(arrived_ref[p, :, width:], folded, preferred_element_type=f32)
        for t in range(tiles):
            spec[p, t] = spectral[:, 128 * t : 128 * t + 128]

    def spec_rows(p, i):
        return jnp.concatenate([spec[p, t, pl.ds(i, BLOCKS, stride=steps), :] for t in range(tiles)], axis=1)

    def factor(p, n, i):
        return factors_ref[p, n, :, i : i + 1]

    running = [None, None]
    for i in range(steps):
        for p in range(2):
            value = spec_rows(p, i) * factor(p, 0, i)
            if i:
                value = value - factor(p, 1, i) * running[p]
            part[p, i] = value
            running[p] = value
    last = list(running)
    for i in reversed(range(steps - 1)):
        for p in range(2):
            value = part[p, i] - factor(p, 2, i) * running[p]
            part[p, i] = value
            running[p] = value
    first = running
    after, before = [], []
    for p in range(2):
        def link(n, b):
            return jnp.concatenate([links_ref[p, n, b : b + 1, :]] * tiles, axis=1)

        alpha = jnp.zeros((1, width), f32)
        heads, tails = [], []
        for b in range(BLOCKS):
            row = slice(b, b + 1)
            head = first[p][row] * link(0, b) - link(1, b) * alpha
            alpha = last[p][row] - link(3, b) * alpha + link(4, b) * head
            heads.append(head)
            tails.append(alpha)
        ahead = jnp.zeros((1, width), f32)
        next_heads, prev_tails = [None] * BLOCKS, [jnp.zeros((1, width), f32)] * BLOCKS
        for b in reversed(range(BLOCKS)):
            next_heads[b] = ahead
            if b + 1 < BLOCKS:
                prev_tails[b + 1] = tails[b] - link(5, b) * ahead
            ahead = heads[b] - link(2, b) * ahead
        after.append(jnp.concatenate(next_heads, axis=0))
        before.append(jnp.concatenate(prev_tails, axis=0))
    half = lax.broadcasted_iota(jnp.int32, (BLOCKS, width), 1) % (width // 2)
    untouched = half < LEV
    for i in range(steps):
        for p in range(2):
            solved = part[p, i] - factor(p, 3, i) * after[p] - factor(p, 4, i) * before[p]
            damped = jnp.where(untouched, spec_rows(p, i), solved) * factor(p, 5, i)
            for t in range(tiles):
                spec[p, t, pl.ds(i, BLOCKS, stride=steps), :] = damped[:, 128 * t : 128 * t + 128]
    parts = []
    for p in range(2):
        damped = jnp.concatenate([spec[p, t].astype(bf16) for t in range(tiles)], axis=1)
        parts.append(
            lax.dot_general(
                arrived_ref[p, :, width:], damped, (((0,), (0,)), ((), ())), preferred_element_type=f32
            )
        )
    home_ref[0] = (parts[0] + parts[1]).astype(bf16)
    home_ref[1] = (parts[0] - parts[1]).astype(bf16)


def pair_kernel(rows_ref, *pairs_refs):
    slots, groups, rows, width = rows_ref.shape
    order = slots * rows
    out_row = lax.broadcasted_iota(jnp.int32, (order, order), 0)
    in_row = lax.broadcasted_iota(jnp.int32, (order, order), 1)
    odd, rest = out_row // (order // 2), out_row % (order // 2)
    source = (rest % slots) * rows + 2 * (rest // slots) + odd
    shuffle = (in_row == source).astype(bf16)
    first_half = lax.broadcasted_iota(jnp.int32, (order // 2, width), 1) < width // 2

    def swap(values):
        return jnp.concatenate([values[:, width // 2 :], values[:, : width // 2]], axis=1)

    places = [ref.at[n] for ref in pairs_refs for n in range(ref.shape[0])]
    for g in range(groups):
        block = rows_ref[:, g].astype(f32).reshape(order, width).astype(bf16)
        moved = jnp.dot(shuffle, block, preferred_element_type=f32)
        even_rows, odd_rows = moved[: order // 2], moved[order // 2 :]
        real = jnp.where(first_half, even_rows, swap(odd_rows)).reshape(rows // 2, slots, width)
        imag = jnp.where(first_half, swap(even_rows), odd_rows).reshape(rows // 2, slots, width)
        both = jnp.concatenate([real, imag], axis=1).astype(bf16)
        for n in range(rows // 2):
            places[g * (rows // 2) + n][...] = both[n]


def zonal_kernel(tile, trig_ref, *refs):
    *operands, grid_ref = refs
    pairs, width = operands[0].shape[-3], operands[0].shape[-1]
    lons = trig_ref.shape[0]

    def coefficients(r):
        found = []
        for ref in operands:
            found += [ref[r]] if ref.ndim == 3 else [ref[z, r] for z in range(ref.shape[0])]
        return jnp.concatenate(found, axis=0)

    for r in range(0, pairs, 2):
        rhs = jnp.concatenate([coefficients(r), coefficients(r + 1)], axis=1)
        for column in range(0, 2 * width, 256):
            for lon in range(0, lons, tile):
                sums = jnp.dot(
                    trig_ref[lon : lon + tile], rhs[:, column : column + 256], preferred_element_type=f32
                )
                grid_ref[lon : lon + tile, r * width + column : r * width + column + 256] = sums.astype(bf16)


def zonal_tail_kernel(tile, trig_ref, *refs):
    zonal_kernel(tile, trig_ref, *refs[:-2], refs[-1])


def params(limit=VMEM_LIMIT):
    return pltpu.CompilerParams(vmem_limit_bytes=limit)


def whole_vmem(count):
    return [pl.BlockSpec(memory_space=pltpu.VMEM)] * count


def make_factors(bands):
    systems, _, _, steps = bands.shape
    return pl.pallas_call(
        factor_kernel,
        out_shape=(
            jax.ShapeDtypeStruct((systems, 6, BLOCKS, steps), f32),
            jax.ShapeDtypeStruct((systems, 6, BLOCKS, 128), f32),
        ),
        in_specs=whole_vmem(1),
        out_specs=tuple(whole_vmem(2)),
        compiler_params=params(),
        cost_estimate=pl.CostEstimate(flops=2_000_000_000, bytes_accessed=2_000_000, transcendentals=0),
        name="factor",
    )(bands)


def outgoing(fourier_rows, legendre, slots, j):
    _, rows, width = fourier_rows.shape
    pair_count = legendre.shape[2]

    anywhere = pl.BlockSpec(memory_space=pl.ANY)
    return pl.pallas_call(
        functools.partial(outgoing_kernel, j * slots),
        out_shape=jax.ShapeDtypeStruct((slots, rows, width + pair_count), bf16),
        in_specs=[anywhere, anywhere],
        out_specs=anywhere,
        scratch_shapes=[
            pltpu.VMEM((slots, rows, pair_count), f32),
            pltpu.VMEM((slots, rows, width + pair_count), bf16),
            pltpu.SemaphoreType.DMA((slots,)),
            pltpu.SemaphoreType.DMA((slots,)),
            pltpu.SemaphoreType.DMA((slots,)),
        ],
        compiler_params=params(),
        cost_estimate=pl.CostEstimate(
            flops=0, bytes_accessed=slots * rows * (4 * width + 6 * pair_count), transcendentals=0
        ),
        name="outgoing",
    )(fourier_rows, legendre)


def wave_step(arrived, factors, links, width):
    _, pair_count, _ = arrived.shape
    return pl.pallas_call(
        wave_kernel,
        out_shape=jax.ShapeDtypeStruct((2, pair_count, width), bf16),
        in_specs=whole_vmem(3),
        out_specs=whole_vmem(1)[0],
        scratch_shapes=[
            pltpu.VMEM((2, width // 128, pair_count, 128), f32),
            pltpu.VMEM((2, pair_count // BLOCKS, BLOCKS, width), f32),
        ],
        compiler_params=params(),
        cost_estimate=pl.CostEstimate(flops=8_000_000_000, bytes_accessed=6_000_000, transcendentals=0),
        name="wave",
    )(arrived, factors, links)


def cut_pairs(count):
    pairs = count // 2
    return [pairs * 4 // 5, pairs // 5] if pairs % 10 == 0 and count % 8 == 0 else [pairs]


def pair_rows(rows, pieces):
    slots, count, width = rows.shape
    if count % 8 or slots % 8:
        split = rows.reshape(slots, count // 2, 2, 2, width // 2)
        joined = split.transpose(1, 3, 0, 2, 4).reshape(count // 2, 2 * slots, width)
        return [joined[sum(pieces[:n]) : sum(pieces[: n + 1])] for n in range(len(pieces))]
    pairs = pl.pallas_call(
        pair_kernel,
        out_shape=[jax.ShapeDtypeStruct((piece, 2 * slots, width), bf16) for piece in pieces],
        in_specs=whole_vmem(1),
        out_specs=whole_vmem(len(pieces)),
        compiler_params=params(),
        cost_estimate=pl.CostEstimate(flops=2_000_000_000, bytes_accessed=2_400_000, transcendentals=0),
        name="pair",
    )(rows.reshape(slots, count // 8, 8, width))
    return list(pairs)


def stage_kernel(*refs):
    count = len(refs) // 2
    sems = refs[-1]
    copies = [pltpu.make_async_copy(refs[n], refs[count + n], sems.at[n]) for n in range(count)]
    for copy in copies:
        copy.start()
    for copy in copies:
        copy.wait()


def stage(arrays):
    return pl.pallas_call(
        stage_kernel,
        out_shape=[pltpu.VMEM(array.shape, array.dtype) for array in arrays],
        in_specs=[pl.BlockSpec(memory_space=pl.ANY)] * len(arrays),
        out_specs=whole_vmem(len(arrays)),
        scratch_shapes=[pltpu.SemaphoreType.DMA((len(arrays),))],
        compiler_params=params(4 * 2**20),
        cost_estimate=pl.CostEstimate(
            flops=0, bytes_accessed=sum(2 * array.size for array in arrays), transcendentals=0
        ),
        name="stage",
    )(*arrays)


def synthesize(trig, whole, extra, first, pieces, grid):
    lons, depth = trig.shape
    piece, pairs = extra[0].shape[-3], sum(pieces)
    width = extra[0].shape[-1]
    step = next(n for n in (10, 8, 6, 4, 2) if piece % n == 0 and first % n == 0)
    ahead = first // step

    def spec(array, shift):
        lead = array.shape[:-3]
        block = lead + (step,) + array.shape[-2:]
        return pl.BlockSpec(block, lambda i: (0,) * len(lead) + (shift + i, 0, 0))

    operands = [trig, *whole, *extra]
    in_specs = [pl.BlockSpec((lons, depth), lambda i: (0, 0))]
    in_specs += [spec(array, ahead) for array in whole] + [spec(array, 0) for array in extra]
    if grid is not None:
        operands.append(grid)
        in_specs.append(pl.BlockSpec(memory_space=pl.ANY))
    return pl.pallas_call(
        functools.partial(zonal_kernel, lons) if grid is None else functools.partial(zonal_tail_kernel, lons if lons % 80 else lons // 5),
        out_shape=jax.ShapeDtypeStruct((lons, pairs * width), bf16),
        grid=(piece // step,),
        in_specs=in_specs,
        out_specs=pl.BlockSpec((lons, step * width), lambda i: (0, ahead + i)),
        input_output_aliases={} if grid is None else {len(operands) - 1: 0},
        compiler_params=params(45 * 2**20),
        cost_estimate=pl.CostEstimate(
            flops=4 * lons * depth * piece * width, bytes_accessed=2 * lons * piece * width, transcendentals=0
        ),
        name="zonal",
    )(*operands)


def on_device(fourier_rows, legendre, wavenumber, lower_diag, main_diag, upper_diag):
    lat_count = lax.axis_size("lat")
    wave_count = lax.axis_size("wave")
    lat_pos = lax.axis_index("lat")
    wave_pos = lax.axis_index("wave")
    group_slots, row_count, row_width = fourier_rows.shape
    pair_count = legendre.shape[2]
    lat_rows = 2 * pair_count
    chunks = group_slots // lat_count
    steps = pair_count // BLOCKS

    slot_ids = wavenumber.reshape(wave_count, chunks, lat_count)
    own_group = lax.dynamic_index_in_dim(slot_ids, wave_pos, 0, keepdims=False)
    wave_ids = lax.dynamic_index_in_dim(own_group, lat_pos, 1, keepdims=False)

    def own(band):
        return lax.dynamic_index_in_dim(
            band.reshape(chunks, lat_count, 2, pair_count), lat_pos, 1, keepdims=False
        )

    column_ids = jnp.arange(pair_count, dtype=jnp.int32)
    parity_ids = jnp.arange(2, dtype=jnp.int32)
    degree_int = wave_ids[:, None, None] + 2 * column_ids[None, None, :] + parity_ids[None, :, None]
    inside_mask = degree_int < lat_rows
    inside = inside_mask.astype(f32)
    degree = degree_int.astype(f32)
    degree_ratio = degree * (degree + 1.0) / (lat_rows * (lat_rows - 1.0))
    damping = 1.0 / (1.0 + damping_rate * degree_ratio * degree_ratio)
    not_first = (column_ids > 0).astype(f32)
    not_last = (column_ids < pair_count - 1).astype(f32)
    sub_band = own(lower_diag) * inside * not_first
    super_band = own(upper_diag) * inside * not_last
    center = jnp.where(inside_mask, own(main_diag), 1.0)
    bands = jnp.stack([sub_band, center, super_band, inside, damping], axis=2)
    factors, links = make_factors(bands.reshape(2 * chunks, 5, BLOCKS, steps))
    factors = factors.reshape(chunks, 2, 6, BLOCKS, steps)
    links = links.reshape(chunks, 2, 6, BLOCKS, 128)

    def swap_lat(values):
        return lax.all_to_all(values, "lat", split_axis=0, concat_axis=0, tiled=True)

    def gather_waves(values):
        return lax.all_gather(values, "wave", axis=0)

    def from_waves(values):
        return [values] + [
            lax.ppermute(values, "wave", [(w, (w + k) % wave_count) for w in range(wave_count)])
            for k in range(1, wave_count)
        ]

    def wave_rows(arrived, j):
        arrived = arrived.reshape(2, pair_count, row_width + pair_count)
        return wave_step(arrived, factors[j], links[j], row_width).reshape(lat_count, row_count, row_width)

    first_out = outgoing(fourier_rows, legendre, lat_count, 0)
    rows_later, table_later, first_out = lax.optimization_barrier((fourier_rows, legendre, first_out))
    ready = wave_rows(swap_lat(first_out), 0)
    pieces = cut_pairs(row_count)
    gathered, rest = [], None
    for j in range(1, chunks):
        out, ready = lax.optimization_barrier((outgoing(rows_later, table_later, lat_count, j), ready))
        gathered.append(gather_waves(ready))
        home = wave_rows(swap_lat(out), j)
        ready, *rest = pair_rows(swap_lat(home), pieces if j == chunks - 1 else [row_count // 2])
    first_rows, ready = lax.optimization_barrier((gathered[0], ready))
    last = gather_waves(ready)
    first_rows = swap_lat(first_rows.swapaxes(0, 1)).reshape(lat_count * wave_count, row_count, row_width)
    whole = pair_rows(first_rows, [row_count // 2]) + gathered[1:]

    lon_dev = NLON // wave_count
    lon_ids = wave_pos * lon_dev + jnp.arange(lon_dev, dtype=jnp.int32)
    blocks = [slot_ids[:, 0].T.reshape(-1)]
    blocks += [slot_ids[w, j] for j in range(1, chunks) for w in range(wave_count)]
    trig = zonal_matrix(blocks, lon_ids)
    if not rest:
        return synthesize(trig, whole, [last], 0, pieces, None)
    sources = (wave_pos - jnp.arange(wave_count)) % wave_count
    seen_ids = slot_ids[sources, chunks - 1]
    rest_trig = zonal_matrix(blocks[:-wave_count] + [seen_ids[k] for k in range(wave_count)], lon_ids)
    rest, last = lax.optimization_barrier((rest[0], last))
    whole = stage(whole)
    rest = from_waves(rest)
    grid = synthesize(trig, whole, [last], 0, pieces, None)
    return synthesize(rest_trig, whole, rest, pieces[0], pieces, grid)


def solution(mesh):
    placed = (
        P("wave", "lat", None),
        P("wave", "lat", None),
        P(),
        P("wave", None),
        P("wave", None),
        P("wave", None),
    )
    return jax.shard_map(
        on_device, mesh=mesh, in_specs=placed, out_specs=P("wave", "lat"), check_vma=False
    )
```

```python
import functools
import math

import jax
import jax.numpy as jnp
from jax import lax
from jax.experimental import pallas as pl
from jax.experimental.pallas import tpu as pltpu
from jax.sharding import PartitionSpec as P

NLON = 3200
LEV = 64
damping_rate = 4.0
BLOCKS = 8
VMEM_LIMIT = 56 * 2**20
f32 = jnp.float32
bf16 = jnp.bfloat16


def zonal_matrix(blocks, lon_ids):
    wave_ids = jnp.concatenate([jnp.concatenate([ids, ids]) for ids in blocks])
    is_sine = jnp.concatenate([jnp.arange(2 * ids.size) >= ids.size for ids in blocks])
    phase_index = lon_ids[:, None] * wave_ids[None, :] % NLON
    phase_angle = phase_index.astype(f32) * (2.0 * math.pi / NLON)
    return jnp.where(is_sine[None, :], -jnp.sin(phase_angle), jnp.cos(phase_angle)).astype(bf16)


def factor_kernel(bands_ref, factors_ref, links_ref):
    systems, _, _, steps = bands_ref.shape
    sub, center, sup, inside, damping = (bands_ref[:, n] for n in range(5))
    lanes = lax.broadcasted_iota(jnp.int32, (systems, BLOCKS, steps), 2)

    def column(values, i):
        return values[:, :, i : i + 1]

    def place(values, i, new):
        return jnp.where(lanes == i, new, values)

    zero = jnp.zeros((systems, BLOCKS, steps), f32)
    inv, scaled_sub, scaled_sup, left, right = zero, zero, zero, zero, zero
    for i in range(steps):
        pivot = column(center, i)
        if i:
            pivot = pivot - column(sub, i) * sup_part
        inv_part = 1.0 / pivot
        sub_part = column(sub, i) * inv_part
        sup_part = column(sup, i) * inv_part
        left_part = -sub_part * left_part if i else sub_part
        inv = place(inv, i, inv_part)
        scaled_sub = place(scaled_sub, i, sub_part)
        scaled_sup = place(scaled_sup, i, sup_part)
        left = place(left, i, left_part)
    solved_left = zero
    for i in reversed(range(steps)):
        if i == steps - 1:
            right_part = column(scaled_sup, i)
            left_part = column(left, i)
        else:
            right_part = -column(scaled_sup, i) * right_part
            left_part = column(left, i) - column(scaled_sup, i) * left_part
        right = place(right, i, right_part)
        solved_left = place(solved_left, i, left_part)
    for n, values in enumerate((inv * inside, scaled_sub, scaled_sup, right, solved_left, damping * inside)):
        factors_ref[:, n] = values
    right_first, right_last = column(right, 0), column(right, steps - 1)
    left_first, left_last = column(solved_left, 0), column(solved_left, steps - 1)
    beta = jnp.zeros((systems, 1, 1), f32)
    width = links_ref.shape[-1]
    for b in range(BLOCKS):
        row = slice(b, b + 1)
        scale = 1.0 / (1.0 - left_first[:, row] * beta)
        step = right_first[:, row] * scale
        across = left_last[:, row] * beta
        beta = right_last[:, row] + across * step
        for n, value in enumerate((scale, left_first[:, row] * scale, step, left_last[:, row], across, beta)):
            links_ref[:, n, b : b + 1, :] = jnp.broadcast_to(value, (systems, 1, width))


def outgoing_kernel(first, rows_hbm, table_hbm, out_hbm, table, joined, rows_sems, table_sems, out_sems):
    slots, _, width = joined.shape[0], joined.shape[1], rows_hbm.shape[2]
    copies = []
    for s in range(slots):
        copies.append(pltpu.make_async_copy(table_hbm.at[first + s], table.at[s], table_sems.at[s]))
        copies.append(
            pltpu.make_async_copy(rows_hbm.at[first + s], joined.at[s, :, pl.ds(0, width)], rows_sems.at[s])
        )
    for copy in copies:
        copy.start()
    sends = []
    for s in range(slots):
        copies[2 * s].wait()
        joined[s, :, width:] = table[s].astype(bf16)
        copies[2 * s + 1].wait()
        sends.append(pltpu.make_async_copy(joined.at[s], out_hbm.at[s], out_sems.at[s]))
        sends[s].start()
    for send in sends:
        send.wait()


def wave_kernel(arrived_ref, factors_ref, links_ref, home_ref, spec, part):
    _, pair_count, width = home_ref.shape
    steps = pair_count // BLOCKS
    tiles = width // 128
    north = arrived_ref[0, :, :width].astype(f32)
    south = arrived_ref[1, :, :width].astype(f32)
    for p in range(2):
        folded = (north + south if p == 0 else north - south).astype(bf16)
        spectral = jnp.dot(arrived_ref[p, :, width:], folded, preferred_element_type=f32)
        for t in range(tiles):
            spec[p, t] = spectral[:, 128 * t : 128 * t + 128]

    def spec_rows(p, i):
        return jnp.concatenate([spec[p, t, pl.ds(i, BLOCKS, stride=steps), :] for t in range(tiles)], axis=1)

    def factor(p, n, i):
        return factors_ref[p, n, :, i : i + 1]

    running = [None, None]
    for i in range(steps):
        for p in range(2):
            value = spec_rows(p, i) * factor(p, 0, i)
            if i:
                value = value - factor(p, 1, i) * running[p]
            part[p, i] = value
            running[p] = value
    last = list(running)
    for i in reversed(range(steps - 1)):
        for p in range(2):
            value = part[p, i] - factor(p, 2, i) * running[p]
            part[p, i] = value
            running[p] = value
    first = running
    after, before = [], []
    for p in range(2):
        def link(n, b):
            return jnp.concatenate([links_ref[p, n, b : b + 1, :]] * tiles, axis=1)

        alpha = jnp.zeros((1, width), f32)
        heads, tails = [], []
        for b in range(BLOCKS):
            row = slice(b, b + 1)
            head = first[p][row] * link(0, b) - link(1, b) * alpha
            alpha = last[p][row] - link(3, b) * alpha + link(4, b) * head
            heads.append(head)
            tails.append(alpha)
        ahead = jnp.zeros((1, width), f32)
        next_heads, prev_tails = [None] * BLOCKS, [jnp.zeros((1, width), f32)] * BLOCKS
        for b in reversed(range(BLOCKS)):
            next_heads[b] = ahead
            if b + 1 < BLOCKS:
                prev_tails[b + 1] = tails[b] - link(5, b) * ahead
            ahead = heads[b] - link(2, b) * ahead
        after.append(jnp.concatenate(next_heads, axis=0))
        before.append(jnp.concatenate(prev_tails, axis=0))
    half = lax.broadcasted_iota(jnp.int32, (BLOCKS, width), 1) % (width // 2)
    untouched = half < LEV
    for i in range(steps):
        for p in range(2):
            solved = part[p, i] - factor(p, 3, i) * after[p] - factor(p, 4, i) * before[p]
            damped = jnp.where(untouched, spec_rows(p, i), solved) * factor(p, 5, i)
            for t in range(tiles):
                spec[p, t, pl.ds(i, BLOCKS, stride=steps), :] = damped[:, 128 * t : 128 * t + 128]
    parts = []
    for p in range(2):
        damped = jnp.concatenate([spec[p, t].astype(bf16) for t in range(tiles)], axis=1)
        parts.append(
            lax.dot_general(
                arrived_ref[p, :, width:], damped, (((0,), (0,)), ((), ())), preferred_element_type=f32
            )
        )
    home_ref[0] = (parts[0] + parts[1]).astype(bf16)
    home_ref[1] = (parts[0] - parts[1]).astype(bf16)


def pair_kernel(rows_ref, *pairs_refs):
    slots, groups, rows, width = rows_ref.shape
    order = slots * rows
    out_row = lax.broadcasted_iota(jnp.int32, (order, order), 0)
    in_row = lax.broadcasted_iota(jnp.int32, (order, order), 1)
    odd, rest = out_row // (order // 2), out_row % (order // 2)
    source = (rest % slots) * rows + 2 * (rest // slots) + odd
    shuffle = (in_row == source).astype(bf16)
    first_half = lax.broadcasted_iota(jnp.int32, (order // 2, width), 1) < width // 2

    def swap(values):
        return jnp.concatenate([values[:, width // 2 :], values[:, : width // 2]], axis=1)

    places = [ref.at[n] for ref in pairs_refs for n in range(ref.shape[0])]
    for g in range(groups):
        block = rows_ref[:, g].astype(f32).reshape(order, width).astype(bf16)
        moved = jnp.dot(shuffle, block, preferred_element_type=f32)
        even_rows, odd_rows = moved[: order // 2], moved[order // 2 :]
        real = jnp.where(first_half, even_rows, swap(odd_rows)).reshape(rows // 2, slots, width)
        imag = jnp.where(first_half, swap(even_rows), odd_rows).reshape(rows // 2, slots, width)
        both = jnp.concatenate([real, imag], axis=1).astype(bf16)
        for n in range(rows // 2):
            places[g * (rows // 2) + n][...] = both[n]


def zonal_kernel(tile, trig_ref, *refs):
    *operands, grid_ref = refs
    pairs, width = operands[0].shape[-3], operands[0].shape[-1]
    lons = trig_ref.shape[0]

    def coefficients(r):
        found = []
        for ref in operands:
            found += [ref[r]] if ref.ndim == 3 else [ref[z, r] for z in range(ref.shape[0])]
        return jnp.concatenate(found, axis=0)

    for r in range(0, pairs, 2):
        rhs = jnp.concatenate([coefficients(r), coefficients(r + 1)], axis=1)
        for column in range(0, 2 * width, 256):
            for lon in range(0, lons, tile):
                sums = jnp.dot(
                    trig_ref[lon : lon + tile], rhs[:, column : column + 256], preferred_element_type=f32
                )
                grid_ref[lon : lon + tile, r * width + column : r * width + column + 256] = sums.astype(bf16)


def zonal_tail_kernel(tile, trig_ref, *refs):
    zonal_kernel(tile, trig_ref, *refs[:-2], refs[-1])


def params(limit=VMEM_LIMIT):
    return pltpu.CompilerParams(vmem_limit_bytes=limit)


def whole_vmem(count):
    return [pl.BlockSpec(memory_space=pltpu.VMEM)] * count


def make_factors(bands):
    systems, _, _, steps = bands.shape
    return pl.pallas_call(
        factor_kernel,
        out_shape=(
            jax.ShapeDtypeStruct((systems, 6, BLOCKS, steps), f32),
            jax.ShapeDtypeStruct((systems, 6, BLOCKS, 128), f32),
        ),
        in_specs=whole_vmem(1),
        out_specs=tuple(whole_vmem(2)),
        compiler_params=params(),
        cost_estimate=pl.CostEstimate(flops=2_000_000_000, bytes_accessed=2_000_000, transcendentals=0),
        name="factor",
    )(bands)


def outgoing(fourier_rows, legendre, slots, j):
    _, rows, width = fourier_rows.shape
    pair_count = legendre.shape[2]

    anywhere = pl.BlockSpec(memory_space=pl.ANY)
    return pl.pallas_call(
        functools.partial(outgoing_kernel, j * slots),
        out_shape=jax.ShapeDtypeStruct((slots, rows, width + pair_count), bf16),
        in_specs=[anywhere, anywhere],
        out_specs=anywhere,
        scratch_shapes=[
            pltpu.VMEM((slots, rows, pair_count), f32),
            pltpu.VMEM((slots, rows, width + pair_count), bf16),
            pltpu.SemaphoreType.DMA((slots,)),
            pltpu.SemaphoreType.DMA((slots,)),
            pltpu.SemaphoreType.DMA((slots,)),
        ],
        compiler_params=params(),
        cost_estimate=pl.CostEstimate(
            flops=0, bytes_accessed=slots * rows * (4 * width + 6 * pair_count), transcendentals=0
        ),
        name="outgoing",
    )(fourier_rows, legendre)


def wave_step(arrived, factors, links, width):
    _, pair_count, _ = arrived.shape
    return pl.pallas_call(
        wave_kernel,
        out_shape=jax.ShapeDtypeStruct((2, pair_count, width), bf16),
        in_specs=whole_vmem(3),
        out_specs=whole_vmem(1)[0],
        scratch_shapes=[
            pltpu.VMEM((2, width // 128, pair_count, 128), f32),
            pltpu.VMEM((2, pair_count // BLOCKS, BLOCKS, width), f32),
        ],
        compiler_params=params(),
        cost_estimate=pl.CostEstimate(flops=8_000_000_000, bytes_accessed=6_000_000, transcendentals=0),
        name="wave",
    )(arrived, factors, links)


def cut_pairs(count):
    pairs = count // 2
    return [pairs * 4 // 5, pairs // 5] if pairs % 10 == 0 and count % 8 == 0 else [pairs]


def pair_rows(rows, pieces):
    slots, count, width = rows.shape
    if count % 8 or slots % 8:
        split = rows.reshape(slots, count // 2, 2, 2, width // 2)
        joined = split.transpose(1, 3, 0, 2, 4).reshape(count // 2, 2 * slots, width)
        return [joined[sum(pieces[:n]) : sum(pieces[: n + 1])] for n in range(len(pieces))]
    pairs = pl.pallas_call(
        pair_kernel,
        out_shape=[jax.ShapeDtypeStruct((piece, 2 * slots, width), bf16) for piece in pieces],
        in_specs=whole_vmem(1),
        out_specs=whole_vmem(len(pieces)),
        compiler_params=params(),
        cost_estimate=pl.CostEstimate(flops=2_000_000_000, bytes_accessed=2_400_000, transcendentals=0),
        name="pair",
    )(rows.reshape(slots, count // 8, 8, width))
    return list(pairs)


def stage_kernel(*refs):
    count = len(refs) // 2
    sems = refs[-1]
    copies = [pltpu.make_async_copy(refs[n], refs[count + n], sems.at[n]) for n in range(count)]
    for copy in copies:
        copy.start()
    for copy in copies:
        copy.wait()


def stage(arrays):
    return pl.pallas_call(
        stage_kernel,
        out_shape=[pltpu.VMEM(array.shape, array.dtype) for array in arrays],
        in_specs=[pl.BlockSpec(memory_space=pl.ANY)] * len(arrays),
        out_specs=whole_vmem(len(arrays)),
        scratch_shapes=[pltpu.SemaphoreType.DMA((len(arrays),))],
        compiler_params=params(4 * 2**20),
        cost_estimate=pl.CostEstimate(
            flops=0, bytes_accessed=sum(2 * array.size for array in arrays), transcendentals=0
        ),
        name="stage",
    )(*arrays)


def synthesize(trig, whole, extra, first, pieces, grid):
    lons, depth = trig.shape
    piece, pairs = extra[0].shape[-3], sum(pieces)
    width = extra[0].shape[-1]
    step = next(n for n in ((4, 2) if first else (10, 8, 6, 4, 2)) if piece % n == 0 and first % n == 0)
    ahead = first // step

    def spec(array, shift):
        lead = array.shape[:-3]
        block = lead + (step,) + array.shape[-2:]
        return pl.BlockSpec(block, lambda i: (0,) * len(lead) + (shift + i, 0, 0))

    operands = [trig, *whole, *extra]
    in_specs = [pl.BlockSpec((lons, depth), lambda i: (0, 0))]
    in_specs += [spec(array, ahead) for array in whole] + [spec(array, 0) for array in extra]
    if grid is not None:
        operands.append(grid)
        in_specs.append(pl.BlockSpec(memory_space=pl.ANY))
    return pl.pallas_call(
        functools.partial(zonal_kernel, lons) if grid is None else functools.partial(zonal_tail_kernel, lons if lons % 80 else lons // 5),
        out_shape=jax.ShapeDtypeStruct((lons, pairs * width), bf16),
        grid=(piece // step,),
        in_specs=in_specs,
        out_specs=pl.BlockSpec((lons, step * width), lambda i: (0, ahead + i)),
        input_output_aliases={} if grid is None else {len(operands) - 1: 0},
        compiler_params=params(30 * 2**20),
        cost_estimate=pl.CostEstimate(
            flops=4 * lons * depth * piece * width, bytes_accessed=2 * lons * piece * width, transcendentals=0
        ),
        name="zonal",
    )(*operands)


def on_device(fourier_rows, legendre, wavenumber, lower_diag, main_diag, upper_diag):
    lat_count = lax.axis_size("lat")
    wave_count = lax.axis_size("wave")
    lat_pos = lax.axis_index("lat")
    wave_pos = lax.axis_index("wave")
    group_slots, row_count, row_width = fourier_rows.shape
    pair_count = legendre.shape[2]
    lat_rows = 2 * pair_count
    chunks = group_slots // lat_count
    steps = pair_count // BLOCKS

    slot_ids = wavenumber.reshape(wave_count, chunks, lat_count)
    own_group = lax.dynamic_index_in_dim(slot_ids, wave_pos, 0, keepdims=False)
    wave_ids = lax.dynamic_index_in_dim(own_group, lat_pos, 1, keepdims=False)

    def own(band):
        return lax.dynamic_index_in_dim(
            band.reshape(chunks, lat_count, 2, pair_count), lat_pos, 1, keepdims=False
        )

    column_ids = jnp.arange(pair_count, dtype=jnp.int32)
    parity_ids = jnp.arange(2, dtype=jnp.int32)
    degree_int = wave_ids[:, None, None] + 2 * column_ids[None, None, :] + parity_ids[None, :, None]
    inside_mask = degree_int < lat_rows
    inside = inside_mask.astype(f32)
    degree = degree_int.astype(f32)
    degree_ratio = degree * (degree + 1.0) / (lat_rows * (lat_rows - 1.0))
    damping = 1.0 / (1.0 + damping_rate * degree_ratio * degree_ratio)
    not_first = (column_ids > 0).astype(f32)
    not_last = (column_ids < pair_count - 1).astype(f32)
    sub_band = own(lower_diag) * inside * not_first
    super_band = own(upper_diag) * inside * not_last
    center = jnp.where(inside_mask, own(main_diag), 1.0)
    bands = jnp.stack([sub_band, center, super_band, inside, damping], axis=2)
    factors, links = make_factors(bands.reshape(2 * chunks, 5, BLOCKS, steps))
    factors = factors.reshape(chunks, 2, 6, BLOCKS, steps)
    links = links.reshape(chunks, 2, 6, BLOCKS, 128)

    def swap_lat(values):
        return lax.all_to_all(values, "lat", split_axis=0, concat_axis=0, tiled=True)

    def gather_waves(values):
        return lax.all_gather(values, "wave", axis=0)

    def from_waves(values):
        return [values] + [
            lax.ppermute(values, "wave", [(w, (w + k) % wave_count) for w in range(wave_count)])
            for k in range(1, wave_count)
        ]

    def wave_rows(arrived, j):
        arrived = arrived.reshape(2, pair_count, row_width + pair_count)
        return wave_step(arrived, factors[j], links[j], row_width).reshape(lat_count, row_count, row_width)

    first_out = outgoing(fourier_rows, legendre, lat_count, 0)
    rows_later, table_later, first_out = lax.optimization_barrier((fourier_rows, legendre, first_out))
    ready = wave_rows(swap_lat(first_out), 0)
    pieces = cut_pairs(row_count)
    gathered, rest = [], None
    for j in range(1, chunks):
        out, ready = lax.optimization_barrier((outgoing(rows_later, table_later, lat_count, j), ready))
        gathered.append(gather_waves(ready))
        home = wave_rows(swap_lat(out), j)
        ready, *rest = pair_rows(swap_lat(home), pieces if j == chunks - 1 else [row_count // 2])
    first_rows, ready = lax.optimization_barrier((gathered[0], ready))
    last = gather_waves(ready)
    first_rows = swap_lat(first_rows.swapaxes(0, 1)).reshape(lat_count * wave_count, row_count, row_width)
    whole = pair_rows(first_rows, [row_count // 2]) + gathered[1:]

    lon_dev = NLON // wave_count
    lon_ids = wave_pos * lon_dev + jnp.arange(lon_dev, dtype=jnp.int32)
    blocks = [slot_ids[:, 0].T.reshape(-1)]
    blocks += [slot_ids[w, j] for j in range(1, chunks) for w in range(wave_count)]
    trig = zonal_matrix(blocks, lon_ids)
    if not rest:
        return synthesize(trig, whole, [last], 0, pieces, None)
    sources = (wave_pos - jnp.arange(wave_count)) % wave_count
    seen_ids = slot_ids[sources, chunks - 1]
    rest_trig = zonal_matrix(blocks[:-wave_count] + [seen_ids[k] for k in range(wave_count)], lon_ids)
    rest, last = lax.optimization_barrier((rest[0], last))
    whole = stage(whole)
    last = pltpu.with_memory_space_constraint(last, pltpu.MemorySpace.HBM)
    rest = from_waves(rest)
    grid = synthesize(trig, whole, [last], 0, pieces, None)
    return synthesize(rest_trig, whole, rest, pieces[0], pieces, grid)


def solution(mesh):
    placed = (
        P("wave", "lat", None),
        P("wave", "lat", None),
        P(),
        P("wave", None),
        P("wave", None),
        P("wave", None),
    )
    return jax.shard_map(
        on_device, mesh=mesh, in_specs=placed, out_specs=P("wave", "lat"), check_vma=False
    )
```

```python
import functools
import math

import jax
import jax.numpy as jnp
from jax import lax
from jax.experimental import pallas as pl
from jax.experimental.pallas import tpu as pltpu
from jax.sharding import PartitionSpec as P

NLON = 3200
LEV = 64
damping_rate = 4.0
BLOCKS = 8
VMEM_LIMIT = 56 * 2**20
f32 = jnp.float32
bf16 = jnp.bfloat16


def zonal_matrix(blocks, lon_ids):
    wave_ids = jnp.concatenate([jnp.concatenate([ids, ids]) for ids in blocks])
    is_sine = jnp.concatenate([jnp.arange(2 * ids.size) >= ids.size for ids in blocks])
    phase_index = lon_ids[:, None] * wave_ids[None, :] % NLON
    phase_angle = phase_index.astype(f32) * (2.0 * math.pi / NLON)
    return jnp.where(is_sine[None, :], -jnp.sin(phase_angle), jnp.cos(phase_angle)).astype(bf16)


def factor_kernel(bands_ref, factors_ref, links_ref):
    systems, _, _, steps = bands_ref.shape
    sub, center, sup, inside, damping = (bands_ref[:, n] for n in range(5))
    lanes = lax.broadcasted_iota(jnp.int32, (systems, BLOCKS, steps), 2)

    def column(values, i):
        return values[:, :, i : i + 1]

    def place(values, i, new):
        return jnp.where(lanes == i, new, values)

    zero = jnp.zeros((systems, BLOCKS, steps), f32)
    inv, scaled_sub, scaled_sup, left, right = zero, zero, zero, zero, zero
    for i in range(steps):
        pivot = column(center, i)
        if i:
            pivot = pivot - column(sub, i) * sup_part
        inv_part = 1.0 / pivot
        sub_part = column(sub, i) * inv_part
        sup_part = column(sup, i) * inv_part
        left_part = -sub_part * left_part if i else sub_part
        inv = place(inv, i, inv_part)
        scaled_sub = place(scaled_sub, i, sub_part)
        scaled_sup = place(scaled_sup, i, sup_part)
        left = place(left, i, left_part)
    solved_left = zero
    for i in reversed(range(steps)):
        if i == steps - 1:
            right_part = column(scaled_sup, i)
            left_part = column(left, i)
        else:
            right_part = -column(scaled_sup, i) * right_part
            left_part = column(left, i) - column(scaled_sup, i) * left_part
        right = place(right, i, right_part)
        solved_left = place(solved_left, i, left_part)
    for n, values in enumerate((inv * inside, scaled_sub, scaled_sup, right, solved_left, damping * inside)):
        factors_ref[:, n] = values
    right_first, right_last = column(right, 0), column(right, steps - 1)
    left_first, left_last = column(solved_left, 0), column(solved_left, steps - 1)
    beta = jnp.zeros((systems, 1, 1), f32)
    width = links_ref.shape[-1]
    for b in range(BLOCKS):
        row = slice(b, b + 1)
        scale = 1.0 / (1.0 - left_first[:, row] * beta)
        step = right_first[:, row] * scale
        across = left_last[:, row] * beta
        beta = right_last[:, row] + across * step
        for n, value in enumerate((scale, left_first[:, row] * scale, step, left_last[:, row], across, beta)):
            links_ref[:, n, b : b + 1, :] = jnp.broadcast_to(value, (systems, 1, width))


def outgoing_kernel(first, rows_hbm, table_hbm, out_hbm, table, joined, rows_sems, table_sems, out_sems):
    slots, _, width = joined.shape[0], joined.shape[1], rows_hbm.shape[2]
    copies = []
    for s in range(slots):
        copies.append(pltpu.make_async_copy(table_hbm.at[first + s], table.at[s], table_sems.at[s]))
        copies.append(
            pltpu.make_async_copy(rows_hbm.at[first + s], joined.at[s, :, pl.ds(0, width)], rows_sems.at[s])
        )
    for copy in copies:
        copy.start()
    sends = []
    for s in range(slots):
        copies[2 * s].wait()
        joined[s, :, width:] = table[s].astype(bf16)
        copies[2 * s + 1].wait()
        sends.append(pltpu.make_async_copy(joined.at[s], out_hbm.at[s], out_sems.at[s]))
        sends[s].start()
    for send in sends:
        send.wait()


def wave_kernel(arrived_ref, factors_ref, links_ref, home_ref, spec, part):
    _, pair_count, width = home_ref.shape
    steps = pair_count // BLOCKS
    tiles = width // 128
    north = arrived_ref[0, :, :width].astype(f32)
    south = arrived_ref[1, :, :width].astype(f32)
    for p in range(2):
        folded = (north + south if p == 0 else north - south).astype(bf16)
        spectral = jnp.dot(arrived_ref[p, :, width:], folded, preferred_element_type=f32)
        for t in range(tiles):
            spec[p, t] = spectral[:, 128 * t : 128 * t + 128]

    def spec_rows(p, i):
        return jnp.concatenate([spec[p, t, pl.ds(i, BLOCKS, stride=steps), :] for t in range(tiles)], axis=1)

    def factor(p, n, i):
        return factors_ref[p, n, :, i : i + 1]

    running = [None, None]
    for i in range(steps):
        for p in range(2):
            value = spec_rows(p, i) * factor(p, 0, i)
            if i:
                value = value - factor(p, 1, i) * running[p]
            part[p, i] = value
            running[p] = value
    last = list(running)
    for i in reversed(range(steps - 1)):
        for p in range(2):
            value = part[p, i] - factor(p, 2, i) * running[p]
            part[p, i] = value
            running[p] = value
    first = running
    after, before = [], []
    for p in range(2):
        def link(n, b):
            return jnp.concatenate([links_ref[p, n, b : b + 1, :]] * tiles, axis=1)

        alpha = jnp.zeros((1, width), f32)
        heads, tails = [], []
        for b in range(BLOCKS):
            row = slice(b, b + 1)
            head = first[p][row] * link(0, b) - link(1, b) * alpha
            alpha = last[p][row] - link(3, b) * alpha + link(4, b) * head
            heads.append(head)
            tails.append(alpha)
        ahead = jnp.zeros((1, width), f32)
        next_heads, prev_tails = [None] * BLOCKS, [jnp.zeros((1, width), f32)] * BLOCKS
        for b in reversed(range(BLOCKS)):
            next_heads[b] = ahead
            if b + 1 < BLOCKS:
                prev_tails[b + 1] = tails[b] - link(5, b) * ahead
            ahead = heads[b] - link(2, b) * ahead
        after.append(jnp.concatenate(next_heads, axis=0))
        before.append(jnp.concatenate(prev_tails, axis=0))
    half = lax.broadcasted_iota(jnp.int32, (BLOCKS, width), 1) % (width // 2)
    untouched = half < LEV
    for i in range(steps):
        for p in range(2):
            solved = part[p, i] - factor(p, 3, i) * after[p] - factor(p, 4, i) * before[p]
            damped = jnp.where(untouched, spec_rows(p, i), solved) * factor(p, 5, i)
            for t in range(tiles):
                spec[p, t, pl.ds(i, BLOCKS, stride=steps), :] = damped[:, 128 * t : 128 * t + 128]
    parts = []
    for p in range(2):
        damped = jnp.concatenate([spec[p, t].astype(bf16) for t in range(tiles)], axis=1)
        parts.append(
            lax.dot_general(
                arrived_ref[p, :, width:], damped, (((0,), (0,)), ((), ())), preferred_element_type=f32
            )
        )
    home_ref[0] = (parts[0] + parts[1]).astype(bf16)
    home_ref[1] = (parts[0] - parts[1]).astype(bf16)


def pair_kernel(rows_ref, *pairs_refs):
    slots, groups, rows, width = rows_ref.shape
    order = slots * rows
    out_row = lax.broadcasted_iota(jnp.int32, (order, order), 0)
    in_row = lax.broadcasted_iota(jnp.int32, (order, order), 1)
    odd, rest = out_row // (order // 2), out_row % (order // 2)
    source = (rest % slots) * rows + 2 * (rest // slots) + odd
    shuffle = (in_row == source).astype(bf16)
    first_half = lax.broadcasted_iota(jnp.int32, (order // 2, width), 1) < width // 2

    def swap(values):
        return jnp.concatenate([values[:, width // 2 :], values[:, : width // 2]], axis=1)

    places = [ref.at[n] for ref in pairs_refs for n in range(ref.shape[0])]
    for g in range(groups):
        block = rows_ref[:, g].astype(f32).reshape(order, width).astype(bf16)
        moved = jnp.dot(shuffle, block, preferred_element_type=f32)
        even_rows, odd_rows = moved[: order // 2], moved[order // 2 :]
        real = jnp.where(first_half, even_rows, swap(odd_rows)).reshape(rows // 2, slots, width)
        imag = jnp.where(first_half, swap(even_rows), odd_rows).reshape(rows // 2, slots, width)
        both = jnp.concatenate([real, imag], axis=1).astype(bf16)
        for n in range(rows // 2):
            places[g * (rows // 2) + n][...] = both[n]


def zonal_kernel(tile, trig_ref, *refs):
    *operands, grid_ref = refs
    pairs, width = operands[0].shape[-3], operands[0].shape[-1]
    lons = trig_ref.shape[0]

    def coefficients(r):
        found = []
        for ref in operands:
            found += [ref[r]] if ref.ndim == 3 else [ref[z, r] for z in range(ref.shape[0])]
        return jnp.concatenate(found, axis=0)

    for r in range(0, pairs, 2):
        rhs = jnp.concatenate([coefficients(r), coefficients(r + 1)], axis=1)
        for column in range(0, 2 * width, 256):
            for lon in range(0, lons, tile):
                sums = jnp.dot(
                    trig_ref[lon : lon + tile], rhs[:, column : column + 256], preferred_element_type=f32
                )
                grid_ref[lon : lon + tile, r * width + column : r * width + column + 256] = sums.astype(bf16)


def zonal_tail_kernel(tile, trig_ref, *refs):
    zonal_kernel(tile, trig_ref, *refs[:-2], refs[-1])


def params(limit=VMEM_LIMIT):
    return pltpu.CompilerParams(vmem_limit_bytes=limit)


def whole_vmem(count):
    return [pl.BlockSpec(memory_space=pltpu.VMEM)] * count


def make_factors(bands):
    systems, _, _, steps = bands.shape
    return pl.pallas_call(
        factor_kernel,
        out_shape=(
            jax.ShapeDtypeStruct((systems, 6, BLOCKS, steps), f32),
            jax.ShapeDtypeStruct((systems, 6, BLOCKS, 128), f32),
        ),
        in_specs=whole_vmem(1),
        out_specs=tuple(whole_vmem(2)),
        compiler_params=params(),
        cost_estimate=pl.CostEstimate(flops=2_000_000_000, bytes_accessed=2_000_000, transcendentals=0),
        name="factor",
    )(bands)


def outgoing(fourier_rows, legendre, slots, j):
    _, rows, width = fourier_rows.shape
    pair_count = legendre.shape[2]

    anywhere = pl.BlockSpec(memory_space=pl.ANY)
    return pl.pallas_call(
        functools.partial(outgoing_kernel, j * slots),
        out_shape=jax.ShapeDtypeStruct((slots, rows, width + pair_count), bf16),
        in_specs=[anywhere, anywhere],
        out_specs=anywhere,
        scratch_shapes=[
            pltpu.VMEM((slots, rows, pair_count), f32),
            pltpu.VMEM((slots, rows, width + pair_count), bf16),
            pltpu.SemaphoreType.DMA((slots,)),
            pltpu.SemaphoreType.DMA((slots,)),
            pltpu.SemaphoreType.DMA((slots,)),
        ],
        compiler_params=params(),
        cost_estimate=pl.CostEstimate(
            flops=0, bytes_accessed=slots * rows * (4 * width + 6 * pair_count), transcendentals=0
        ),
        name="outgoing",
    )(fourier_rows, legendre)


def wave_step(arrived, factors, links, width):
    _, pair_count, _ = arrived.shape
    return pl.pallas_call(
        wave_kernel,
        out_shape=jax.ShapeDtypeStruct((2, pair_count, width), bf16),
        in_specs=whole_vmem(3),
        out_specs=whole_vmem(1)[0],
        scratch_shapes=[
            pltpu.VMEM((2, width // 128, pair_count, 128), f32),
            pltpu.VMEM((2, pair_count // BLOCKS, BLOCKS, width), f32),
        ],
        compiler_params=params(),
        cost_estimate=pl.CostEstimate(flops=8_000_000_000, bytes_accessed=6_000_000, transcendentals=0),
        name="wave",
    )(arrived, factors, links)


def cut_pairs(count):
    pairs = count // 2
    return [pairs * 4 // 5, pairs // 5] if pairs % 10 == 0 and count % 8 == 0 else [pairs]


def pair_rows(rows, pieces):
    slots, count, width = rows.shape
    if count % 8 or slots % 8:
        split = rows.reshape(slots, count // 2, 2, 2, width // 2)
        joined = split.transpose(1, 3, 0, 2, 4).reshape(count // 2, 2 * slots, width)
        return [joined[sum(pieces[:n]) : sum(pieces[: n + 1])] for n in range(len(pieces))]
    pairs = pl.pallas_call(
        pair_kernel,
        out_shape=[jax.ShapeDtypeStruct((piece, 2 * slots, width), bf16) for piece in pieces],
        in_specs=whole_vmem(1),
        out_specs=whole_vmem(len(pieces)),
        compiler_params=params(),
        cost_estimate=pl.CostEstimate(flops=2_000_000_000, bytes_accessed=2_400_000, transcendentals=0),
        name="pair",
    )(rows.reshape(slots, count // 8, 8, width))
    return list(pairs)


def synthesize(trig, whole, extra, first, pieces, grid):
    lons, depth = trig.shape
    piece, pairs = extra[0].shape[-3], sum(pieces)
    width = extra[0].shape[-1]
    step = next(n for n in ((4, 2) if first else (10, 8, 6, 4, 2)) if piece % n == 0 and first % n == 0)
    ahead = first // step

    def spec(array, shift):
        lead = array.shape[:-3]
        block = lead + (step,) + array.shape[-2:]
        return pl.BlockSpec(block, lambda i: (0,) * len(lead) + (shift + i, 0, 0))

    operands = [trig, *whole, *extra]
    in_specs = [pl.BlockSpec((lons, depth), lambda i: (0, 0))]
    in_specs += [spec(array, ahead) for array in whole] + [spec(array, 0) for array in extra]
    if grid is not None:
        operands.append(grid)
        in_specs.append(pl.BlockSpec(memory_space=pl.ANY))
    return pl.pallas_call(
        functools.partial(zonal_kernel, lons) if grid is None else functools.partial(zonal_tail_kernel, lons if lons % 80 else lons // 5),
        out_shape=jax.ShapeDtypeStruct((lons, pairs * width), bf16),
        grid=(piece // step,),
        in_specs=in_specs,
        out_specs=pl.BlockSpec((lons, step * width), lambda i: (0, ahead + i)),
        input_output_aliases={} if grid is None else {len(operands) - 1: 0},
        compiler_params=params(30 * 2**20),
        cost_estimate=pl.CostEstimate(
            flops=4 * lons * depth * piece * width, bytes_accessed=2 * lons * piece * width, transcendentals=0
        ),
        name="zonal",
    )(*operands)


def on_device(fourier_rows, legendre, wavenumber, lower_diag, main_diag, upper_diag):
    lat_count = lax.axis_size("lat")
    wave_count = lax.axis_size("wave")
    lat_pos = lax.axis_index("lat")
    wave_pos = lax.axis_index("wave")
    group_slots, row_count, row_width = fourier_rows.shape
    pair_count = legendre.shape[2]
    lat_rows = 2 * pair_count
    chunks = group_slots // lat_count
    steps = pair_count // BLOCKS

    slot_ids = wavenumber.reshape(wave_count, chunks, lat_count)
    own_group = lax.dynamic_index_in_dim(slot_ids, wave_pos, 0, keepdims=False)
    wave_ids = lax.dynamic_index_in_dim(own_group, lat_pos, 1, keepdims=False)

    def own(band):
        return lax.dynamic_index_in_dim(
            band.reshape(chunks, lat_count, 2, pair_count), lat_pos, 1, keepdims=False
        )

    column_ids = jnp.arange(pair_count, dtype=jnp.int32)
    parity_ids = jnp.arange(2, dtype=jnp.int32)
    degree_int = wave_ids[:, None, None] + 2 * column_ids[None, None, :] + parity_ids[None, :, None]
    inside_mask = degree_int < lat_rows
    inside = inside_mask.astype(f32)
    degree = degree_int.astype(f32)
    degree_ratio = degree * (degree + 1.0) / (lat_rows * (lat_rows - 1.0))
    damping = 1.0 / (1.0 + damping_rate * degree_ratio * degree_ratio)
    not_first = (column_ids > 0).astype(f32)
    not_last = (column_ids < pair_count - 1).astype(f32)
    sub_band = own(lower_diag) * inside * not_first
    super_band = own(upper_diag) * inside * not_last
    center = jnp.where(inside_mask, own(main_diag), 1.0)
    bands = jnp.stack([sub_band, center, super_band, inside, damping], axis=2)
    factors, links = make_factors(bands.reshape(2 * chunks, 5, BLOCKS, steps))
    factors = factors.reshape(chunks, 2, 6, BLOCKS, steps)
    links = links.reshape(chunks, 2, 6, BLOCKS, 128)

    def swap_lat(values):
        return lax.all_to_all(values, "lat", split_axis=0, concat_axis=0, tiled=True)

    def gather_waves(values):
        return lax.all_gather(values, "wave", axis=0)

    def from_waves(values):
        return [values] + [
            lax.ppermute(values, "wave", [(w, (w + k) % wave_count) for w in range(wave_count)])
            for k in range(1, wave_count)
        ]

    def wave_rows(arrived, j):
        arrived = arrived.reshape(2, pair_count, row_width + pair_count)
        return wave_step(arrived, factors[j], links[j], row_width).reshape(lat_count, row_count, row_width)

    first_out = outgoing(fourier_rows, legendre, lat_count, 0)
    rows_later, table_later, first_out = lax.optimization_barrier((fourier_rows, legendre, first_out))
    ready = wave_rows(swap_lat(first_out), 0)
    pieces = cut_pairs(row_count)
    gathered, rest = [], None
    for j in range(1, chunks):
        out, ready = lax.optimization_barrier((outgoing(rows_later, table_later, lat_count, j), ready))
        gathered.append(gather_waves(ready))
        home = wave_rows(swap_lat(out), j)
        ready, *rest = pair_rows(swap_lat(home), pieces if j == chunks - 1 else [row_count // 2])
    first_rows, ready = lax.optimization_barrier((gathered[0], ready))
    last = gather_waves(ready)
    first_rows = swap_lat(first_rows.swapaxes(0, 1)).reshape(lat_count * wave_count, row_count, row_width)
    whole = pair_rows(first_rows, [row_count // 2]) + gathered[1:]

    lon_dev = NLON // wave_count
    lon_ids = wave_pos * lon_dev + jnp.arange(lon_dev, dtype=jnp.int32)
    blocks = [slot_ids[:, 0].T.reshape(-1)]
    blocks += [slot_ids[w, j] for j in range(1, chunks) for w in range(wave_count)]
    trig = zonal_matrix(blocks, lon_ids)
    if not rest:
        return synthesize(trig, whole, [last], 0, pieces, None)
    sources = (wave_pos - jnp.arange(wave_count)) % wave_count
    seen_ids = slot_ids[sources, chunks - 1]
    rest_trig = zonal_matrix(blocks[:-wave_count] + [seen_ids[k] for k in range(wave_count)], lon_ids)
    rest, last, trig, rest_trig, *whole = lax.optimization_barrier((rest[0], last, trig, rest_trig, *whole))
    whole = [pltpu.with_memory_space_constraint(array, pltpu.MemorySpace.HBM) for array in whole]
    last = pltpu.with_memory_space_constraint(last, pltpu.MemorySpace.HBM)
    rest = from_waves(rest)
    grid = synthesize(trig, whole, [last], 0, pieces, None)
    return synthesize(rest_trig, whole, rest, pieces[0], pieces, grid)


def solution(mesh):
    placed = (
        P("wave", "lat", None),
        P("wave", "lat", None),
        P(),
        P("wave", None),
        P("wave", None),
        P("wave", None),
    )
    return jax.shard_map(
        on_device, mesh=mesh, in_specs=placed, out_specs=P("wave", "lat"), check_vma=False
    )
```

```python
import functools
import math

import jax
import jax.numpy as jnp
from jax import lax
from jax.experimental import pallas as pl
from jax.experimental.pallas import tpu as pltpu
from jax.sharding import PartitionSpec as P

NLON = 3200
LEV = 64
damping_rate = 4.0
BLOCKS = 8
VMEM_LIMIT = 56 * 2**20
f32 = jnp.float32
bf16 = jnp.bfloat16


def zonal_matrix(blocks, lon_ids):
    wave_ids = jnp.concatenate([jnp.concatenate([ids, ids]) for ids in blocks])
    is_sine = jnp.concatenate([jnp.arange(2 * ids.size) >= ids.size for ids in blocks])
    phase_index = lon_ids[:, None] * wave_ids[None, :] % NLON
    phase_angle = phase_index.astype(f32) * (2.0 * math.pi / NLON)
    return jnp.where(is_sine[None, :], -jnp.sin(phase_angle), jnp.cos(phase_angle)).astype(bf16)


def factor_kernel(bands_ref, factors_ref, links_ref):
    systems, _, _, steps = bands_ref.shape
    sub, center, sup, inside, damping = (bands_ref[:, n] for n in range(5))
    lanes = lax.broadcasted_iota(jnp.int32, (systems, BLOCKS, steps), 2)

    def column(values, i):
        return values[:, :, i : i + 1]

    def place(values, i, new):
        return jnp.where(lanes == i, new, values)

    zero = jnp.zeros((systems, BLOCKS, steps), f32)
    inv, scaled_sub, scaled_sup, left, right = zero, zero, zero, zero, zero
    for i in range(steps):
        pivot = column(center, i)
        if i:
            pivot = pivot - column(sub, i) * sup_part
        inv_part = 1.0 / pivot
        sub_part = column(sub, i) * inv_part
        sup_part = column(sup, i) * inv_part
        left_part = -sub_part * left_part if i else sub_part
        inv = place(inv, i, inv_part)
        scaled_sub = place(scaled_sub, i, sub_part)
        scaled_sup = place(scaled_sup, i, sup_part)
        left = place(left, i, left_part)
    solved_left = zero
    for i in reversed(range(steps)):
        if i == steps - 1:
            right_part = column(scaled_sup, i)
            left_part = column(left, i)
        else:
            right_part = -column(scaled_sup, i) * right_part
            left_part = column(left, i) - column(scaled_sup, i) * left_part
        right = place(right, i, right_part)
        solved_left = place(solved_left, i, left_part)
    for n, values in enumerate((inv * inside, scaled_sub, scaled_sup, right, solved_left, damping * inside)):
        factors_ref[:, n] = values
    right_first, right_last = column(right, 0), column(right, steps - 1)
    left_first, left_last = column(solved_left, 0), column(solved_left, steps - 1)
    beta = jnp.zeros((systems, 1, 1), f32)
    width = links_ref.shape[-1]
    for b in range(BLOCKS):
        row = slice(b, b + 1)
        scale = 1.0 / (1.0 - left_first[:, row] * beta)
        step = right_first[:, row] * scale
        across = left_last[:, row] * beta
        beta = right_last[:, row] + across * step
        for n, value in enumerate((scale, left_first[:, row] * scale, step, left_last[:, row], across, beta)):
            links_ref[:, n, b : b + 1, :] = jnp.broadcast_to(value, (systems, 1, width))


def outgoing_kernel(first, rows_hbm, table_hbm, out_hbm, table, joined, rows_sems, table_sems, out_sems):
    slots, _, width = joined.shape[0], joined.shape[1], rows_hbm.shape[2]
    copies = []
    for s in range(slots):
        copies.append(pltpu.make_async_copy(table_hbm.at[first + s], table.at[s], table_sems.at[s]))
        copies.append(
            pltpu.make_async_copy(rows_hbm.at[first + s], joined.at[s, :, pl.ds(0, width)], rows_sems.at[s])
        )
    for copy in copies:
        copy.start()
    sends = []
    for s in range(slots):
        copies[2 * s].wait()
        joined[s, :, width:] = table[s].astype(bf16)
        copies[2 * s + 1].wait()
        sends.append(pltpu.make_async_copy(joined.at[s], out_hbm.at[s], out_sems.at[s]))
        sends[s].start()
    for send in sends:
        send.wait()


def wave_kernel(arrived_ref, factors_ref, links_ref, home_ref, spec, part):
    _, pair_count, width = home_ref.shape
    steps = pair_count // BLOCKS
    tiles = width // 128
    north = arrived_ref[0, :, :width].astype(f32)
    south = arrived_ref[1, :, :width].astype(f32)
    for p in range(2):
        folded = (north + south if p == 0 else north - south).astype(bf16)
        spectral = jnp.dot(arrived_ref[p, :, width:], folded, preferred_element_type=f32)
        for t in range(tiles):
            spec[p, t] = spectral[:, 128 * t : 128 * t + 128]

    def spec_rows(p, i):
        return jnp.concatenate([spec[p, t, pl.ds(i, BLOCKS, stride=steps), :] for t in range(tiles)], axis=1)

    def factor(p, n, i):
        return factors_ref[p, n, :, i : i + 1]

    running = [None, None]
    for i in range(steps):
        for p in range(2):
            value = spec_rows(p, i) * factor(p, 0, i)
            if i:
                value = value - factor(p, 1, i) * running[p]
            part[p, i] = value
            running[p] = value
    last = list(running)
    for i in reversed(range(steps - 1)):
        for p in range(2):
            value = part[p, i] - factor(p, 2, i) * running[p]
            part[p, i] = value
            running[p] = value
    first = running
    after, before = [], []
    for p in range(2):
        def link(n, b):
            return jnp.concatenate([links_ref[p, n, b : b + 1, :]] * tiles, axis=1)

        alpha = jnp.zeros((1, width), f32)
        heads, tails = [], []
        for b in range(BLOCKS):
            row = slice(b, b + 1)
            head = first[p][row] * link(0, b) - link(1, b) * alpha
            alpha = last[p][row] - link(3, b) * alpha + link(4, b) * head
            heads.append(head)
            tails.append(alpha)
        ahead = jnp.zeros((1, width), f32)
        next_heads, prev_tails = [None] * BLOCKS, [jnp.zeros((1, width), f32)] * BLOCKS
        for b in reversed(range(BLOCKS)):
            next_heads[b] = ahead
            if b + 1 < BLOCKS:
                prev_tails[b + 1] = tails[b] - link(5, b) * ahead
            ahead = heads[b] - link(2, b) * ahead
        after.append(jnp.concatenate(next_heads, axis=0))
        before.append(jnp.concatenate(prev_tails, axis=0))
    half = lax.broadcasted_iota(jnp.int32, (BLOCKS, width), 1) % (width // 2)
    untouched = half < LEV
    for i in range(steps):
        for p in range(2):
            solved = part[p, i] - factor(p, 3, i) * after[p] - factor(p, 4, i) * before[p]
            damped = jnp.where(untouched, spec_rows(p, i), solved) * factor(p, 5, i)
            for t in range(tiles):
                spec[p, t, pl.ds(i, BLOCKS, stride=steps), :] = damped[:, 128 * t : 128 * t + 128]
    parts = []
    for p in range(2):
        damped = jnp.concatenate([spec[p, t].astype(bf16) for t in range(tiles)], axis=1)
        parts.append(
            lax.dot_general(
                arrived_ref[p, :, width:], damped, (((0,), (0,)), ((), ())), preferred_element_type=f32
            )
        )
    home_ref[0] = (parts[0] + parts[1]).astype(bf16)
    home_ref[1] = (parts[0] - parts[1]).astype(bf16)


def pair_kernel(rows_ref, *pairs_refs):
    slots, groups, rows, width = rows_ref.shape
    order = slots * rows
    out_row = lax.broadcasted_iota(jnp.int32, (order, order), 0)
    in_row = lax.broadcasted_iota(jnp.int32, (order, order), 1)
    odd, rest = out_row // (order // 2), out_row % (order // 2)
    source = (rest % slots) * rows + 2 * (rest // slots) + odd
    shuffle = (in_row == source).astype(bf16)
    first_half = lax.broadcasted_iota(jnp.int32, (order // 2, width), 1) < width // 2

    def swap(values):
        return jnp.concatenate([values[:, width // 2 :], values[:, : width // 2]], axis=1)

    places = [ref.at[n] for ref in pairs_refs for n in range(ref.shape[0])]
    for g in range(groups):
        block = rows_ref[:, g].astype(f32).reshape(order, width).astype(bf16)
        moved = jnp.dot(shuffle, block, preferred_element_type=f32)
        even_rows, odd_rows = moved[: order // 2], moved[order // 2 :]
        real = jnp.where(first_half, even_rows, swap(odd_rows)).reshape(rows // 2, slots, width)
        imag = jnp.where(first_half, swap(even_rows), odd_rows).reshape(rows // 2, slots, width)
        both = jnp.concatenate([real, imag], axis=1).astype(bf16)
        for n in range(rows // 2):
            places[g * (rows // 2) + n][...] = both[n]


def zonal_kernel(tile, trig_ref, *refs):
    *operands, grid_ref = refs
    pairs, width = operands[0].shape[-3], operands[0].shape[-1]
    lons = trig_ref.shape[0]

    def coefficients(r):
        found = []
        for ref in operands:
            found += [ref[r]] if ref.ndim == 3 else [ref[z, r] for z in range(ref.shape[0])]
        return jnp.concatenate(found, axis=0)

    for r in range(0, pairs, 2):
        rhs = jnp.concatenate([coefficients(r), coefficients(r + 1)], axis=1)
        for column in range(0, 2 * width, 256):
            for lon in range(0, lons, tile):
                sums = jnp.dot(
                    trig_ref[lon : lon + tile], rhs[:, column : column + 256], preferred_element_type=f32
                )
                grid_ref[lon : lon + tile, r * width + column : r * width + column + 256] = sums.astype(bf16)


def zonal_tail_kernel(tile, trig_ref, *refs):
    zonal_kernel(tile, trig_ref, *refs[:-2], refs[-1])


def params(limit=VMEM_LIMIT):
    return pltpu.CompilerParams(vmem_limit_bytes=limit)


def whole_vmem(count):
    return [pl.BlockSpec(memory_space=pltpu.VMEM)] * count


def make_factors(bands):
    systems, _, _, steps = bands.shape
    return pl.pallas_call(
        factor_kernel,
        out_shape=(
            jax.ShapeDtypeStruct((systems, 6, BLOCKS, steps), f32),
            jax.ShapeDtypeStruct((systems, 6, BLOCKS, 128), f32),
        ),
        in_specs=whole_vmem(1),
        out_specs=tuple(whole_vmem(2)),
        compiler_params=params(),
        cost_estimate=pl.CostEstimate(flops=2_000_000_000, bytes_accessed=2_000_000, transcendentals=0),
        name="factor",
    )(bands)


def outgoing(fourier_rows, legendre, slots, j):
    _, rows, width = fourier_rows.shape
    pair_count = legendre.shape[2]

    anywhere = pl.BlockSpec(memory_space=pl.ANY)
    return pl.pallas_call(
        functools.partial(outgoing_kernel, j * slots),
        out_shape=jax.ShapeDtypeStruct((slots, rows, width + pair_count), bf16),
        in_specs=[anywhere, anywhere],
        out_specs=anywhere,
        scratch_shapes=[
            pltpu.VMEM((slots, rows, pair_count), f32),
            pltpu.VMEM((slots, rows, width + pair_count), bf16),
            pltpu.SemaphoreType.DMA((slots,)),
            pltpu.SemaphoreType.DMA((slots,)),
            pltpu.SemaphoreType.DMA((slots,)),
        ],
        compiler_params=params(),
        cost_estimate=pl.CostEstimate(
            flops=0, bytes_accessed=slots * rows * (4 * width + 6 * pair_count), transcendentals=0
        ),
        name="outgoing",
    )(fourier_rows, legendre)


def wave_step(arrived, factors, links, width):
    _, pair_count, _ = arrived.shape
    return pl.pallas_call(
        wave_kernel,
        out_shape=jax.ShapeDtypeStruct((2, pair_count, width), bf16),
        in_specs=whole_vmem(3),
        out_specs=whole_vmem(1)[0],
        scratch_shapes=[
            pltpu.VMEM((2, width // 128, pair_count, 128), f32),
            pltpu.VMEM((2, pair_count // BLOCKS, BLOCKS, width), f32),
        ],
        compiler_params=params(),
        cost_estimate=pl.CostEstimate(flops=8_000_000_000, bytes_accessed=6_000_000, transcendentals=0),
        name="wave",
    )(arrived, factors, links)


def cut_pairs(count):
    pairs = count // 2
    return [pairs * 7 // 10, pairs * 3 // 10] if pairs % 20 == 0 and count % 8 == 0 else [pairs]


def pair_rows(rows, pieces):
    slots, count, width = rows.shape
    if count % 8 or slots % 8:
        split = rows.reshape(slots, count // 2, 2, 2, width // 2)
        joined = split.transpose(1, 3, 0, 2, 4).reshape(count // 2, 2 * slots, width)
        return [joined[sum(pieces[:n]) : sum(pieces[: n + 1])] for n in range(len(pieces))]
    pairs = pl.pallas_call(
        pair_kernel,
        out_shape=[jax.ShapeDtypeStruct((piece, 2 * slots, width), bf16) for piece in pieces],
        in_specs=whole_vmem(1),
        out_specs=whole_vmem(len(pieces)),
        compiler_params=params(),
        cost_estimate=pl.CostEstimate(flops=2_000_000_000, bytes_accessed=2_400_000, transcendentals=0),
        name="pair",
    )(rows.reshape(slots, count // 8, 8, width))
    return list(pairs)


def synthesize(trig, whole, extra, first, pieces, grid):
    lons, depth = trig.shape
    piece, pairs = extra[0].shape[-3], sum(pieces)
    width = extra[0].shape[-1]
    step = next(n for n in (10, 8, 6, 4, 2) if piece % n == 0 and first % n == 0)
    ahead = first // step

    def spec(array, shift):
        lead = array.shape[:-3]
        block = lead + (step,) + array.shape[-2:]
        return pl.BlockSpec(block, lambda i: (0,) * len(lead) + (shift + i, 0, 0))

    operands = [trig, *whole, *extra]
    in_specs = [pl.BlockSpec((lons, depth), lambda i: (0, 0))]
    in_specs += [spec(array, ahead) for array in whole] + [spec(array, 0) for array in extra]
    if grid is not None:
        operands.append(grid)
        in_specs.append(pl.BlockSpec(memory_space=pl.ANY))
    return pl.pallas_call(
        functools.partial(zonal_kernel, lons) if grid is None else functools.partial(zonal_tail_kernel, lons if lons % 80 else lons // 5),
        out_shape=jax.ShapeDtypeStruct((lons, pairs * width), bf16),
        grid=(piece // step,),
        in_specs=in_specs,
        out_specs=pl.BlockSpec((lons, step * width), lambda i: (0, ahead + i)),
        input_output_aliases={} if grid is None else {len(operands) - 1: 0},
        compiler_params=params(30 * 2**20),
        cost_estimate=pl.CostEstimate(
            flops=4 * lons * depth * piece * width, bytes_accessed=2 * lons * piece * width, transcendentals=0
        ),
        name="zonal",
    )(*operands)


def on_device(fourier_rows, legendre, wavenumber, lower_diag, main_diag, upper_diag):
    lat_count = lax.axis_size("lat")
    wave_count = lax.axis_size("wave")
    lat_pos = lax.axis_index("lat")
    wave_pos = lax.axis_index("wave")
    group_slots, row_count, row_width = fourier_rows.shape
    pair_count = legendre.shape[2]
    lat_rows = 2 * pair_count
    chunks = group_slots // lat_count
    steps = pair_count // BLOCKS

    slot_ids = wavenumber.reshape(wave_count, chunks, lat_count)
    own_group = lax.dynamic_index_in_dim(slot_ids, wave_pos, 0, keepdims=False)
    wave_ids = lax.dynamic_index_in_dim(own_group, lat_pos, 1, keepdims=False)

    def own(band):
        return lax.dynamic_index_in_dim(
            band.reshape(chunks, lat_count, 2, pair_count), lat_pos, 1, keepdims=False
        )

    column_ids = jnp.arange(pair_count, dtype=jnp.int32)
    parity_ids = jnp.arange(2, dtype=jnp.int32)
    degree_int = wave_ids[:, None, None] + 2 * column_ids[None, None, :] + parity_ids[None, :, None]
    inside_mask = degree_int < lat_rows
    inside = inside_mask.astype(f32)
    degree = degree_int.astype(f32)
    degree_ratio = degree * (degree + 1.0) / (lat_rows * (lat_rows - 1.0))
    damping = 1.0 / (1.0 + damping_rate * degree_ratio * degree_ratio)
    not_first = (column_ids > 0).astype(f32)
    not_last = (column_ids < pair_count - 1).astype(f32)
    sub_band = own(lower_diag) * inside * not_first
    super_band = own(upper_diag) * inside * not_last
    center = jnp.where(inside_mask, own(main_diag), 1.0)
    bands = jnp.stack([sub_band, center, super_band, inside, damping], axis=2)
    factors, links = make_factors(bands.reshape(2 * chunks, 5, BLOCKS, steps))
    factors = factors.reshape(chunks, 2, 6, BLOCKS, steps)
    links = links.reshape(chunks, 2, 6, BLOCKS, 128)

    def swap_lat(values):
        return lax.all_to_all(values, "lat", split_axis=0, concat_axis=0, tiled=True)

    def gather_waves(values):
        return lax.all_gather(values, "wave", axis=0)

    def from_waves(values):
        return [values] + [
            lax.ppermute(values, "wave", [(w, (w + k) % wave_count) for w in range(wave_count)])
            for k in range(1, wave_count)
        ]

    def wave_rows(arrived, j):
        arrived = arrived.reshape(2, pair_count, row_width + pair_count)
        return wave_step(arrived, factors[j], links[j], row_width).reshape(lat_count, row_count, row_width)

    first_out = outgoing(fourier_rows, legendre, lat_count, 0)
    rows_later, table_later, first_out = lax.optimization_barrier((fourier_rows, legendre, first_out))
    ready = wave_rows(swap_lat(first_out), 0)
    pieces = cut_pairs(row_count)
    gathered, rest = [], None
    for j in range(1, chunks):
        out, ready = lax.optimization_barrier((outgoing(rows_later, table_later, lat_count, j), ready))
        gathered.append(gather_waves(ready))
        home = wave_rows(swap_lat(out), j)
        ready, *rest = pair_rows(swap_lat(home), pieces if j == chunks - 1 else [row_count // 2])
    first_rows, ready = lax.optimization_barrier((gathered[0], ready))
    last = gather_waves(ready)
    first_rows = swap_lat(first_rows.swapaxes(0, 1)).reshape(lat_count * wave_count, row_count, row_width)
    whole = pair_rows(first_rows, [row_count // 2]) + gathered[1:]

    lon_dev = NLON // wave_count
    lon_ids = wave_pos * lon_dev + jnp.arange(lon_dev, dtype=jnp.int32)
    blocks = [slot_ids[:, 0].T.reshape(-1)]
    blocks += [slot_ids[w, j] for j in range(1, chunks) for w in range(wave_count)]
    trig = zonal_matrix(blocks, lon_ids)
    if not rest:
        return synthesize(trig, whole, [last], 0, pieces, None)
    sources = (wave_pos - jnp.arange(wave_count)) % wave_count
    seen_ids = slot_ids[sources, chunks - 1]
    rest_trig = zonal_matrix(blocks[:-wave_count] + [seen_ids[k] for k in range(wave_count)], lon_ids)
    rest, last, trig, rest_trig, *whole = lax.optimization_barrier((rest[0], last, trig, rest_trig, *whole))
    whole = [pltpu.with_memory_space_constraint(array, pltpu.MemorySpace.HBM) for array in whole]
    last = pltpu.with_memory_space_constraint(last, pltpu.MemorySpace.HBM)
    rest = from_waves(rest)
    grid = synthesize(trig, whole, [last], 0, pieces, None)
    return synthesize(rest_trig, whole, rest, pieces[0], pieces, grid)


def solution(mesh):
    placed = (
        P("wave", "lat", None),
        P("wave", "lat", None),
        P(),
        P("wave", None),
        P("wave", None),
        P("wave", None),
    )
    return jax.shard_map(
        on_device, mesh=mesh, in_specs=placed, out_specs=P("wave", "lat"), check_vma=False
    )
```
